256 devices in a mesh: slab: 64 (over z, y, core), group: 4 (over x).
Axes of the slice: x: 4, y: 4, z: 8, core: 2. Of those that a mesh axis runs over, the one named last changes fastest.
Arguments:
- coarse: bfloat16 [4, 64, 4, 2, 64, 128], P('group', 'slab'), may hold values from -6 to 6
- tconv_weight: bfloat16 [3, 3, 3, 128, 64], replicated, may hold values from -0.3125 to 0.3125
- conv_weight: bfloat16 [3, 3, 3, 64, 64], replicated, may hold values from -0.15625 to 0.15625
- cotangent: bfloat16 [4, 64, 64, 8, 4, 128], P('group', 'slab'), may hold values from -6 to 6
Outputs:
- field: bfloat16 [4, 64, 64, 8, 4, 128], P('group', 'slab')
- grad_coarse: bfloat16 [4, 64, 4, 2, 64, 128], P('group', 'slab')
- grad_conv_weight: float32 [3, 3, 3, 64, 64], replicated
- grad_tconv_weight: float32 [3, 3, 3, 128, 64], replicated
The draws below stay inside these ranges and needn't reach their ends.
All inputs are finite; a program needn't handle non-finite values.
Results may differ from the reference program's by a relative error of at most 0.009.
Values may be sent and summed in bfloat16 or wider, within the bound.
A program may use at most 64 MiB of HBM per device.

```python
import jax
import jax.numpy as jnp
from jax import lax

CIN = 128
COUT = 64
XC = 64
YC = 8
PY = 4
CZB = 4
PZ = 16
YB = 2
BZ = 8
BYF = 4
NZC = 64
NZ = 128
NY = 16
NX = 128
GROUPS = 4
N_SLAB = 64


def block_levels(rng, extent, pieces, low, top_value):
    gain, own = 1.0, jax.random.fold_in(rng, 6)
    for axis_at, shards_of in pieces:
        draws = jnp.exp(jax.random.uniform(jax.random.fold_in(own, axis_at), (shards_of,), jnp.float32, low / len(pieces), top_value / len(pieces)))
        gain = gain * jnp.repeat(draws, extent[axis_at] // shards_of).reshape([-1 if axis == axis_at else 1 for axis in range(len(extent))])
    return gain


def gaussian(rng, extent, spread, bound, shards=(), held_as=jnp.bfloat16):
    factor_of = block_levels(rng, extent, shards, -0.22, 0.18) if shards else 1.0
    values = jax.random.normal(rng, extent, jnp.float32) * spread * factor_of
    return jnp.minimum(jnp.maximum(values, -bound), bound).astype(held_as)


def setup_inputs(seed: int = 0) -> dict:
    key_of = jax.random.split(jax.random.key(seed), 5)
    coarse = gaussian(key_of[0], (GROUPS, N_SLAB, CZB, YB, XC, CIN), 1.0, 6.0, ((0, 4), (1, 64)))
    tconv_weight = gaussian(key_of[1], (3, 3, 3, CIN, COUT), (CIN * 27 // 8) ** -0.5, 0.3125)
    conv_weight = gaussian(key_of[2], (3, 3, 3, COUT, COUT), (COUT * 27) ** -0.5, 0.15625)
    cotangent = gaussian(key_of[3], (GROUPS, N_SLAB, COUT, BZ, BYF, NX), 1.0, 6.0, ((0, 4), (1, 64)))
    return {"coarse": coarse, "tconv_weight": tconv_weight, "conv_weight": conv_weight, "cotangent": cotangent}


def up_conv(coarse32, weight32):
    return lax.conv_general_dilated(coarse32, weight32[::-1, ::-1, ::-1], (1, 1, 1), [(1, 2), (1, 2), (1, 2)], lhs_dilation=(2, 2, 2), dimension_numbers=('NDHWC', 'DHWIO', 'NCDHW'), precision=lax.Precision.HIGHEST)

def same_conv(active32, weight32):
    return lax.conv_general_dilated(active32, weight32, (1, 1, 1), [(1, 1), (1, 1), (1, 1)], dimension_numbers=('NCDHW', 'DHWIO', 'NCDHW'), precision=lax.Precision.HIGHEST)

def whole_coarse(blocks):
    return blocks.reshape(GROUPS, PZ, PY, CZB, YB, XC, CIN).transpose(0, 1, 3, 2, 4, 5, 6).reshape(GROUPS, NZC, YC, XC, CIN)

def block_coarse(whole):
    return whole.reshape(GROUPS, PZ, CZB, PY, YB, XC, CIN).transpose(0, 1, 3, 2, 4, 5, 6).reshape(GROUPS, N_SLAB, CZB, YB, XC, CIN)

def whole_fine(blocks):
    return blocks.reshape(GROUPS, PZ, PY, COUT, BZ, BYF, NX).transpose(0, 3, 1, 4, 2, 5, 6).reshape(GROUPS, COUT, NZ, NY, NX)

def block_fine(whole):
    return whole.reshape(GROUPS, COUT, PZ, BZ, PY, BYF, NX).transpose(0, 2, 4, 1, 3, 5, 6).reshape(GROUPS, N_SLAB, COUT, BZ, BYF, NX)

def reference(coarse, tconv_weight, conv_weight, cotangent):
    tconv32 = tconv_weight.astype(jnp.float32)
    conv32 = conv_weight.astype(jnp.float32)
    coarse_whole = whole_coarse(coarse)
    grad_whole = whole_fine(cotangent)

    def single(pair):
        coarse_one, grad_one = pair
        coarse32 = coarse_one[None].astype(jnp.float32)
        hidden = up_conv(coarse32, tconv32)
        squash = jax.nn.sigmoid(hidden)
        active = (hidden * squash).astype(jnp.bfloat16)
        field = same_conv(active.astype(jnp.float32), conv32)
        unused, pull = jax.vjp(same_conv, active.astype(jnp.float32), conv32)
        grad_active, grad_conv = pull(grad_one[None].astype(jnp.float32))
        grad_hidden = (grad_active * squash * (1.0 + hidden * (1.0 - squash))).astype(jnp.bfloat16)
        unused2, pull2 = jax.vjp(up_conv, coarse32, tconv32)
        grad_in, grad_tconv = pull2(grad_hidden.astype(jnp.float32))
        return (field[0].astype(jnp.bfloat16), grad_in[0].astype(jnp.bfloat16), grad_conv, grad_tconv)
    field, grad_coarse, conv_terms, tconv_terms = lax.map(single, (coarse_whole, grad_whole))
    fine_cells = GROUPS * NZ * NY * NX
    coarse_cells = GROUPS * NZC * YC * XC
    grad_conv_weight = lax.optimization_barrier(jnp.sum(conv_terms, axis=0)) / jnp.sqrt(jnp.float32(fine_cells))
    grad_tconv_weight = lax.optimization_barrier(jnp.sum(tconv_terms, axis=0)) / jnp.sqrt(jnp.float32(coarse_cells))
    return (block_fine(field), block_coarse(grad_coarse), grad_conv_weight, grad_tconv_weight)
```

```python
import functools
import math

import jax
import jax.numpy as jnp
from jax import lax
from jax.experimental import pallas as pl
from jax.experimental.pallas import tpu as pltpu
from jax.sharding import PartitionSpec as P

MESH = pl.DeviceIdType.MESH
F32 = jnp.float32
BF16 = jnp.bfloat16
PY = 4
CIN = 128
C = 64
NT = (((1,), (1,)), ((), ()))

DIRS = [(0, 1), (0, -1), (1, 0), (-1, 0), (1, 1), (1, -1), (-1, 1), (-1, -1)]
COT_Z = {1: (6, 2), 0: (0, 8), -1: (0, 1)}
COT_Y = {1: (256, 256), 0: (0, 512), -1: (0, 128)}
COA_Z = {1: (3, 1), 0: (0, 4), -1: (0, 1)}
COA_Y = {1: (1, 1), 0: (0, 2), -1: (0, 1)}


def dot(a, b):
    return jnp.dot(a, b, preferred_element_type=F32)


def dot_nt(a, b):
    return lax.dot_general(a, b, NT, preferred_element_type=F32)


def ceil16(n):
    return -(-n // 16) * 16


class Place:
    def __init__(self, nz, ny, nx):
        self.nz, self.ny, self.nx = nz, ny, nx
        self.plane = ny * nx
        self.slab = lax.axis_index("slab")
        self.x = lax.axis_index("group")
        self.core = lax.rem(self.slab, 2)
        chip = lax.div(self.slab, 2)
        self.y = lax.rem(chip, ny)
        self.z = lax.div(chip, ny)
        self.p = self.y * nx + self.x
        lane = lax.rem(self.slab, PY)
        zb = lax.div(self.slab, PY)
        self.has_y = {1: lane < PY - 1, -1: lane > 0}
        self.has_z = {1: zb < nz * ny * 2 // PY - 1, -1: zb > 0}

    def has(self, dz, dy):
        if dz == 0:
            return self.has_y[dy]
        if dy == 0:
            return self.has_z[dz]
        return jnp.logical_and(self.has_z[dz], self.has_y[dy])

    def halo(self, dz, dy):
        return (self.slab + PY * dz + dy, self.x)

    def pair(self):
        return (self.slab + 1 - 2 * self.core, self.x)

    def in_plane(self, k):
        p = lax.rem(self.p + k, self.plane)
        y, x = lax.div(p, self.nx), lax.rem(p, self.nx)
        return p, ((self.z * self.ny + y) * 2 + self.core, x)

    def along_z(self, k):
        z = lax.rem(self.z + k, self.nz)
        return ((z * self.ny + self.y) * 2 + self.core, self.x)


def remote(src, dst, send, recv, device):
    return pltpu.make_async_remote_copy(
        src_ref=src, dst_ref=dst, send_sem=send, recv_sem=recv, device_id=device, device_id_type=MESH
    )


class Reduction:
    def __init__(self, at, rows, bufs, sems):
        self.at, self.r = at, rows
        self.v, self.r0, self.s0, self.r1, self.s1, self.r2, self.g = bufs
        self.pair_sems, self.plane_send, self.plane_recv, self.z_send, self.z_recv, self.back_send, self.back_recv = sems
        self.sent = []

    def go(self, copy):
        copy.start()
        self.sent.append(copy)
        return copy

    def start_pair(self):
        at = self.at
        self.c0 = self.go(remote(self.v.at[1 - at.core], self.r0, self.pair_sems.at[0], self.pair_sems.at[1], at.pair()))

    def start_plane(self):
        at, r = self.at, self.r
        self.c0.wait_recv()
        self.s0[...] = (self.v[at.core].astype(F32) + self.r0[...].astype(F32)).astype(BF16)
        self.c1 = []
        for k in range(1, at.plane):
            p, device = at.in_plane(k)
            rows = pl.ds(pl.multiple_of(p * r, 16), r)
            self.c1.append(
                self.go(remote(self.s0.at[rows], self.r1.at[k - 1], self.plane_send.at[k - 1], self.plane_recv.at[k - 1], device))
            )

    def start_z(self):
        at, r = self.at, self.r
        total = self.s0[pl.ds(pl.multiple_of(at.p * r, 16), r), :].astype(F32)
        for k, c in enumerate(self.c1):
            c.wait_recv()
            total = total + self.r1[k].astype(F32)
        self.s1[...] = total.astype(BF16)
        self.r2[at.z] = self.s1[...]
        self.c2 = []
        for k in range(1, at.nz):
            self.c2.append(
                self.go(remote(self.s1, self.r2.at[at.z], self.z_send.at[k - 1], self.z_recv.at[k - 1], at.along_z(k)))
            )

    def start_back(self):
        at, r = self.at, self.r
        for c in self.c2:
            c.wait_recv()
        total = self.r2[0].astype(F32)
        for k in range(1, at.nz):
            total = total + self.r2[k].astype(F32)
        rows = pl.ds(pl.multiple_of(at.p * r, 16), r)
        self.g[at.core, rows, :] = total.astype(BF16)
        self.c3 = []
        for k in range(1, at.plane):
            _, device = at.in_plane(k)
            self.c3.append(
                self.go(
                    remote(
                        self.g.at[at.core, rows], self.g.at[at.core, rows], self.back_send.at[k - 1], self.back_recv.at[k - 1], device
                    )
                )
            )

    def start_share(self):
        at = self.at
        for c in self.c3:
            c.wait_recv()
        self.c4 = self.go(
            remote(self.g.at[at.core], self.g.at[at.core], self.pair_sems.at[2], self.pair_sems.at[3], at.pair())
        )

    def finish(self):
        self.c4.wait_recv()
        for c in self.sent:
            c.wait_send()


def kernel(
    dims,
    rows_of,
    coarse_hbm,
    tw_hbm,
    cw_hbm,
    cot_hbm,
    field_out,
    gc_out,
    gcw_out,
    gtw_out,
    coarse,
    tw,
    cw,
    cot,
    wide,
    rows_cot,
    *rest,
):
    rest = list(rest)
    cot_halo = {d: rest.pop(0) for d in DIRS}
    coa_halo = {d: rest.pop(0) for d in DIRS}
    up, w1, w2, w4, w3, act, ds, bb, gh, taps, et, cols, pair_buf = (rest.pop(0) for _ in range(13))
    bufs = [[rest.pop(0) for _ in range(7)] for _ in range(2)]
    sems = [[rest.pop(0) for _ in range(7)] for _ in range(2)]
    load_sem, cot_send, cot_recv, coa_send, coa_recv = rest
    nz, ny, nx = dims
    at = Place(nz, ny, nx)

    barrier = pltpu.get_barrier_semaphore()
    others = [at.pair()]
    others += [at.in_plane(k)[1] for k in range(1, at.plane)]
    others += [at.along_z(k) for k in range(1, nz)]
    for device in others:
        pl.semaphore_signal(barrier, inc=1, device_id=device, device_id_type=MESH)
    for d in DIRS:

        @pl.when(at.has(*d))
        def _():
            pl.semaphore_signal(barrier, inc=1, device_id=at.halo(*d), device_id_type=MESH)

    loads = [
        pltpu.make_async_copy(src, dst, load_sem.at[i])
        for i, (src, dst) in enumerate(((cot_hbm, cot), (coarse_hbm, coarse), (tw_hbm, tw), (cw_hbm, cw)))
    ]
    for load in loads:
        load.start()

    loads[0].wait()
    wide[...] = cot[...].astype(F32)
    for z in range(8):
        for y in range(4):
            rows_cot[z, :, y * 128 : y * 128 + 128] = wide[pl.ds(z * 4 + y, C, stride=32), :].astype(BF16)

    for d in DIRS:

        @pl.when(jnp.logical_not(at.has(-d[0], -d[1])))
        def _():
            cot_halo[d][...] = jnp.zeros_like(cot_halo[d])
            coa_halo[d][...] = jnp.zeros_like(coa_halo[d])

    loads[1].wait()
    count = len(others)
    for d in DIRS:
        count = count + jnp.where(at.has(*d), 1, 0)
    pl.semaphore_wait(barrier, count)

    def coa_copy(i, d):
        (z, dz), (y, dy) = COA_Z[d[0]], COA_Y[d[1]]
        return remote(
            coarse.at[pl.ds(z, dz), pl.ds(y, dy)], coa_halo[d], coa_send.at[i], coa_recv.at[i], at.halo(*d)
        )

    def cot_copy(i, d):
        (z, dz), (y, dy) = COT_Z[d[0]], COT_Y[d[1]]
        return remote(
            rows_cot.at[pl.ds(z, dz), :, pl.ds(y, dy)], cot_halo[d], cot_send.at[i], cot_recv.at[i], at.halo(*d)
        )

    for copy_of in (coa_copy, cot_copy):
        for i, d in enumerate(DIRS):

            @pl.when(at.has(*d))
            def _():
                copy_of(i, d).start()

    def arrived(copy_of):
        for i, d in enumerate(DIRS):

            @pl.when(at.has(-d[0], -d[1]))
            def _():
                copy_of(i, d).wait_recv()

    loads[2].wait()
    loads[3].wait()
    for kz in range(3):
        for ky in range(3):
            for kx in range(3):
                block = tw[((kz * 3 + ky) * 3 + kx) * C : ((kz * 3 + ky) * 3 + kx + 1) * C, :]
                w1[kz, ky * C : (ky + 1) * C, kx * 128 : kx * 128 + 128] = block
                w3[ky * 3 + kx, kz * C : (kz + 1) * C, :] = block
    for a in range(3):
        tall = jnp.concatenate([cw[(b * 3 + a) * 192 : (b * 3 + a + 1) * 192, :].astype(F32) for b in range(3)], axis=0)
        w4[a * C : (a + 1) * C, :] = tall.T.astype(BF16)
        w2[a * C : (a + 1) * C, :] = jnp.concatenate(
            [
                cw[((b * 3 + a) * 3 + x) * C : ((b * 3 + a) * 3 + x + 1) * C, :].astype(F32)
                for b in (2, 1, 0)
                for x in range(3)
            ],
            axis=1,
        ).astype(BF16)

    lane_at = lax.broadcasted_iota(jnp.int32, (C, 128), 1)
    not_first = jnp.where(lane_at == 0, 0.0, 1.0).astype(F32)
    not_last = jnp.where(lane_at == 127, 0.0, 1.0).astype(F32)

    def taps_of(row):
        return pltpu.roll(row, 1, 1) * not_first, row, pltpu.roll(row, 127, 1) * not_last

    def put_cot(ze, ye, row):
        before, row, after = taps_of(row.astype(F32))
        for i, value in enumerate((after, row, before)):
            bb[pl.ds(pl.multiple_of(ze * 192 + i * C, C), C), ye * 128 : ye * 128 + 128] = value.astype(BF16)

    @pl.loop(0, 8)
    def _(z):
        for y in range(4):
            put_cot(z + 2, y + 2, rows_cot[z, :, y * 128 : y * 128 + 128])

    cell = lax.broadcasted_iota(jnp.int32, (C, 384), 0)
    place = lax.broadcasted_iota(jnp.int32, (C, 384), 1)
    spread = jnp.zeros((C, 384), F32)
    for k in range(3):
        spread = spread + jnp.where(place == 2 * cell + (k - 1) + 128 * k, 1.0, 0.0) * jnp.where(
            jnp.logical_and(place >= 128 * k, place < 128 * k + 128), 1.0, 0.0
        )
    spread = spread.astype(BF16)

    def put_coarse(ze, ye, block):
        wide_block = dot(block.astype(F32).T.astype(BF16), spread).astype(BF16)
        for k in range(3):
            up[pl.ds(pl.multiple_of(ze * 384 + k * 128, 128), 128), ye * 128 : ye * 128 + 128] = wide_block[:, k * 128 : k * 128 + 128]

    @pl.loop(0, 4)
    def _(z):
        for y in range(2):
            put_coarse(z + 1, y + 1, coarse[z, y])

    arrived(coa_copy)

    @pl.loop(0, 4)
    def _(z):
        put_coarse(z + 1, 0, coa_halo[(0, 1)][z, 0])
        put_coarse(z + 1, 3, coa_halo[(0, -1)][z, 0])

    for dz, ze in ((1, 0), (-1, 5)):
        put_coarse(ze, 0, coa_halo[(dz, 1)][0, 0])
        for y in range(2):
            put_coarse(ze, y + 1, coa_halo[(dz, 0)][0, y])
        put_coarse(ze, 3, coa_halo[(dz, -1)][0, 0])

    has_zl = jnp.where(at.has_z[-1], 1.0, 0.0).astype(F32)
    has_zh = jnp.where(at.has_z[1], 1.0, 0.0).astype(F32)
    has_yl = jnp.where(at.has_y[-1], 1.0, 0.0).astype(F32)
    has_yh = jnp.where(at.has_y[1], 1.0, 0.0).astype(F32)

    def put_hidden(zf, partial, z_mask, slopes):
        for yf in range(6):
            n = yf // 2
            if yf % 2:
                h = partial[C : 2 * C, (n + 1) * 128 : (n + 2) * 128]
            else:
                h = partial[2 * C :, n * 128 : n * 128 + 128] + partial[:C, (n + 1) * 128 : (n + 2) * 128]
            mask = z_mask
            if yf == 0:
                mask = mask * has_yl
            if yf == 5:
                mask = mask * has_yh
            s = 1.0 / (1.0 + jnp.exp(-h))
            row = (h * s) * mask
            for i, value in enumerate(taps_of(row)):
                act[pl.ds(pl.multiple_of(zf * 192 + i * C, C), C), yf * 128 : yf * 128 + 128] = value.astype(BF16)
            if yf < 5:

                @pl.when(slopes)
                def _():
                    ds[zf, :, yf * 128 : yf * 128 + 128] = s * (1.0 + h * (1.0 - s)) * (mask if yf == 0 else z_mask)

    w1_odd = jnp.concatenate([w1[2], w1[0]], axis=1)

    @pl.loop(0, 5)
    def _(m):
        start = pl.multiple_of(m * 384, 128)
        odd = dot(w1_odd, up[pl.ds(start, 768), :])
        put_hidden(2 * m, odd, jnp.where(m == 0, has_zl, 1.0), m >= 0)
        even = dot(w1[1], up[pl.ds(pl.multiple_of(start + 384, 128), 384), :])
        put_hidden(2 * m + 1, even, jnp.where(m == 4, has_zh, 1.0), m < 4)

    gc_v, gt_v = bufs[0][0], bufs[1][0]
    conv_sum = Reduction(at, rows_of[0], bufs[0], sems[0])
    tconv_sum = Reduction(at, rows_of[1], bufs[1], sems[1])
    taps[...] = jnp.zeros_like(taps)

    @pl.loop(0, 8)
    def _(z):
        blocks = [
            act[pl.ds(pl.multiple_of((z + dz) * 192 + C, C), C), dy * 128 : dy * 128 + 512]
            for dz in range(3)
            for dy in range(3)
        ]
        right = bb[pl.ds(pl.multiple_of((z + 2) * 192, C), 192), 256:768]
        taps[...] += dot_nt(jnp.concatenate(blocks, axis=0), right)

    def fill(v, half_rows, parts):
        at_row = 0
        for part in parts:
            done, n = 0, part.shape[0]
            while done < n:
                half, row = divmod(at_row, half_rows)
                m = min(n - done, half_rows - row)
                v[half, row : row + m, :] = part[done : done + m, :].astype(BF16)
                done, at_row = done + m, at_row + m
        while at_row < 2 * half_rows:
            half, row = divmod(at_row, half_rows)
            v[half, row:, :] = jnp.zeros((half_rows - row, 128), BF16)
            at_row += half_rows - row

    fill(
        gc_v,
        at.plane * rows_of[0],
        [taps[:, :128], jnp.concatenate([taps[:288, 128:], taps[288:, 128:]], axis=1)],
    )
    conv_sum.start_pair()

    arrived(cot_copy)

    @pl.loop(0, 8)
    def _(z):
        for y in range(2):
            put_cot(z + 2, y, cot_halo[(0, 1)][z, :, y * 128 : y * 128 + 128])
        put_cot(z + 2, 6, cot_halo[(0, -1)][z])

    for dz, planes in ((1, 2), (-1, 1)):
        for z in range(planes):
            ze = z if dz > 0 else 10
            for y in range(2):
                put_cot(ze, y, cot_halo[(dz, 1)][z, :, y * 128 : y * 128 + 128])
            for y in range(4):
                put_cot(ze, y + 2, cot_halo[(dz, 0)][z, :, y * 128 : y * 128 + 128])
            put_cot(ze, 6, cot_halo[(dz, -1)][z])
    conv_sum.start_plane()

    @pl.loop(0, 9)
    def _(q):
        partial = dot(w2[...], bb[pl.ds(pl.multiple_of(q * 192, C), 576), :])
        for yf in range(5):
            ga = partial[:C, (yf + 2) * 128 : (yf + 3) * 128]
            ga = ga + partial[C : 2 * C, (yf + 1) * 128 : (yf + 2) * 128]
            ga = ga + partial[2 * C :, yf * 128 : yf * 128 + 128]
            gh[pl.ds(pl.multiple_of(q * C, C), C), yf * 128 : yf * 128 + 128] = (
                ga * ds[q, :, yf * 128 : yf * 128 + 128]
            ).astype(BF16)

    conv_sum.start_z()

    def picks(shape, f_dim):
        f = lax.broadcasted_iota(jnp.int32, shape, f_dim)
        c = lax.broadcasted_iota(jnp.int32, shape, 1 - f_dim)
        out = jnp.zeros(shape, F32)
        for k in range(3):
            for y in range(2):
                cell0 = k * 128 + y * C
                inside = jnp.logical_and(c >= cell0, c < cell0 + C)
                hit = jnp.logical_and(f == 2 * (c - cell0) + (k - 1) + 128 * y, inside)
                own = jnp.logical_and(f >= 128 * y, f < 128 * y + 128)
                out = out + jnp.where(jnp.logical_and(hit, own), 1.0, 0.0)
        return out.astype(BF16)

    pick = picks((256, 384), 0)
    pick_t = picks((384, 256), 1)
    for ky in range(3):
        pair_buf[:, :128] = gh[:, ky * 128 : ky * 128 + 128]
        pair_buf[:, 128:] = gh[:, (ky + 2) * 128 : (ky + 3) * 128]
        some = dot(pair_buf[...], pick).astype(BF16)
        for zc in range(4):
            for kz in range(3):
                for kx in range(3):
                    row = ((kz * 3 + ky) * 3 + kx) * C
                    q = (2 * zc + kz) * C
                    cols[row : row + C, zc * 128 : zc * 128 + 128] = some[q : q + C, kx * 128 : kx * 128 + 128]
        et[ky] = dot_nt(pick_t, pair_buf[...]).astype(BF16)

    fill(gt_v, at.plane * rows_of[1], [dot(cols[...], coarse[...].reshape(512, CIN))])
    tconv_sum.start_pair()
    conv_sum.start_back()

    for zc in range(4):
        total = jnp.zeros((128, CIN), F32)
        for ky in range(3):
            for kx in range(3):
                total = total + dot(et[ky, kx * 128 : kx * 128 + 128, zc * 128 : zc * 128 + 192], w3[ky * 3 + kx])
        gc_out[zc * 128 : zc * 128 + 128, :] = total.astype(BF16)
    tconv_sum.start_plane()

    def put_field(z):
        partial = dot(w4[...], act[pl.ds(pl.multiple_of(z * 192, C), 576), :])
        for y in range(4):
            row = partial[:C, y * 128 : y * 128 + 128]
            row = row + partial[C : 2 * C, (y + 1) * 128 : (y + 2) * 128]
            row = row + partial[2 * C :, (y + 2) * 128 : (y + 3) * 128]
            wide[pl.ds(z * 4 + y, C, stride=32), :] = row

    pl.loop(0, 4)(put_field)
    conv_sum.start_share()
    tconv_sum.start_z()
    pl.loop(4, 8)(put_field)
    tconv_sum.start_back()
    field_out[...] = wide[...].astype(BF16)

    n_dev = nz * ny * nx * 2
    conv_sum.finish()
    conv_scale = 1.0 / math.sqrt(n_dev * 8 * 4 * 128)
    g = conv_sum.g[...].reshape(-1, 128)
    first = g[:576].astype(F32) * conv_scale
    second = g[576:864].astype(F32) * conv_scale
    for zy in range(9):
        for dx in range(2):
            gcw_out[zy * 3 + dx] = first[zy * C : (zy + 1) * C, dx * C : (dx + 1) * C]
    for half in range(18):
        src = second[(half % 9) * 32 : (half % 9) * 32 + 32, (half // 9) * C : (half // 9 + 1) * C]
        gcw_out[(half // 2) * 3 + 2, (half % 2) * 32 : (half % 2) * 32 + 32, :] = src
    tconv_sum.start_share()
    tconv_sum.finish()
    tconv_scale = 1.0 / math.sqrt(n_dev * 4 * 2 * 64)
    gtw_out[...] = tconv_sum.g[...].reshape(-1, 128)[:1728].astype(F32) * tconv_scale

    for copy_of in (coa_copy, cot_copy):
        for i, d in enumerate(DIRS):

            @pl.when(at.has(*d))
            def _():
                copy_of(i, d).wait_send()


def solution(mesh):
    nx = mesh.shape["group"]
    n_slab = mesh.shape["slab"]
    ny = 4
    nz = n_slab // (2 * ny)
    plane = ny * nx
    rows_of = [ceil16(-(-n // (2 * plane))) for n in (864, 1728)]

    def step(coarse, tw, cw, cot):
        dma = pltpu.SemaphoreType.DMA
        vmem = pltpu.VMEM
        scratch = [
            vmem((4, 2, 64, CIN), BF16),
            vmem((27 * C, CIN), BF16),
            vmem((27 * C, C), BF16),
            vmem((2048, 128), BF16),
            vmem((2048, 128), F32),
            vmem((8, C, 512), BF16),
        ]
        scratch += [vmem((COT_Z[dz][1], C, COT_Y[dy][1]), BF16) for dz, dy in DIRS]
        scratch += [vmem((COA_Z[dz][1], COA_Y[dy][1], 64, CIN), BF16) for dz, dy in DIRS]
        scratch += [
            vmem((6 * 384, 512), BF16),
            vmem((3, 192, 384), BF16),
            vmem((192, 576), BF16),
            vmem((192, 576), BF16),
            vmem((9, 192, CIN), BF16),
            vmem((10 * 192, 768), BF16),
            vmem((9, C, 640), F32),
            vmem((11 * 192, 896), BF16),
            vmem((9 * C, 640), BF16),
            vmem((576, 192), F32),
            vmem((3, 384, 576), BF16),
            vmem((1728, 512), BF16),
            vmem((576, 256), BF16),
        ]
        for r in rows_of:
            scratch += [
                vmem((2, plane * r, 128), BF16),
                vmem((plane * r, 128), BF16),
                vmem((plane * r, 128), BF16),
                vmem((plane - 1, r, 128), BF16),
                vmem((r, 128), BF16),
                vmem((nz, r, 128), BF16),
                vmem((2, plane * r, 128), BF16),
            ]
        for r in rows_of:
            scratch += [dma((4,)), dma((plane - 1,)), dma((plane - 1,)), dma((nz - 1,)), dma((nz - 1,))]
            scratch += [dma((plane - 1,)), dma((plane - 1,))]
        scratch += [dma((4,)), dma((8,)), dma((8,)), dma((8,)), dma((8,))]
        any_space = pl.BlockSpec(memory_space=pl.ANY)
        in_vmem = pl.BlockSpec(memory_space=pltpu.VMEM)
        field, gc, gcw, gtw = pl.pallas_call(
            functools.partial(kernel, (nz, ny, nx), rows_of),
            out_shape=(
                jax.ShapeDtypeStruct((2048, 128), BF16),
                jax.ShapeDtypeStruct((512, CIN), BF16),
                jax.ShapeDtypeStruct((27, C, C), F32),
                jax.ShapeDtypeStruct((27 * C, CIN), F32),
            ),
            in_specs=[any_space] * 4,
            out_specs=(in_vmem,) * 4,
            scratch_shapes=scratch,
            compiler_params=pltpu.CompilerParams(
                collective_id=0, has_side_effects=True, vmem_limit_bytes=50 * 2**20
            ),
            cost_estimate=pl.CostEstimate(flops=7 * 10**9, bytes_accessed=4 * 10**6, transcendentals=500000),
        )(
            coarse.reshape(4, 2, 64, CIN),
            jnp.swapaxes(tw, 3, 4).reshape(27 * C, CIN),
            cw.reshape(27 * C, C),
            cot.reshape(2048, 128),
        )
        return (
            field.reshape(1, 1, C, 8, 4, 128),
            gc.reshape(1, 1, 4, 2, 64, CIN),
            gcw.reshape(3, 3, 3, C, C),
            jnp.swapaxes(gtw.reshape(3, 3, 3, C, CIN), 3, 4),
        )

    blocks = P("group", "slab", None, None, None, None)
    return jax.shard_map(
        step,
        mesh=mesh,
        in_specs=(blocks, P(), P(), blocks),
        out_specs=(blocks, blocks, P(), P()),
        check_vma=False,
    )
```

```python
import functools
import math

import jax
import jax.numpy as jnp
from jax import lax
from jax.experimental import pallas as pl
from jax.experimental.pallas import tpu as pltpu
from jax.sharding import PartitionSpec as P

MESH = pl.DeviceIdType.MESH
F32 = jnp.float32
BF16 = jnp.bfloat16
PY = 4
CIN = 128
C = 64
NT = (((1,), (1,)), ((), ()))

DIRS = [(0, 1), (0, -1), (1, 0), (-1, 0), (1, 1), (1, -1), (-1, 1), (-1, -1)]
COT_Z = {1: (6, 2), 0: (0, 8), -1: (0, 1)}
COT_Y = {1: (256, 256), 0: (0, 512), -1: (0, 128)}
COA_Z = {1: (3, 1), 0: (0, 4), -1: (0, 1)}
COA_Y = {1: (1, 1), 0: (0, 2), -1: (0, 1)}


def dot(a, b):
    return jnp.dot(a, b, preferred_element_type=F32)


def dot_nt(a, b):
    return lax.dot_general(a, b, NT, preferred_element_type=F32)


def mult(n, of):
    return n


def unrolled(start, stop):
    def run(body):
        for i in range(start, stop):
            body(i)

    return run


def ceil16(n):
    return -(-n // 16) * 16


class Place:
    def __init__(self, nz, ny, nx):
        self.nz, self.ny, self.nx = nz, ny, nx
        self.plane = ny * nx
        self.slab = lax.axis_index("slab")
        self.x = lax.axis_index("group")
        self.core = lax.rem(self.slab, 2)
        chip = lax.div(self.slab, 2)
        self.y = lax.rem(chip, ny)
        self.z = lax.div(chip, ny)
        self.p = self.y * nx + self.x
        lane = lax.rem(self.slab, PY)
        zb = lax.div(self.slab, PY)
        self.has_y = {1: lane < PY - 1, -1: lane > 0}
        self.has_z = {1: zb < nz * ny * 2 // PY - 1, -1: zb > 0}

    def has(self, dz, dy):
        if dz == 0:
            return self.has_y[dy]
        if dy == 0:
            return self.has_z[dz]
        return jnp.logical_and(self.has_z[dz], self.has_y[dy])

    def halo(self, dz, dy):
        return (self.slab + PY * dz + dy, self.x)

    def pair(self):
        return (self.slab + 1 - 2 * self.core, self.x)

    def in_plane(self, k):
        p = lax.rem(self.p + k, self.plane)
        y, x = lax.div(p, self.nx), lax.rem(p, self.nx)
        return p, ((self.z * self.ny + y) * 2 + self.core, x)

    def along_z(self, k):
        z = lax.rem(self.z + k, self.nz)
        return ((z * self.ny + self.y) * 2 + self.core, self.x)


def remote(src, dst, send, recv, device):
    return pltpu.make_async_remote_copy(
        src_ref=src, dst_ref=dst, send_sem=send, recv_sem=recv, device_id=device, device_id_type=MESH
    )


class Reduction:
    def __init__(self, at, rows, bufs, sems):
        self.at, self.r = at, rows
        self.v, self.r0, self.s0, self.r1, self.s1, self.r2, self.g = bufs
        self.pair_sems, self.plane_send, self.plane_recv, self.z_send, self.z_recv, self.back_send, self.back_recv = sems
        self.sent = []

    def go(self, copy):
        copy.start()
        self.sent.append(copy)
        return copy

    def start_pair(self):
        at = self.at
        self.c0 = self.go(remote(self.v.at[1 - at.core], self.r0, self.pair_sems.at[0], self.pair_sems.at[1], at.pair()))

    def start_plane(self):
        at, r = self.at, self.r
        self.c0.wait_recv()
        self.s0[...] = (self.v[at.core].astype(F32) + self.r0[...].astype(F32)).astype(BF16)
        self.c1 = []
        for k in range(1, at.plane):
            p, device = at.in_plane(k)
            rows = pl.ds(pl.multiple_of(p * r, 16), r)
            self.c1.append(
                self.go(remote(self.s0.at[rows], self.r1.at[k - 1], self.plane_send.at[k - 1], self.plane_recv.at[k - 1], device))
            )

    def start_z(self):
        at, r = self.at, self.r
        total = self.s0[pl.ds(pl.multiple_of(at.p * r, 16), r), :].astype(F32)
        for k, c in enumerate(self.c1):
            c.wait_recv()
            total = total + self.r1[k].astype(F32)
        self.s1[...] = total.astype(BF16)
        self.r2[at.z] = self.s1[...]
        self.c2 = []
        for k in range(1, at.nz):
            self.c2.append(
                self.go(remote(self.s1, self.r2.at[at.z], self.z_send.at[k - 1], self.z_recv.at[k - 1], at.along_z(k)))
            )

    def start_back(self):
        at, r = self.at, self.r
        for c in self.c2:
            c.wait_recv()
        total = self.r2[0].astype(F32)
        for k in range(1, at.nz):
            total = total + self.r2[k].astype(F32)
        rows = pl.ds(pl.multiple_of(at.p * r, 16), r)
        self.g[at.core, rows, :] = total.astype(BF16)
        self.c3 = []
        for k in range(1, at.plane):
            _, device = at.in_plane(k)
            self.c3.append(
                self.go(
                    remote(
                        self.g.at[at.core, rows], self.g.at[at.core, rows], self.back_send.at[k - 1], self.back_recv.at[k - 1], device
                    )
                )
            )

    def start_share(self):
        at = self.at
        for c in self.c3:
            c.wait_recv()
        self.c4 = self.go(
            remote(self.g.at[at.core], self.g.at[at.core], self.pair_sems.at[2], self.pair_sems.at[3], at.pair())
        )

    def finish(self):
        self.c4.wait_recv()
        for c in self.sent:
            c.wait_send()


def kernel(
    dims,
    rows_of,
    coarse_hbm,
    tw_hbm,
    cw_hbm,
    cot_hbm,
    field_out,
    gc_out,
    gcw_out,
    gtw_out,
    coarse,
    tw,
    cw,
    cot,
    wide,
    rows_cot,
    *rest,
):
    rest = list(rest)
    cot_halo = {d: rest.pop(0) for d in DIRS}
    coa_halo = {d: rest.pop(0) for d in DIRS}
    up, w1, w2, w4, w3, act, ds, bb, gh, taps, et, cols, pair_buf = (rest.pop(0) for _ in range(13))
    bufs = [[rest.pop(0) for _ in range(7)] for _ in range(2)]
    sems = [[rest.pop(0) for _ in range(7)] for _ in range(2)]
    load_sem, cot_send, cot_recv, coa_send, coa_recv = rest
    nz, ny, nx = dims
    at = Place(nz, ny, nx)

    barrier = pltpu.get_barrier_semaphore()
    others = [at.pair()]
    others += [at.in_plane(k)[1] for k in range(1, at.plane)]
    others += [at.along_z(k) for k in range(1, nz)]
    for device in others:
        pl.semaphore_signal(barrier, inc=1, device_id=device, device_id_type=MESH)
    for d in DIRS:

        @pl.when(at.has(*d))
        def _():
            pl.semaphore_signal(barrier, inc=1, device_id=at.halo(*d), device_id_type=MESH)

    loads = [
        pltpu.make_async_copy(src, dst, load_sem.at[i])
        for i, (src, dst) in enumerate(((cot_hbm, cot), (coarse_hbm, coarse), (tw_hbm, tw), (cw_hbm, cw)))
    ]
    for load in loads:
        load.start()

    loads[0].wait()
    wide[...] = cot[...].astype(F32)
    for z in range(8):
        for y in range(4):
            rows_cot[z, :, y * 128 : y * 128 + 128] = wide[pl.ds(z * 4 + y, C, stride=32), :].astype(BF16)

    for d in DIRS:

        @pl.when(jnp.logical_not(at.has(-d[0], -d[1])))
        def _():
            cot_halo[d][...] = jnp.zeros_like(cot_halo[d])
            coa_halo[d][...] = jnp.zeros_like(coa_halo[d])

    loads[1].wait()
    count = len(others)
    for d in DIRS:
        count = count + jnp.where(at.has(*d), 1, 0)
    pl.semaphore_wait(barrier, count)

    def coa_copy(i, d):
        (z, dz), (y, dy) = COA_Z[d[0]], COA_Y[d[1]]
        return remote(
            coarse.at[pl.ds(z, dz), pl.ds(y, dy)], coa_halo[d], coa_send.at[i], coa_recv.at[i], at.halo(*d)
        )

    def cot_copy(i, d):
        (z, dz), (y, dy) = COT_Z[d[0]], COT_Y[d[1]]
        return remote(
            rows_cot.at[pl.ds(z, dz), :, pl.ds(y, dy)], cot_halo[d], cot_send.at[i], cot_recv.at[i], at.halo(*d)
        )

    for copy_of in (coa_copy, cot_copy):
        for i, d in enumerate(DIRS):

            @pl.when(at.has(*d))
            def _():
                copy_of(i, d).start()

    def arrived(copy_of):
        for i, d in enumerate(DIRS):

            @pl.when(at.has(-d[0], -d[1]))
            def _():
                copy_of(i, d).wait_recv()

    loads[2].wait()
    loads[3].wait()
    for kz in range(3):
        for ky in range(3):
            for kx in range(3):
                block = tw[((kz * 3 + ky) * 3 + kx) * C : ((kz * 3 + ky) * 3 + kx + 1) * C, :]
                w1[kz, ky * C : (ky + 1) * C, kx * 128 : kx * 128 + 128] = block
                w3[ky * 3 + kx, kz * C : (kz + 1) * C, :] = block
    for a in range(3):
        tall = jnp.concatenate([cw[(b * 3 + a) * 192 : (b * 3 + a + 1) * 192, :].astype(F32) for b in range(3)], axis=0)
        w4[a * C : (a + 1) * C, :] = tall.T.astype(BF16)
        w2[a * C : (a + 1) * C, :] = jnp.concatenate(
            [
                cw[((b * 3 + a) * 3 + x) * C : ((b * 3 + a) * 3 + x + 1) * C, :].astype(F32)
                for b in (2, 1, 0)
                for x in range(3)
            ],
            axis=1,
        ).astype(BF16)

    lane_at = lax.broadcasted_iota(jnp.int32, (C, 128), 1)
    not_first = jnp.where(lane_at == 0, 0.0, 1.0).astype(F32)
    not_last = jnp.where(lane_at == 127, 0.0, 1.0).astype(F32)

    def taps_of(row):
        return pltpu.roll(row, 1, 1) * not_first, row, pltpu.roll(row, 127, 1) * not_last

    def put_cot(ze, ye, row):
        before, row, after = taps_of(row.astype(F32))
        for i, value in enumerate((after, row, before)):
            bb[pl.ds(mult(ze * 192 + i * C, C), C), ye * 128 : ye * 128 + 128] = value.astype(BF16)

    @unrolled(0, 8)
    def _(z):
        for y in range(4):
            put_cot(z + 2, y + 2, rows_cot[z, :, y * 128 : y * 128 + 128])

    cell = lax.broadcasted_iota(jnp.int32, (C, 384), 0)
    place = lax.broadcasted_iota(jnp.int32, (C, 384), 1)
    spread = jnp.zeros((C, 384), F32)
    for k in range(3):
        spread = spread + jnp.where(place == 2 * cell + (k - 1) + 128 * k, 1.0, 0.0) * jnp.where(
            jnp.logical_and(place >= 128 * k, place < 128 * k + 128), 1.0, 0.0
        )
    spread = spread.astype(BF16)

    def put_coarse(ze, ye, block):
        wide_block = dot(block.astype(F32).T.astype(BF16), spread).astype(BF16)
        for k in range(3):
            up[pl.ds(mult(ze * 384 + k * 128, 128), 128), ye * 128 : ye * 128 + 128] = wide_block[:, k * 128 : k * 128 + 128]

    @unrolled(0, 4)
    def _(z):
        for y in range(2):
            put_coarse(z + 1, y + 1, coarse[z, y])

    arrived(coa_copy)

    @unrolled(0, 4)
    def _(z):
        put_coarse(z + 1, 0, coa_halo[(0, 1)][z, 0])
        put_coarse(z + 1, 3, coa_halo[(0, -1)][z, 0])

    for dz, ze in ((1, 0), (-1, 5)):
        put_coarse(ze, 0, coa_halo[(dz, 1)][0, 0])
        for y in range(2):
            put_coarse(ze, y + 1, coa_halo[(dz, 0)][0, y])
        put_coarse(ze, 3, coa_halo[(dz, -1)][0, 0])

    has_zl = jnp.where(at.has_z[-1], 1.0, 0.0).astype(F32)
    has_zh = jnp.where(at.has_z[1], 1.0, 0.0).astype(F32)
    has_yl = jnp.where(at.has_y[-1], 1.0, 0.0).astype(F32)
    has_yh = jnp.where(at.has_y[1], 1.0, 0.0).astype(F32)

    def put_hidden(zf, partial, z_mask, slopes):
        for yf in range(6):
            n = yf // 2
            if yf % 2:
                h = partial[C : 2 * C, (n + 1) * 128 : (n + 2) * 128]
            else:
                h = partial[2 * C :, n * 128 : n * 128 + 128] + partial[:C, (n + 1) * 128 : (n + 2) * 128]
            mask = z_mask
            if yf in (0, 5):
                y_mask = has_yl if yf == 0 else has_yh
                mask = y_mask if mask is None else mask * y_mask
            s = 0.5 * jnp.tanh(0.5 * h) + 0.5
            row = h * s
            if mask is not None:
                row = row * mask
            for i, value in enumerate(taps_of(row)):
                act[pl.ds(mult(zf * 192 + i * C, C), C), yf * 128 : yf * 128 + 128] = value.astype(BF16)
            if yf < 5 and slopes:
                slope = s * (1.0 + h * (1.0 - s))
                ds[zf, :, yf * 128 : yf * 128 + 128] = slope if mask is None else slope * mask

    w1_odd = jnp.concatenate([w1[2], w1[0]], axis=1)

    @unrolled(0, 5)
    def _(m):
        start = mult(m * 384, 128)
        odd = dot(w1_odd, up[pl.ds(start, 768), :])
        put_hidden(2 * m, odd, has_zl if m == 0 else None, True)
        even = dot(w1[1], up[pl.ds(mult(start + 384, 128), 384), :])
        put_hidden(2 * m + 1, even, has_zh if m == 4 else None, m < 4)

    gc_v, gt_v = bufs[0][0], bufs[1][0]
    conv_sum = Reduction(at, rows_of[0], bufs[0], sems[0])
    tconv_sum = Reduction(at, rows_of[1], bufs[1], sems[1])
    taps[...] = jnp.zeros_like(taps)

    @unrolled(0, 8)
    def _(z):
        blocks = [
            act[pl.ds(mult((z + dz) * 192 + C, C), C), dy * 128 : dy * 128 + 512]
            for dz in range(3)
            for dy in range(3)
        ]
        right = bb[pl.ds(mult((z + 2) * 192, C), 192), 256:768]
        taps[...] += dot_nt(jnp.concatenate(blocks, axis=0), right)

    def fill(v, half_rows, parts):
        at_row = 0
        for part in parts:
            done, n = 0, part.shape[0]
            while done < n:
                half, row = divmod(at_row, half_rows)
                m = min(n - done, half_rows - row)
                v[half, row : row + m, :] = part[done : done + m, :].astype(BF16)
                done, at_row = done + m, at_row + m
        while at_row < 2 * half_rows:
            half, row = divmod(at_row, half_rows)
            v[half, row:, :] = jnp.zeros((half_rows - row, 128), BF16)
            at_row += half_rows - row

    fill(
        gc_v,
        at.plane * rows_of[0],
        [taps[:, :128], jnp.concatenate([taps[:288, 128:], taps[288:, 128:]], axis=1)],
    )
    conv_sum.start_pair()

    arrived(cot_copy)

    @unrolled(0, 8)
    def _(z):
        for y in range(2):
            put_cot(z + 2, y, cot_halo[(0, 1)][z, :, y * 128 : y * 128 + 128])
        put_cot(z + 2, 6, cot_halo[(0, -1)][z])

    for dz, planes in ((1, 2), (-1, 1)):
        for z in range(planes):
            ze = z if dz > 0 else 10
            for y in range(2):
                put_cot(ze, y, cot_halo[(dz, 1)][z, :, y * 128 : y * 128 + 128])
            for y in range(4):
                put_cot(ze, y + 2, cot_halo[(dz, 0)][z, :, y * 128 : y * 128 + 128])
            put_cot(ze, 6, cot_halo[(dz, -1)][z])
    conv_sum.start_plane()

    @unrolled(0, 9)
    def _(q):
        partial = dot(w2[...], bb[pl.ds(mult(q * 192, C), 576), :])
        for yf in range(5):
            ga = partial[:C, (yf + 2) * 128 : (yf + 3) * 128]
            ga = ga + partial[C : 2 * C, (yf + 1) * 128 : (yf + 2) * 128]
            ga = ga + partial[2 * C :, yf * 128 : yf * 128 + 128]
            gh[pl.ds(mult(q * C, C), C), yf * 128 : yf * 128 + 128] = (
                ga * ds[q, :, yf * 128 : yf * 128 + 128]
            ).astype(BF16)

    conv_sum.start_z()

    def picks(shape, f_dim):
        f = lax.broadcasted_iota(jnp.int32, shape, f_dim)
        c = lax.broadcasted_iota(jnp.int32, shape, 1 - f_dim)
        out = jnp.zeros(shape, F32)
        for k in range(3):
            for y in range(2):
                cell0 = k * 128 + y * C
                inside = jnp.logical_and(c >= cell0, c < cell0 + C)
                hit = jnp.logical_and(f == 2 * (c - cell0) + (k - 1) + 128 * y, inside)
                own = jnp.logical_and(f >= 128 * y, f < 128 * y + 128)
                out = out + jnp.where(jnp.logical_and(hit, own), 1.0, 0.0)
        return out.astype(BF16)

    pick = picks((256, 384), 0)
    pick_t = picks((384, 256), 1)
    for ky in range(3):
        pair_buf[:, :128] = gh[:, ky * 128 : ky * 128 + 128]
        pair_buf[:, 128:] = gh[:, (ky + 2) * 128 : (ky + 3) * 128]
        some = dot(pair_buf[...], pick).astype(BF16)
        for zc in range(4):
            for kz in range(3):
                for kx in range(3):
                    row = ((kz * 3 + ky) * 3 + kx) * C
                    q = (2 * zc + kz) * C
                    cols[row : row + C, zc * 128 : zc * 128 + 128] = some[q : q + C, kx * 128 : kx * 128 + 128]
        et[ky] = dot_nt(pick_t, pair_buf[...]).astype(BF16)

    fill(gt_v, at.plane * rows_of[1], [dot(cols[...], coarse[...].reshape(512, CIN))])
    tconv_sum.start_pair()
    conv_sum.start_back()

    for zc in range(4):
        total = jnp.zeros((128, CIN), F32)
        for ky in range(3):
            for kx in range(3):
                total = total + dot(et[ky, kx * 128 : kx * 128 + 128, zc * 128 : zc * 128 + 192], w3[ky * 3 + kx])
        gc_out[zc * 128 : zc * 128 + 128, :] = total.astype(BF16)
    tconv_sum.start_plane()

    def put_field(z):
        partial = dot(w4[...], act[pl.ds(mult(z * 192, C), 576), :])
        for y in range(4):
            row = partial[:C, y * 128 : y * 128 + 128]
            row = row + partial[C : 2 * C, (y + 1) * 128 : (y + 2) * 128]
            row = row + partial[2 * C :, (y + 2) * 128 : (y + 3) * 128]
            wide[pl.ds(z * 4 + y, C, stride=32), :] = row

    unrolled(0, 4)(put_field)
    conv_sum.start_share()
    tconv_sum.start_z()
    unrolled(4, 8)(put_field)
    tconv_sum.start_back()
    field_out[...] = wide[...].astype(BF16)

    n_dev = nz * ny * nx * 2
    conv_sum.finish()
    conv_scale = 1.0 / math.sqrt(n_dev * 8 * 4 * 128)
    g = conv_sum.g[...].reshape(-1, 128)
    first = g[:576].astype(F32) * conv_scale
    second = g[576:864].astype(F32) * conv_scale
    for zy in range(9):
        for dx in range(2):
            gcw_out[zy * 3 + dx] = first[zy * C : (zy + 1) * C, dx * C : (dx + 1) * C]
    for half in range(18):
        src = second[(half % 9) * 32 : (half % 9) * 32 + 32, (half // 9) * C : (half // 9 + 1) * C]
        gcw_out[(half // 2) * 3 + 2, (half % 2) * 32 : (half % 2) * 32 + 32, :] = src
    tconv_sum.start_share()
    tconv_sum.finish()
    tconv_scale = 1.0 / math.sqrt(n_dev * 4 * 2 * 64)
    gtw_out[...] = tconv_sum.g[...].reshape(-1, 128)[:1728].astype(F32) * tconv_scale

    for copy_of in (coa_copy, cot_copy):
        for i, d in enumerate(DIRS):

            @pl.when(at.has(*d))
            def _():
                copy_of(i, d).wait_send()


def solution(mesh):
    nx = mesh.shape["group"]
    n_slab = mesh.shape["slab"]
    ny = 4
    nz = n_slab // (2 * ny)
    plane = ny * nx
    rows_of = [ceil16(-(-n // (2 * plane))) for n in (864, 1728)]

    def step(coarse, tw, cw, cot):
        dma = pltpu.SemaphoreType.DMA
        vmem = pltpu.VMEM
        scratch = [
            vmem((4, 2, 64, CIN), BF16),
            vmem((27 * C, CIN), BF16),
            vmem((27 * C, C), BF16),
            vmem((2048, 128), BF16),
            vmem((2048, 128), F32),
            vmem((8, C, 512), BF16),
        ]
        scratch += [vmem((COT_Z[dz][1], C, COT_Y[dy][1]), BF16) for dz, dy in DIRS]
        scratch += [vmem((COA_Z[dz][1], COA_Y[dy][1], 64, CIN), BF16) for dz, dy in DIRS]
        scratch += [
            vmem((6 * 384, 512), BF16),
            vmem((3, 192, 384), BF16),
            vmem((192, 576), BF16),
            vmem((192, 576), BF16),
            vmem((9, 192, CIN), BF16),
            vmem((10 * 192, 768), BF16),
            vmem((9, C, 640), F32),
            vmem((11 * 192, 896), BF16),
            vmem((9 * C, 640), BF16),
            vmem((576, 192), F32),
            vmem((3, 384, 576), BF16),
            vmem((1728, 512), BF16),
            vmem((576, 256), BF16),
        ]
        for r in rows_of:
            scratch += [
                vmem((2, plane * r, 128), BF16),
                vmem((plane * r, 128), BF16),
                vmem((plane * r, 128), BF16),
                vmem((plane - 1, r, 128), BF16),
                vmem((r, 128), BF16),
                vmem((nz, r, 128), BF16),
                vmem((2, plane * r, 128), BF16),
            ]
        for r in rows_of:
            scratch += [dma((4,)), dma((plane - 1,)), dma((plane - 1,)), dma((nz - 1,)), dma((nz - 1,))]
            scratch += [dma((plane - 1,)), dma((plane - 1,))]
        scratch += [dma((4,)), dma((8,)), dma((8,)), dma((8,)), dma((8,))]
        any_space = pl.BlockSpec(memory_space=pl.ANY)
        in_vmem = pl.BlockSpec(memory_space=pltpu.VMEM)
        field, gc, gcw, gtw = pl.pallas_call(
            functools.partial(kernel, (nz, ny, nx), rows_of),
            out_shape=(
                jax.ShapeDtypeStruct((2048, 128), BF16),
                jax.ShapeDtypeStruct((512, CIN), BF16),
                jax.ShapeDtypeStruct((27, C, C), F32),
                jax.ShapeDtypeStruct((27 * C, CIN), F32),
            ),
            in_specs=[any_space] * 4,
            out_specs=(in_vmem,) * 4,
            scratch_shapes=scratch,
            compiler_params=pltpu.CompilerParams(
                collective_id=0, has_side_effects=True, vmem_limit_bytes=50 * 2**20
            ),
            cost_estimate=pl.CostEstimate(flops=7 * 10**9, bytes_accessed=4 * 10**6, transcendentals=500000),
        )(
            coarse.reshape(4, 2, 64, CIN),
            jnp.swapaxes(tw, 3, 4).reshape(27 * C, CIN),
            cw.reshape(27 * C, C),
            cot.reshape(2048, 128),
        )
        return (
            field.reshape(1, 1, C, 8, 4, 128),
            gc.reshape(1, 1, 4, 2, 64, CIN),
            gcw.reshape(3, 3, 3, C, C),
            jnp.swapaxes(gtw.reshape(3, 3, 3, C, CIN), 3, 4),
        )

    blocks = P("group", "slab", None, None, None, None)
    return jax.shard_map(
        step,
        mesh=mesh,
        in_specs=(blocks, P(), P(), blocks),
        out_specs=(blocks, blocks, P(), P()),
        check_vma=False,
    )
```

```python
import functools
import math

import jax
import jax.numpy as jnp
from jax import lax
from jax.experimental import pallas as pl
from jax.experimental.pallas import tpu as pltpu
from jax.sharding import PartitionSpec as P

MESH = pl.DeviceIdType.MESH
F32 = jnp.float32
BF16 = jnp.bfloat16
PY = 4
CIN = 128
C = 64
NT = (((1,), (1,)), ((), ()))

DIRS = [(0, 1), (0, -1), (1, 0), (-1, 0), (1, 1), (1, -1), (-1, 1), (-1, -1)]
COT_Z = {1: (7, 1), 0: (0, 8), -1: (0, 1)}
COT_Y = {1: (384, 128), 0: (0, 512), -1: (0, 128)}
COA_Z = {1: (3, 1), 0: (0, 4), -1: (0, 1)}
COA_Y = {1: (1, 1), 0: (0, 2), -1: (0, 1)}
BACK = {(0, 1): (4, 64, CIN), (1, 0): (2, 64, CIN), (1, 1): (1, 64, CIN)}


def dot(a, b):
    return jnp.dot(a, b, preferred_element_type=F32)


def dot_nt(a, b):
    return lax.dot_general(a, b, NT, preferred_element_type=F32)


def unrolled(start, stop):
    def run(body):
        for i in range(start, stop):
            body(i)

    return run


def ceil16(n):
    return -(-n // 16) * 16


class Place:
    def __init__(self, nz, ny, nx):
        self.nz, self.ny, self.nx = nz, ny, nx
        self.plane = ny * nx
        self.slab = lax.axis_index("slab")
        self.x = lax.axis_index("group")
        self.core = lax.rem(self.slab, 2)
        chip = lax.div(self.slab, 2)
        self.y = lax.rem(chip, ny)
        self.z = lax.div(chip, ny)
        self.p = self.y * nx + self.x
        lane = lax.rem(self.slab, PY)
        zb = lax.div(self.slab, PY)
        self.has_y = {1: lane < PY - 1, -1: lane > 0}
        self.has_z = {1: zb < nz * ny * 2 // PY - 1, -1: zb > 0}

    def has(self, dz, dy):
        if dz == 0:
            return self.has_y[dy]
        if dy == 0:
            return self.has_z[dz]
        return jnp.logical_and(self.has_z[dz], self.has_y[dy])

    def halo(self, dz, dy):
        return (self.slab + PY * dz + dy, self.x)

    def pair(self):
        return (self.slab + 1 - 2 * self.core, self.x)

    def in_plane(self, k):
        p = lax.rem(self.p + k, self.plane)
        y, x = lax.div(p, self.nx), lax.rem(p, self.nx)
        return p, ((self.z * self.ny + y) * 2 + self.core, x)

    def along_z(self, k):
        z = lax.rem(self.z + k, self.nz)
        return ((z * self.ny + self.y) * 2 + self.core, self.x)


def remote(src, dst, send, recv, device):
    return pltpu.make_async_remote_copy(
        src_ref=src, dst_ref=dst, send_sem=send, recv_sem=recv, device_id=device, device_id_type=MESH
    )


class Reduction:
    def __init__(self, at, rows, bufs, sems):
        self.at, self.r = at, rows
        self.v, self.r0, self.s0, self.r1, self.s1, self.r2, self.g = bufs
        self.pair_sems, self.plane_send, self.plane_recv, self.z_send, self.z_recv, self.back_send, self.back_recv = sems[:7]
        self.share_send, self.share_recv = sems[7:]
        self.sent = []

    def go(self, copy):
        copy.start()
        self.sent.append(copy)
        return copy

    def start_pair(self):
        at = self.at
        self.c0 = self.go(remote(self.v.at[1 - at.core], self.r0, self.pair_sems.at[0], self.pair_sems.at[1], at.pair()))

    def start_plane(self):
        at, r = self.at, self.r
        self.c0.wait_recv()
        self.s0[...] = (self.v[at.core].astype(F32) + self.r0[...].astype(F32)).astype(BF16)
        self.c1 = []
        for k in range(1, at.plane):
            p, device = at.in_plane(k)
            rows = pl.ds(pl.multiple_of(p * r, 16), r)
            self.c1.append(
                self.go(remote(self.s0.at[rows], self.r1.at[k - 1], self.plane_send.at[k - 1], self.plane_recv.at[k - 1], device))
            )

    def start_z(self):
        at, r = self.at, self.r
        total = self.s0[pl.ds(pl.multiple_of(at.p * r, 16), r), :].astype(F32)
        for k, c in enumerate(self.c1):
            c.wait_recv()
            total = total + self.r1[k].astype(F32)
        self.s1[...] = total.astype(BF16)
        self.r2[at.z] = self.s1[...]
        self.c2 = []
        for k in range(1, at.nz):
            self.c2.append(
                self.go(remote(self.s1, self.r2.at[at.z], self.z_send.at[k - 1], self.z_recv.at[k - 1], at.along_z(k)))
            )

    def start_back(self):
        at, r = self.at, self.r
        for c in self.c2:
            c.wait_recv()
        total = self.r2[0].astype(F32)
        for k in range(1, at.nz):
            total = total + self.r2[k].astype(F32)
        rows = pl.ds(pl.multiple_of(at.p * r, 16), r)
        self.g[at.core, rows, :] = total.astype(BF16)
        self.c3 = []
        for k in range(1, at.plane):
            _, device = at.in_plane(k)
            self.c3.append(
                self.go(
                    remote(
                        self.g.at[at.core, rows], self.g.at[at.core, rows], self.back_send.at[k - 1], self.back_recv.at[k - 1], device
                    )
                )
            )

    def start_share(self):
        at, r = self.at, self.r
        self.c4 = []
        for k in range(at.plane):
            if k:
                self.c3[k - 1].wait_recv()
            p = lax.rem(at.p + at.plane - k, at.plane)
            piece = self.g.at[at.core, pl.ds(pl.multiple_of(p * r, 16), r)]
            self.c4.append(self.go(remote(piece, piece, self.share_send.at[k], self.share_recv.at[k], at.pair())))

    def finish(self):
        for c in self.c4:
            c.wait_recv()
        for c in self.sent:
            c.wait_send()


def kernel(
    dims,
    rows_of,
    coarse_hbm,
    tw_hbm,
    cw_hbm,
    cot_hbm,
    field_out,
    gc_out,
    conv_out,
    tconv_out,
    coarse,
    tw,
    cw,
    cot,
    wide,
    rows_cot,
    *rest,
):
    rest = list(rest)
    cot_halo = {d: rest.pop(0) for d in DIRS}
    coa_halo = {d: rest.pop(0) for d in DIRS}
    back_from = {d: rest.pop(0) for d in BACK}
    back_to = {d: rest.pop(0) for d in BACK}
    up, w1, w2, w4, w3, act, ds, bb, gh, taps, et, cols, local_gc = (rest.pop(0) for _ in range(13))
    bufs = [[rest.pop(0) for _ in range(6)] for _ in range(2)]
    bufs = [b + [out] for b, out in zip(bufs, (conv_out, tconv_out))]
    sems = [[rest.pop(0) for _ in range(9)] for _ in range(2)]
    load_sem, cot_send, cot_recv, coa_send, coa_recv, back_send, back_recv = rest
    nz, ny, nx = dims
    at = Place(nz, ny, nx)

    barrier = pltpu.get_barrier_semaphore()
    others = [at.pair()]
    others += [at.in_plane(k)[1] for k in range(1, at.plane)]
    others += [at.along_z(k) for k in range(1, nz)]
    for device in others:
        pl.semaphore_signal(barrier, inc=1, device_id=device, device_id_type=MESH)
    for d in DIRS:

        @pl.when(at.has(*d))
        def _():
            pl.semaphore_signal(barrier, inc=1, device_id=at.halo(*d), device_id_type=MESH)

    loads = [
        pltpu.make_async_copy(src, dst, load_sem.at[i])
        for i, (src, dst) in enumerate(((cot_hbm, cot), (coarse_hbm, coarse), (tw_hbm, tw), (cw_hbm, cw)))
    ]
    for load in loads:
        load.start()

    count = len(others)
    for d in DIRS:
        count = count + jnp.where(at.has(*d), 1, 0)
    pl.semaphore_wait(barrier, count)

    def coa_copy(i, d):
        (z, dz), (y, dy) = COA_Z[d[0]], COA_Y[d[1]]
        return remote(
            coarse_hbm.at[pl.ds(z, dz), pl.ds(y, dy)], coa_halo[d], coa_send.at[i], coa_recv.at[i], at.halo(*d)
        )

    def cot_copy(i, d):
        (z, dz), (y, dy) = COT_Z[d[0]], COT_Y[d[1]]
        return remote(
            rows_cot.at[pl.ds(z, dz), :, pl.ds(y, dy)], cot_halo[d], cot_send.at[i], cot_recv.at[i], at.halo(*d)
        )

    def back_copy(i, d):
        return remote(back_to[d], back_from[d], back_send.at[i], back_recv.at[i], at.halo(*d))

    def start(copy_of, dirs=DIRS):
        for i, d in enumerate(dirs):

            @pl.when(at.has(*d))
            def _():
                copy_of(i, d).start()

    def arrived(copy_of, dirs=DIRS):
        for i, d in enumerate(dirs):

            @pl.when(at.has(-d[0], -d[1]))
            def _():
                copy_of(i, d).wait_recv()

    start(coa_copy)

    loads[0].wait()
    wide[...] = cot[...].astype(F32)
    for z in (0, 7, 1, 2, 3, 4, 5, 6):
        for y in range(4):
            rows_cot[z, :, y * 128 : y * 128 + 128] = wide[pl.ds(z * 4 + y, C, stride=32), :].astype(BF16)
    start(cot_copy)

    for d in DIRS:

        @pl.when(jnp.logical_not(at.has(-d[0], -d[1])))
        def _():
            cot_halo[d][...] = jnp.zeros_like(cot_halo[d])
            coa_halo[d][...] = jnp.zeros_like(coa_halo[d])
            if d in BACK:
                back_from[d][...] = jnp.zeros_like(back_from[d])

    loads[1].wait()

    loads[2].wait()
    loads[3].wait()
    for kz in range(3):
        for ky in range(3):
            for kx in range(3):
                block = tw[((kz * 3 + ky) * 3 + kx) * C : ((kz * 3 + ky) * 3 + kx + 1) * C, :]
                w1[kz, ky * C : (ky + 1) * C, kx * 128 : kx * 128 + 128] = block
                w3[ky * 3 + kx, kz * C : (kz + 1) * C, :] = block
    for a in range(3):
        tall = jnp.concatenate([cw[(b * 3 + a) * 192 : (b * 3 + a + 1) * 192, :].astype(F32) for b in range(3)], axis=0)
        w4[a * C : (a + 1) * C, :] = tall.T.astype(BF16)
        w2[a * C : (a + 1) * C, :] = jnp.concatenate(
            [
                cw[((b * 3 + a) * 3 + x) * C : ((b * 3 + a) * 3 + x + 1) * C, :].astype(F32)
                for b in (2, 1, 0)
                for x in range(3)
            ],
            axis=1,
        ).astype(BF16)

    lane_at = lax.broadcasted_iota(jnp.int32, (C, 128), 1)
    not_first = jnp.where(lane_at == 0, 0.0, 1.0).astype(F32)
    not_last = jnp.where(lane_at == 127, 0.0, 1.0).astype(F32)

    def taps_of(row):
        return pltpu.roll(row, 1, 1) * not_first, row, pltpu.roll(row, 127, 1) * not_last

    def put_cot(ze, ye, row):
        before, row, after = taps_of(row.astype(F32))
        for i, value in enumerate((after, row, before)):
            bb[pl.ds(ze * 192 + i * C, C), ye * 128 : ye * 128 + 128] = value.astype(BF16)

    @unrolled(0, 8)
    def _(z):
        for y in range(4):
            put_cot(z + 1, y + 1, rows_cot[z, :, y * 128 : y * 128 + 128])

    cell = lax.broadcasted_iota(jnp.int32, (C, 384), 0)
    place = lax.broadcasted_iota(jnp.int32, (C, 384), 1)
    spread = jnp.zeros((C, 384), F32)
    for k in range(3):
        spread = spread + jnp.where(place == 2 * cell + (k - 1) + 128 * k, 1.0, 0.0) * jnp.where(
            jnp.logical_and(place >= 128 * k, place < 128 * k + 128), 1.0, 0.0
        )
    spread = spread.astype(BF16)

    def put_coarse(ze, ye, block):
        wide_block = dot(block.astype(F32).T.astype(BF16), spread).astype(BF16)
        for k in range(3):
            up[pl.ds(ze * 384 + k * 128, 128), ye * 128 : ye * 128 + 128] = wide_block[:, k * 128 : k * 128 + 128]

    @unrolled(0, 4)
    def _(z):
        for y in range(2):
            put_coarse(z + 1, y + 1, coarse[z, y])

    arrived(coa_copy)

    @unrolled(0, 4)
    def _(z):
        put_coarse(z + 1, 0, coa_halo[(0, 1)][z, 0])
        put_coarse(z + 1, 3, coa_halo[(0, -1)][z, 0])

    for dz, ze in ((1, 0), (-1, 5)):
        put_coarse(ze, 0, coa_halo[(dz, 1)][0, 0])
        for y in range(2):
            put_coarse(ze, y + 1, coa_halo[(dz, 0)][0, y])
        put_coarse(ze, 3, coa_halo[(dz, -1)][0, 0])

    has_zl = jnp.where(at.has_z[-1], 1.0, 0.0).astype(F32)
    has_zh = jnp.where(at.has_z[1], 1.0, 0.0).astype(F32)
    has_yl = jnp.where(at.has_y[-1], 1.0, 0.0).astype(F32)
    has_yh = jnp.where(at.has_y[1], 1.0, 0.0).astype(F32)

    def put_hidden(zf, partial, z_mask):
        for yf in range(6):
            n = yf // 2
            if yf % 2:
                h = partial[C : 2 * C, (n + 1) * 128 : (n + 2) * 128]
            else:
                h = partial[2 * C :, n * 128 : n * 128 + 128] + partial[:C, (n + 1) * 128 : (n + 2) * 128]
            mask = z_mask
            if yf in (0, 5):
                y_mask = has_yl if yf == 0 else has_yh
                mask = y_mask if mask is None else mask * y_mask
            s = 0.5 * jnp.tanh(0.5 * h) + 0.5
            row = h * s
            if mask is not None:
                row = row * mask
            for i, value in enumerate(taps_of(row)):
                act[pl.ds(zf * 192 + i * C, C), yf * 128 : yf * 128 + 128] = value.astype(BF16)
            if 0 < zf < 9 and 0 < yf < 5:
                ds[zf - 1, :, (yf - 1) * 128 : yf * 128] = s * (1.0 + h * (1.0 - s))

    w1_odd = jnp.concatenate([w1[2], w1[0]], axis=1)

    @unrolled(0, 5)
    def _(m):
        start = m * 384
        odd = dot(w1_odd, up[pl.ds(start, 768), :])
        put_hidden(2 * m, odd, has_zl if m == 0 else None)
        even = dot(w1[1], up[pl.ds(start + 384, 384), :])
        put_hidden(2 * m + 1, even, has_zh if m == 4 else None)

    gc_v, gt_v = bufs[0][0], bufs[1][0]
    conv_sum = Reduction(at, rows_of[0], bufs[0], sems[0])
    tconv_sum = Reduction(at, rows_of[1], bufs[1], sems[1])
    taps[...] = jnp.zeros_like(taps)

    @unrolled(0, 8)
    def _(z):
        blocks = [
            act[pl.ds((z + dz) * 192 + C, C), dy * 128 : dy * 128 + 512]
            for dz in range(3)
            for dy in range(3)
        ]
        right = bb[pl.ds((z + 1) * 192, 192), 128:640]
        taps[...] += dot_nt(jnp.concatenate(blocks, axis=0), right)

    def fill(v, half_rows, parts):
        at_row = 0
        for part in parts:
            done, n = 0, part.shape[0]
            while done < n:
                half, row = divmod(at_row, half_rows)
                m = min(n - done, half_rows - row)
                v[half, row : row + m, :] = part[done : done + m, :].astype(BF16)
                done, at_row = done + m, at_row + m
        while at_row < 2 * half_rows:
            half, row = divmod(at_row, half_rows)
            v[half, row:, :] = jnp.zeros((half_rows - row, 128), BF16)
            at_row += half_rows - row

    fill(
        gc_v,
        at.plane * rows_of[0],
        [taps[:, :128], jnp.concatenate([taps[:288, 128:], taps[288:, 128:]], axis=1)],
    )
    conv_sum.start_pair()

    arrived(cot_copy)

    @unrolled(0, 8)
    def _(z):
        put_cot(z + 1, 0, cot_halo[(0, 1)][z])
        put_cot(z + 1, 5, cot_halo[(0, -1)][z])

    for dz, ze in ((1, 0), (-1, 9)):
        put_cot(ze, 0, cot_halo[(dz, 1)][0])
        for y in range(4):
            put_cot(ze, y + 1, cot_halo[(dz, 0)][0, :, y * 128 : y * 128 + 128])
        put_cot(ze, 5, cot_halo[(dz, -1)][0])
    conv_sum.start_plane()

    for half in range(2):
        for q in (0, 9):
            gh[half, q * C : q * C + C, :] = jnp.zeros((C, 256), BF16)

    @unrolled(0, 8)
    def _(z):
        partial = dot(w2[...], bb[pl.ds(z * 192, 576), :])
        for y in range(4):
            ga = partial[:C, (y + 2) * 128 : (y + 3) * 128]
            ga = ga + partial[C : 2 * C, (y + 1) * 128 : (y + 2) * 128]
            ga = ga + partial[2 * C :, y * 128 : y * 128 + 128]
            gh[y % 2, (z + 1) * C : (z + 2) * C, y // 2 * 128 : y // 2 * 128 + 128] = (
                ga * ds[z, :, y * 128 : y * 128 + 128]
            ).astype(BF16)

    def picks(shape, f_dim):
        f = lax.broadcasted_iota(jnp.int32, shape, f_dim)
        c = lax.broadcasted_iota(jnp.int32, shape, 1 - f_dim)
        out = jnp.zeros(shape, F32)
        for k in range(3):
            for y in range(2):
                cell0 = k * 128 + y * C
                inside = jnp.logical_and(c >= cell0, c < cell0 + C)
                hit = jnp.logical_and(f == 2 * (c - cell0) + (k - 1) + 128 * y, inside)
                own = jnp.logical_and(f >= 128 * y, f < 128 * y + 128)
                out = out + jnp.where(jnp.logical_and(hit, own), 1.0, 0.0)
        return out.astype(BF16)

    pick = picks((256, 384), 0)
    for half in range(2):
        some = dot(gh[half, C : 9 * C, :], pick).astype(BF16)
        for z in range(8):
            for kx in range(3):
                cols[z % 2, half, kx * C : (kx + 1) * C, z // 2 * 128 : z // 2 * 128 + 128] = some[
                    z * C : (z + 1) * C, kx * 128 : kx * 128 + 128
                ]

    def cells(z, y):
        if z < 4 and y < 2:
            return coarse[z, y]
        if z < 4:
            return coa_halo[(0, -1)][z, 0]
        return coa_halo[(-1, 0)][0, y] if y < 2 else coa_halo[(-1, -1)][0, 0]

    by_tap = {}
    for odd_z in range(2):
        for odd_y in range(2):
            shifts = [(z, y) for z in range(odd_z + 1) for y in range(odd_y + 1)]
            right = jnp.concatenate(
                [
                    jnp.concatenate([cells(z + sz, y + sy) for z in range(4) for y in range(2)], axis=0)
                    for sz, sy in shifts
                ],
                axis=1,
            )
            result = dot(cols[odd_z, odd_y], right)
            for n, (sz, sy) in enumerate(shifts):
                kz = 1 if not odd_z else 2 - 2 * sz
                ky = 1 if not odd_y else 2 - 2 * sy
                by_tap[kz, ky] = result[:, n * 128 : n * 128 + 128]
    fill(gt_v, at.plane * rows_of[1], [by_tap[kz, ky] for kz in range(3) for ky in range(3)])
    tconv_sum.start_pair()
    conv_sum.start_z()

    pick_t = picks((384, 256), 1)
    for half in range(2):
        et[half] = dot_nt(pick_t, gh[half]).astype(BF16)

    def gather(ky, zc):
        total = None
        for kx in range(3):
            rows = slice(kx * 128, kx * 128 + 128)
            if zc < 4:
                term = dot(et[int(ky != 1), rows, zc * 128 : zc * 128 + 192], w3[ky * 3 + kx])
            else:
                term = dot(et[int(ky != 1), rows, 512:576], w3[ky * 3 + kx, :C, :])
            total = term if total is None else total + term
        return total

    for zc in (4, 3, 2, 1, 0):
        low = gather(1, zc) + gather(2, zc)
        high = gather(0, zc)
        rows = (low[:C], low[C:] + high[:C])
        if zc < 4:
            for y in range(2):
                local_gc[zc, y] = rows[y]
            back_to[(0, 1)][zc] = high[C:].astype(BF16)
        else:
            for y in range(2):
                back_to[(1, 0)][y] = rows[y].astype(BF16)
            back_to[(1, 1)][0] = high[C:].astype(BF16)
    tconv_sum.start_plane()
    start(back_copy, BACK)
    conv_sum.start_back()

    @unrolled(0, 8)
    def _(z):
        partial = dot(w4[...], act[pl.ds(z * 192, 576), :])
        for y in range(4):
            row = partial[:C, y * 128 : y * 128 + 128]
            row = row + partial[C : 2 * C, (y + 1) * 128 : (y + 2) * 128]
            row = row + partial[2 * C :, (y + 2) * 128 : (y + 3) * 128]
            wide[pl.ds(z * 4 + y, C, stride=32), :] = row

    field_out[...] = wide[...].astype(BF16)
    tconv_sum.start_z()
    conv_sum.start_share()

    arrived(back_copy, BACK)
    for zc in range(4):
        for y in range(2):
            total = local_gc[zc, y]
            if y == 0:
                total = total + back_from[(0, 1)][zc].astype(F32)
            if zc == 0:
                total = total + back_from[(1, 0)][y].astype(F32)
            if zc == 0 and y == 0:
                total = total + back_from[(1, 1)][0].astype(F32)
            gc_out[zc, y] = total.astype(BF16)
    tconv_sum.start_back()
    conv_sum.finish()
    tconv_sum.start_share()
    tconv_sum.finish()

    def sent(copy_of, dirs=DIRS):
        for i, d in enumerate(dirs):

            @pl.when(at.has(*d))
            def _():
                copy_of(i, d).wait_send()

    sent(coa_copy)
    sent(cot_copy)
    sent(back_copy, BACK)


def unpack(n_dev, field_in, gc_in, conv_in, tconv_in, field_out, gc_out, gcw_out, gtw_out, conv, tconv, gcw, gtw, sems):
    copies = [
        pltpu.make_async_copy(src, dst, sems.at[i])
        for i, (src, dst) in enumerate(
            ((conv_in, conv), (tconv_in, tconv), (field_in, field_out), (gc_in, gc_out), (gcw, gcw_out), (gtw, gtw_out))
        )
    ]
    for copy in copies[:4]:
        copy.start()
    copies[0].wait()
    conv_scale = 1.0 / math.sqrt(n_dev * 8 * 4 * 128)
    g = conv[...].reshape(-1, 128)
    first = g[:576].astype(F32) * conv_scale
    second = g[576:864].astype(F32) * conv_scale
    for zy in range(9):
        for dx in range(2):
            gcw[zy * 3 + dx] = first[zy * C : (zy + 1) * C, dx * C : (dx + 1) * C]
    for half in range(18):
        src = second[(half % 9) * 32 : (half % 9) * 32 + 32, (half // 9) * C : (half // 9 + 1) * C]
        gcw[(half // 2) * 3 + 2, (half % 2) * 32 : (half % 2) * 32 + 32, :] = src
    copies[4].start()
    copies[1].wait()
    tconv_scale = 1.0 / math.sqrt(n_dev * 4 * 2 * 64)
    gtw[...] = tconv[...].reshape(-1, 128)[:1728].astype(F32) * tconv_scale
    copies[5].start()
    for copy in copies[2:]:
        copy.wait()


def solution(mesh):
    nx = mesh.shape["group"]
    n_slab = mesh.shape["slab"]
    ny = 4
    nz = n_slab // (2 * ny)
    plane = ny * nx
    rows_of = [ceil16(-(-n // (2 * plane))) for n in (864, 1728)]

    def step(coarse, tw, cw, cot):
        dma = pltpu.SemaphoreType.DMA
        vmem = pltpu.VMEM
        scratch = [
            vmem((4, 2, 64, CIN), BF16),
            vmem((27 * C, CIN), BF16),
            vmem((27 * C, C), BF16),
            vmem((2048, 128), BF16),
            vmem((2048, 128), F32),
            vmem((8, C, 512), BF16),
        ]
        scratch += [vmem((COT_Z[dz][1], C, COT_Y[dy][1]), BF16) for dz, dy in DIRS]
        scratch += [vmem((COA_Z[dz][1], COA_Y[dy][1], 64, CIN), BF16) for dz, dy in DIRS]
        scratch += [vmem(shape, BF16) for shape in BACK.values()] * 2
        scratch += [
            vmem((6 * 384, 512), BF16),
            vmem((3, 192, 384), BF16),
            vmem((192, 576), BF16),
            vmem((192, 576), BF16),
            vmem((9, 192, CIN), BF16),
            vmem((10 * 192, 768), BF16),
            vmem((8, C, 512), F32),
            vmem((10 * 192, 768), BF16),
            vmem((2, 10 * C, 256), BF16),
            vmem((576, 192), F32),
            vmem((2, 384, 640), BF16),
            vmem((2, 2, 192, 512), BF16),
            vmem((4, 2, 64, CIN), F32),
        ]
        for r in rows_of:
            scratch += [
                vmem((2, plane * r, 128), BF16),
                vmem((plane * r, 128), BF16),
                vmem((plane * r, 128), BF16),
                vmem((plane - 1, r, 128), BF16),
                vmem((r, 128), BF16),
                vmem((nz, r, 128), BF16),
            ]
        for r in rows_of:
            scratch += [dma((2,)), dma((plane - 1,)), dma((plane - 1,)), dma((nz - 1,)), dma((nz - 1,))]
            scratch += [dma((plane - 1,)), dma((plane - 1,)), dma((plane,)), dma((plane,))]
        scratch += [dma((4,)), dma((8,)), dma((8,)), dma((8,)), dma((8,)), dma((3,)), dma((3,))]
        in_hbm = pl.BlockSpec(memory_space=pltpu.HBM)
        in_vmem = pl.BlockSpec(memory_space=pltpu.VMEM)
        parts = pl.pallas_call(
            functools.partial(kernel, (nz, ny, nx), rows_of),
            out_shape=(
                jax.ShapeDtypeStruct((2048, 128), BF16),
                jax.ShapeDtypeStruct((4, 2, 64, CIN), BF16),
                jax.ShapeDtypeStruct((2, plane * rows_of[0], 128), BF16),
                jax.ShapeDtypeStruct((2, plane * rows_of[1], 128), BF16),
            ),
            in_specs=[in_hbm] * 4,
            out_specs=(in_vmem,) * 4,
            scratch_shapes=scratch,
            compiler_params=pltpu.CompilerParams(
                collective_id=0, has_side_effects=True, vmem_limit_bytes=61 * 2**20
            ),
            cost_estimate=pl.CostEstimate(flops=7 * 10**9, bytes_accessed=4 * 10**6, transcendentals=500000),
        )(
            coarse.reshape(4, 2, 64, CIN),
            jnp.swapaxes(tw, 3, 4).reshape(27 * C, CIN),
            cw.reshape(27 * C, C),
            cot.reshape(2048, 128),
        )
        any_space = pl.BlockSpec(memory_space=pl.ANY)
        field, gc, gcw, gtw = pl.pallas_call(
            functools.partial(unpack, n_slab * nx),
            out_shape=(
                jax.ShapeDtypeStruct((2048, 128), BF16),
                jax.ShapeDtypeStruct((4, 2, 64, CIN), BF16),
                jax.ShapeDtypeStruct((27, C, C), F32),
                jax.ShapeDtypeStruct((27 * C, CIN), F32),
            ),
            in_specs=[any_space] * 4,
            out_specs=(any_space,) * 4,
            scratch_shapes=[
                vmem(parts[2].shape, BF16),
                vmem(parts[3].shape, BF16),
                vmem((27, C, C), F32),
                vmem((27 * C, CIN), F32),
                dma((6,)),
            ],
            compiler_params=pltpu.CompilerParams(vmem_limit_bytes=61 * 2**20),
        )(*parts)
        return (
            field.reshape(1, 1, C, 8, 4, 128),
            gc.reshape(1, 1, 4, 2, 64, CIN),
            gcw.reshape(3, 3, 3, C, C),
            jnp.swapaxes(gtw.reshape(3, 3, 3, C, CIN), 3, 4),
        )

    blocks = P("group", "slab", None, None, None, None)
    return jax.shard_map(
        step,
        mesh=mesh,
        in_specs=(blocks, P(), P(), blocks),
        out_specs=(blocks, blocks, P(), P()),
        check_vma=False,
    )
```

```python
import functools
import math

import jax
import jax.numpy as jnp
from jax import lax
from jax.experimental import pallas as pl
from jax.experimental.pallas import tpu as pltpu
from jax.sharding import PartitionSpec as P

MESH = pl.DeviceIdType.MESH
F32 = jnp.float32
BF16 = jnp.bfloat16
PY = 4
CIN = 128
C = 64
NT = (((1,), (1,)), ((), ()))

DIRS = [(0, 1), (0, -1), (1, 0), (-1, 0), (1, 1), (1, -1), (-1, 1), (-1, -1)]
COT_Z = {1: (7, 1), 0: (0, 8), -1: (0, 1)}
COT_Y = {1: (384, 128), 0: (0, 512), -1: (0, 128)}
COA_Z = {1: (3, 1), 0: (0, 4), -1: (0, 1)}
COA_Y = {1: (1, 1), 0: (0, 2), -1: (0, 1)}
BACK = {(0, 1): (4, 64, CIN), (1, 0): (2, 64, CIN), (1, 1): (1, 64, CIN)}


def dot(a, b):
    return jnp.dot(a, b, preferred_element_type=F32)


def dot_nt(a, b):
    return lax.dot_general(a, b, NT, preferred_element_type=F32)


def unrolled(start, stop):
    def run(body):
        for i in range(start, stop):
            body(i)

    return run


def ceil16(n):
    return -(-n // 16) * 16


class Place:
    def __init__(self, nz, ny, nx):
        self.nz, self.ny, self.nx = nz, ny, nx
        self.plane = ny * nx
        self.slab = lax.axis_index("slab")
        self.x = lax.axis_index("group")
        self.core = lax.rem(self.slab, 2)
        chip = lax.div(self.slab, 2)
        self.y = lax.rem(chip, ny)
        self.z = lax.div(chip, ny)
        self.p = self.y * nx + self.x
        lane = lax.rem(self.slab, PY)
        zb = lax.div(self.slab, PY)
        self.has_y = {1: lane < PY - 1, -1: lane > 0}
        self.has_z = {1: zb < nz * ny * 2 // PY - 1, -1: zb > 0}

    def has(self, dz, dy):
        if dz == 0:
            return self.has_y[dy]
        if dy == 0:
            return self.has_z[dz]
        return jnp.logical_and(self.has_z[dz], self.has_y[dy])

    def halo(self, dz, dy):
        return (self.slab + PY * dz + dy, self.x)

    def pair(self):
        return (self.slab + 1 - 2 * self.core, self.x)

    def in_plane(self, k):
        p = lax.rem(self.p + k, self.plane)
        y, x = lax.div(p, self.nx), lax.rem(p, self.nx)
        return p, ((self.z * self.ny + y) * 2 + self.core, x)

    def along_z(self, k):
        z = lax.rem(self.z + k, self.nz)
        return ((z * self.ny + self.y) * 2 + self.core, self.x)


def remote(src, dst, send, recv, device):
    return pltpu.make_async_remote_copy(
        src_ref=src, dst_ref=dst, send_sem=send, recv_sem=recv, device_id=device, device_id_type=MESH
    )


class Reduction:
    def __init__(self, at, rows, bufs, sems):
        self.at, self.r = at, rows
        self.v, self.r0, self.s0, self.r1, self.s1, self.r2, self.g = bufs
        self.pair_sems, self.plane_send, self.plane_recv, self.z_send, self.z_recv, self.back_send, self.back_recv = sems[:7]
        self.share_send, self.share_recv = sems[7:]
        self.sent = []

    def go(self, copy):
        copy.start()
        self.sent.append(copy)
        return copy

    def start_pair(self):
        at = self.at
        self.c0 = self.go(remote(self.v.at[1 - at.core], self.r0, self.pair_sems.at[0], self.pair_sems.at[1], at.pair()))

    def start_plane(self):
        at, r = self.at, self.r
        self.c0.wait_recv()
        self.s0[...] = (self.v[at.core].astype(F32) + self.r0[...].astype(F32)).astype(BF16)
        self.c1 = []
        for k in range(1, at.plane):
            p, device = at.in_plane(k)
            rows = pl.ds(pl.multiple_of(p * r, 16), r)
            self.c1.append(
                self.go(remote(self.s0.at[rows], self.r1.at[k - 1], self.plane_send.at[k - 1], self.plane_recv.at[k - 1], device))
            )

    def start_z(self):
        at, r = self.at, self.r
        total = self.s0[pl.ds(pl.multiple_of(at.p * r, 16), r), :].astype(F32)
        for k, c in enumerate(self.c1):
            c.wait_recv()
            total = total + self.r1[k].astype(F32)
        self.s1[...] = total.astype(BF16)
        self.r2[at.z] = self.s1[...]
        self.c2 = []
        for k in range(1, at.nz):
            self.c2.append(
                self.go(remote(self.s1, self.r2.at[at.z], self.z_send.at[k - 1], self.z_recv.at[k - 1], at.along_z(k)))
            )

    def start_back(self):
        at, r = self.at, self.r
        for c in self.c2:
            c.wait_recv()
        total = self.r2[0].astype(F32)
        for k in range(1, at.nz):
            total = total + self.r2[k].astype(F32)
        rows = pl.ds(pl.multiple_of(at.p * r, 16), r)
        self.g[at.core, rows, :] = total.astype(BF16)
        self.c3 = []
        for k in range(1, at.plane):
            _, device = at.in_plane(k)
            self.c3.append(
                self.go(
                    remote(
                        self.g.at[at.core, rows], self.g.at[at.core, rows], self.back_send.at[k - 1], self.back_recv.at[k - 1], device
                    )
                )
            )

    def start_share(self):
        at, r = self.at, self.r
        self.c4 = []
        for k in range(at.plane):
            if k:
                self.c3[k - 1].wait_recv()
            p = lax.rem(at.p + at.plane - k, at.plane)
            piece = self.g.at[at.core, pl.ds(pl.multiple_of(p * r, 16), r)]
            self.c4.append(self.go(remote(piece, piece, self.share_send.at[k], self.share_recv.at[k], at.pair())))

    def finish(self):
        for c in self.c4:
            c.wait_recv()
        for c in self.sent:
            c.wait_send()


def kernel(
    dims,
    rows_of,
    coarse_hbm,
    tw_hbm,
    cw_hbm,
    cot_hbm,
    field_out,
    gc_out,
    conv_out,
    tconv_out,
    coarse,
    tw,
    cw,
    cot,
    wide,
    rows_cot,
    *rest,
):
    rest = list(rest)
    cot_halo = {d: rest.pop(0) for d in DIRS}
    coa_halo = {d: rest.pop(0) for d in DIRS}
    back_from = {d: rest.pop(0) for d in BACK}
    back_to = {d: rest.pop(0) for d in BACK}
    up, w1, w2, w4, w3, act, ds, bb, gh, taps, et, cols, local_gc = (rest.pop(0) for _ in range(13))
    bufs = [[rest.pop(0) for _ in range(6)] for _ in range(2)]
    bufs = [b + [out] for b, out in zip(bufs, (conv_out, tconv_out))]
    sems = [[rest.pop(0) for _ in range(9)] for _ in range(2)]
    load_sem, cot_send, cot_recv, coa_send, coa_recv, back_send, back_recv = rest
    nz, ny, nx = dims
    at = Place(nz, ny, nx)

    barrier = pltpu.get_barrier_semaphore()
    others = [at.pair()]
    others += [at.in_plane(k)[1] for k in range(1, at.plane)]
    others += [at.along_z(k) for k in range(1, nz)]
    for device in others:
        pl.semaphore_signal(barrier, inc=1, device_id=device, device_id_type=MESH)
    for d in DIRS:

        @pl.when(at.has(*d))
        def _():
            pl.semaphore_signal(barrier, inc=1, device_id=at.halo(*d), device_id_type=MESH)

    loads = [
        pltpu.make_async_copy(src, dst, load_sem.at[i])
        for i, (src, dst) in enumerate(((cot_hbm, cot), (coarse_hbm, coarse), (tw_hbm, tw), (cw_hbm, cw)))
    ]
    for load in loads:
        load.start()

    count = len(others)
    for d in DIRS:
        count = count + jnp.where(at.has(*d), 1, 0)
    pl.semaphore_wait(barrier, count)

    def coa_copy(i, d):
        (z, dz), (y, dy) = COA_Z[d[0]], COA_Y[d[1]]
        return remote(
            coarse_hbm.at[pl.ds(z, dz), pl.ds(y, dy)], coa_halo[d], coa_send.at[i], coa_recv.at[i], at.halo(*d)
        )

    def cot_copy(i, d):
        (z, dz), (y, dy) = COT_Z[d[0]], COT_Y[d[1]]
        return remote(
            rows_cot.at[pl.ds(z, dz), :, pl.ds(y, dy)], cot_halo[d], cot_send.at[i], cot_recv.at[i], at.halo(*d)
        )

    def back_copy(i, d):
        return remote(back_to[d], back_from[d], back_send.at[i], back_recv.at[i], at.halo(*d))

    def start(copy_of, dirs=DIRS):
        for i, d in enumerate(dirs):

            @pl.when(at.has(*d))
            def _():
                copy_of(i, d).start()

    def arrived(copy_of, dirs=DIRS):
        for i, d in enumerate(dirs):

            @pl.when(at.has(-d[0], -d[1]))
            def _():
                copy_of(i, d).wait_recv()

    start(coa_copy)

    loads[0].wait()
    wide[...] = cot[...].astype(F32)
    for z in (0, 7, 1, 2, 3, 4, 5, 6):
        for y in range(4):
            rows_cot[z, :, y * 128 : y * 128 + 128] = wide[pl.ds(z * 4 + y, C, stride=32), :].astype(BF16)
    start(cot_copy)

    for d in DIRS:

        @pl.when(jnp.logical_not(at.has(-d[0], -d[1])))
        def _():
            cot_halo[d][...] = jnp.zeros_like(cot_halo[d])
            coa_halo[d][...] = jnp.zeros_like(coa_halo[d])
            if d in BACK:
                back_from[d][...] = jnp.zeros_like(back_from[d])

    loads[1].wait()

    loads[2].wait()
    loads[3].wait()
    for kz in range(3):
        for ky in range(3):
            for kx in range(3):
                block = tw[((kz * 3 + ky) * 3 + kx) * C : ((kz * 3 + ky) * 3 + kx + 1) * C, :]
                w1[kz, ky * C : (ky + 1) * C, kx * 128 : kx * 128 + 128] = block
                w3[ky * 3 + kx, kz * C : (kz + 1) * C, :] = block
    for a in range(3):
        tall = jnp.concatenate([cw[(b * 3 + a) * 192 : (b * 3 + a + 1) * 192, :].astype(F32) for b in range(3)], axis=0)
        w4[a * C : (a + 1) * C, :] = tall.T.astype(BF16)
        w2[a * C : (a + 1) * C, :] = jnp.concatenate(
            [
                cw[((b * 3 + a) * 3 + x) * C : ((b * 3 + a) * 3 + x + 1) * C, :].astype(F32)
                for b in (2, 1, 0)
                for x in range(3)
            ],
            axis=1,
        ).astype(BF16)

    lane_at = lax.broadcasted_iota(jnp.int32, (C, 128), 1)
    not_first = jnp.where(lane_at == 0, 0.0, 1.0).astype(F32)
    not_last = jnp.where(lane_at == 127, 0.0, 1.0).astype(F32)

    def taps_of(row):
        return pltpu.roll(row, 1, 1) * not_first, row, pltpu.roll(row, 127, 1) * not_last

    def put_cot(ze, ye, row):
        before, row, after = taps_of(row.astype(F32))
        for i, value in enumerate((after, row, before)):
            bb[pl.ds(ze * 192 + i * C, C), ye * 128 : ye * 128 + 128] = value.astype(BF16)

    @unrolled(0, 8)
    def _(z):
        for y in range(4):
            put_cot(z + 1, y + 1, rows_cot[z, :, y * 128 : y * 128 + 128])

    cell = lax.broadcasted_iota(jnp.int32, (C, 384), 0)
    place = lax.broadcasted_iota(jnp.int32, (C, 384), 1)
    spread = jnp.zeros((C, 384), F32)
    for k in range(3):
        spread = spread + jnp.where(place == 2 * cell + (k - 1) + 128 * k, 1.0, 0.0) * jnp.where(
            jnp.logical_and(place >= 128 * k, place < 128 * k + 128), 1.0, 0.0
        )
    spread = spread.astype(BF16)

    def put_coarse(ze, ye, block):
        wide_block = dot(block.astype(F32).T.astype(BF16), spread).astype(BF16)
        for k in range(3):
            up[pl.ds(ze * 384 + k * 128, 128), ye * 128 : ye * 128 + 128] = wide_block[:, k * 128 : k * 128 + 128]

    @unrolled(0, 4)
    def _(z):
        for y in range(2):
            put_coarse(z + 1, y + 1, coarse[z, y])

    arrived(coa_copy)

    @unrolled(0, 4)
    def _(z):
        put_coarse(z + 1, 0, coa_halo[(0, 1)][z, 0])
        put_coarse(z + 1, 3, coa_halo[(0, -1)][z, 0])

    for dz, ze in ((1, 0), (-1, 5)):
        put_coarse(ze, 0, coa_halo[(dz, 1)][0, 0])
        for y in range(2):
            put_coarse(ze, y + 1, coa_halo[(dz, 0)][0, y])
        put_coarse(ze, 3, coa_halo[(dz, -1)][0, 0])

    has_zl = jnp.where(at.has_z[-1], 1.0, 0.0).astype(F32)
    has_zh = jnp.where(at.has_z[1], 1.0, 0.0).astype(F32)
    has_yl = jnp.where(at.has_y[-1], 1.0, 0.0).astype(F32)
    has_yh = jnp.where(at.has_y[1], 1.0, 0.0).astype(F32)

    def put_hidden(zf, partial, z_mask):
        for yf in range(6):
            n = yf // 2
            if yf % 2:
                h = partial[C : 2 * C, (n + 1) * 128 : (n + 2) * 128]
            else:
                h = partial[2 * C :, n * 128 : n * 128 + 128] + partial[:C, (n + 1) * 128 : (n + 2) * 128]
            mask = z_mask
            if yf in (0, 5):
                y_mask = has_yl if yf == 0 else has_yh
                mask = y_mask if mask is None else mask * y_mask
            s = 0.5 * jnp.tanh(0.5 * h) + 0.5
            row = h * s
            if mask is not None:
                row = row * mask
            for i, value in enumerate(taps_of(row)):
                act[pl.ds(zf * 192 + i * C, C), yf * 128 : yf * 128 + 128] = value.astype(BF16)
            if 0 < zf < 9 and 0 < yf < 5:
                ds[zf - 1, :, (yf - 1) * 128 : yf * 128] = s * (1.0 + h * (1.0 - s))

    w1_odd = jnp.concatenate([w1[2], w1[0]], axis=1)

    @unrolled(0, 5)
    def _(m):
        start = m * 384
        odd = dot(w1_odd, up[pl.ds(start, 768), :])
        put_hidden(2 * m, odd, has_zl if m == 0 else None)
        even = dot(w1[1], up[pl.ds(start + 384, 384), :])
        put_hidden(2 * m + 1, even, has_zh if m == 4 else None)

    gc_v, gt_v = bufs[0][0], bufs[1][0]
    conv_sum = Reduction(at, rows_of[0], bufs[0], sems[0])
    tconv_sum = Reduction(at, rows_of[1], bufs[1], sems[1])
    taps[...] = jnp.zeros_like(taps)

    @unrolled(0, 8)
    def _(z):
        blocks = [
            act[pl.ds((z + dz) * 192 + C, C), dy * 128 : dy * 128 + 512]
            for dz in range(3)
            for dy in range(3)
        ]
        right = bb[pl.ds((z + 1) * 192, 192), 128:640]
        taps[...] += dot_nt(jnp.concatenate(blocks, axis=0), right)

    def fill(v, half_rows, parts):
        at_row = 0
        for part in parts:
            done, n = 0, part.shape[0]
            while done < n:
                half, row = divmod(at_row, half_rows)
                m = min(n - done, half_rows - row)
                v[half, row : row + m, :] = part[done : done + m, :].astype(BF16)
                done, at_row = done + m, at_row + m
        while at_row < 2 * half_rows:
            half, row = divmod(at_row, half_rows)
            v[half, row:, :] = jnp.zeros((half_rows - row, 128), BF16)
            at_row += half_rows - row

    fill(
        gc_v,
        at.plane * rows_of[0],
        [taps[:, :128], jnp.concatenate([taps[:288, 128:], taps[288:, 128:]], axis=1)],
    )
    conv_sum.start_pair()

    arrived(cot_copy)

    @unrolled(0, 8)
    def _(z):
        put_cot(z + 1, 0, cot_halo[(0, 1)][z])
        put_cot(z + 1, 5, cot_halo[(0, -1)][z])

    for dz, ze in ((1, 0), (-1, 9)):
        put_cot(ze, 0, cot_halo[(dz, 1)][0])
        for y in range(4):
            put_cot(ze, y + 1, cot_halo[(dz, 0)][0, :, y * 128 : y * 128 + 128])
        put_cot(ze, 5, cot_halo[(dz, -1)][0])
    conv_sum.start_plane()

    for half in range(2):
        for q in (0, 9):
            gh[half, q * C : q * C + C, :] = jnp.zeros((C, 256), BF16)

    @unrolled(0, 8)
    def _(z):
        partial = dot(w2[...], bb[pl.ds(z * 192, 576), :])
        for y in range(4):
            ga = partial[:C, (y + 2) * 128 : (y + 3) * 128]
            ga = ga + partial[C : 2 * C, (y + 1) * 128 : (y + 2) * 128]
            ga = ga + partial[2 * C :, y * 128 : y * 128 + 128]
            gh[y % 2, (z + 1) * C : (z + 2) * C, y // 2 * 128 : y // 2 * 128 + 128] = (
                ga * ds[z, :, y * 128 : y * 128 + 128]
            ).astype(BF16)

    def picks(shape, f_dim):
        f = lax.broadcasted_iota(jnp.int32, shape, f_dim)
        c = lax.broadcasted_iota(jnp.int32, shape, 1 - f_dim)
        out = jnp.zeros(shape, F32)
        for k in range(3):
            for y in range(2):
                cell0 = k * 128 + y * C
                inside = jnp.logical_and(c >= cell0, c < cell0 + C)
                hit = jnp.logical_and(f == 2 * (c - cell0) + (k - 1) + 128 * y, inside)
                own = jnp.logical_and(f >= 128 * y, f < 128 * y + 128)
                out = out + jnp.where(jnp.logical_and(hit, own), 1.0, 0.0)
        return out.astype(BF16)

    pick = picks((256, 384), 0)
    for half in range(2):
        some = dot(gh[half, C : 9 * C, :], pick).astype(BF16)
        for z in range(8):
            for kx in range(3):
                cols[z % 2, half, kx * C : (kx + 1) * C, z // 2 * 128 : z // 2 * 128 + 128] = some[
                    z * C : (z + 1) * C, kx * 128 : kx * 128 + 128
                ]

    def cells(z, y):
        if z < 4 and y < 2:
            return coarse[z, y]
        if z < 4:
            return coa_halo[(0, -1)][z, 0]
        return coa_halo[(-1, 0)][0, y] if y < 2 else coa_halo[(-1, -1)][0, 0]

    by_tap = {}
    for odd_z in range(2):
        for odd_y in range(2):
            shifts = [(z, y) for z in range(odd_z + 1) for y in range(odd_y + 1)]
            right = jnp.concatenate(
                [
                    jnp.concatenate([cells(z + sz, y + sy) for z in range(4) for y in range(2)], axis=0)
                    for sz, sy in shifts
                ],
                axis=1,
            )
            result = dot(cols[odd_z, odd_y], right)
            for n, (sz, sy) in enumerate(shifts):
                kz = 1 if not odd_z else 2 - 2 * sz
                ky = 1 if not odd_y else 2 - 2 * sy
                by_tap[kz, ky] = result[:, n * 128 : n * 128 + 128]
    fill(gt_v, at.plane * rows_of[1], [by_tap[kz, ky] for kz in range(3) for ky in range(3)])
    tconv_sum.start_pair()
    conv_sum.start_z()

    pick_t = picks((384, 256), 1)
    for half in range(2):
        et[half] = dot_nt(pick_t, gh[half]).astype(BF16)

    def gather(ky, zc):
        total = None
        for kx in range(3):
            rows = slice(kx * 128, kx * 128 + 128)
            if zc < 4:
                term = dot(et[int(ky != 1), rows, zc * 128 : zc * 128 + 192], w3[ky * 3 + kx])
            else:
                term = dot(et[int(ky != 1), rows, 512:576], w3[ky * 3 + kx, :C, :])
            total = term if total is None else total + term
        return total

    for zc in (4, 3, 2, 1, 0):
        low = gather(1, zc) + gather(2, zc)
        high = gather(0, zc)
        rows = (low[:C], low[C:] + high[:C])
        if zc < 4:
            for y in range(2):
                local_gc[zc, y] = rows[y]
            back_to[(0, 1)][zc] = high[C:].astype(BF16)
        else:
            for y in range(2):
                back_to[(1, 0)][y] = rows[y].astype(BF16)
            back_to[(1, 1)][0] = high[C:].astype(BF16)
    tconv_sum.start_plane()
    start(back_copy, BACK)
    conv_sum.start_back()

    @unrolled(0, 8)
    def _(z):
        partial = dot(w4[...], act[pl.ds(z * 192, 576), :])
        for y in range(4):
            row = partial[:C, y * 128 : y * 128 + 128]
            row = row + partial[C : 2 * C, (y + 1) * 128 : (y + 2) * 128]
            row = row + partial[2 * C :, (y + 2) * 128 : (y + 3) * 128]
            wide[pl.ds(z * 4 + y, C, stride=32), :] = row

    field_out[...] = wide[...].astype(BF16)
    tconv_sum.start_z()
    conv_sum.start_share()

    arrived(back_copy, BACK)
    for zc in range(4):
        for y in range(2):
            total = local_gc[zc, y]
            if y == 0:
                total = total + back_from[(0, 1)][zc].astype(F32)
            if zc == 0:
                total = total + back_from[(1, 0)][y].astype(F32)
            if zc == 0 and y == 0:
                total = total + back_from[(1, 1)][0].astype(F32)
            gc_out[zc, y] = total.astype(BF16)
    tconv_sum.start_back()
    conv_sum.finish()
    tconv_sum.start_share()
    tconv_sum.finish()

    def sent(copy_of, dirs=DIRS):
        for i, d in enumerate(dirs):

            @pl.when(at.has(*d))
            def _():
                copy_of(i, d).wait_send()

    sent(coa_copy)
    sent(cot_copy)
    sent(back_copy, BACK)


def unpack(n_dev, *refs):
    ins, outs, held, (gcw, gtw), (sems,) = refs[:4], refs[4:8], refs[8:12], refs[12:14], refs[14:]
    loads = [pltpu.make_async_copy(src, dst, sems.at[i]) for i, (src, dst) in enumerate(zip(ins, held))]
    stores = [
        pltpu.make_async_copy(src, dst, sems.at[4 + i])
        for i, (src, dst) in enumerate(zip((held[0], held[1], gcw, gtw), outs))
    ]
    for i in (2, 3, 0, 1):
        loads[i].start()
    conv, tconv = held[2:]
    loads[2].wait()
    conv_scale = 1.0 / math.sqrt(n_dev * 8 * 4 * 128)
    g = conv[...].reshape(-1, 128)
    first = g[:576].astype(F32) * conv_scale
    second = g[576:864].astype(F32) * conv_scale
    for zy in range(9):
        for dx in range(2):
            gcw[zy * 3 + dx] = first[zy * C : (zy + 1) * C, dx * C : (dx + 1) * C]
    for half in range(18):
        src = second[(half % 9) * 32 : (half % 9) * 32 + 32, (half // 9) * C : (half // 9 + 1) * C]
        gcw[(half // 2) * 3 + 2, (half % 2) * 32 : (half % 2) * 32 + 32, :] = src
    stores[2].start()
    loads[3].wait()
    tconv_scale = 1.0 / math.sqrt(n_dev * 4 * 2 * 64)
    gtw[...] = tconv[...].reshape(-1, 128)[:1728].astype(F32) * tconv_scale
    stores[3].start()
    for i in range(2):
        loads[i].wait()
        stores[i].start()
    for store in stores:
        store.wait()


def solution(mesh):
    nx = mesh.shape["group"]
    n_slab = mesh.shape["slab"]
    ny = 4
    nz = n_slab // (2 * ny)
    plane = ny * nx
    rows_of = [ceil16(-(-n // (2 * plane))) for n in (864, 1728)]

    def step(coarse, tw, cw, cot):
        dma = pltpu.SemaphoreType.DMA
        vmem = pltpu.VMEM
        scratch = [
            vmem((4, 2, 64, CIN), BF16),
            vmem((27 * C, CIN), BF16),
            vmem((27 * C, C), BF16),
            vmem((2048, 128), BF16),
            vmem((2048, 128), F32),
            vmem((8, C, 512), BF16),
        ]
        scratch += [vmem((COT_Z[dz][1], C, COT_Y[dy][1]), BF16) for dz, dy in DIRS]
        scratch += [vmem((COA_Z[dz][1], COA_Y[dy][1], 64, CIN), BF16) for dz, dy in DIRS]
        scratch += [vmem(shape, BF16) for shape in BACK.values()] * 2
        scratch += [
            vmem((6 * 384, 512), BF16),
            vmem((3, 192, 384), BF16),
            vmem((192, 576), BF16),
            vmem((192, 576), BF16),
            vmem((9, 192, CIN), BF16),
            vmem((10 * 192, 768), BF16),
            vmem((8, C, 512), F32),
            vmem((10 * 192, 768), BF16),
            vmem((2, 10 * C, 256), BF16),
            vmem((576, 192), F32),
            vmem((2, 384, 640), BF16),
            vmem((2, 2, 192, 512), BF16),
            vmem((4, 2, 64, CIN), F32),
        ]
        for r in rows_of:
            scratch += [
                vmem((2, plane * r, 128), BF16),
                vmem((plane * r, 128), BF16),
                vmem((plane * r, 128), BF16),
                vmem((plane - 1, r, 128), BF16),
                vmem((r, 128), BF16),
                vmem((nz, r, 128), BF16),
            ]
        for r in rows_of:
            scratch += [dma((2,)), dma((plane - 1,)), dma((plane - 1,)), dma((nz - 1,)), dma((nz - 1,))]
            scratch += [dma((plane - 1,)), dma((plane - 1,)), dma((plane,)), dma((plane,))]
        scratch += [dma((4,)), dma((8,)), dma((8,)), dma((8,)), dma((8,)), dma((3,)), dma((3,))]
        in_hbm = pl.BlockSpec(memory_space=pltpu.HBM)
        in_vmem = pl.BlockSpec(memory_space=pltpu.VMEM)
        parts = pl.pallas_call(
            functools.partial(kernel, (nz, ny, nx), rows_of),
            out_shape=(
                jax.ShapeDtypeStruct((2048, 128), BF16),
                jax.ShapeDtypeStruct((4, 2, 64, CIN), BF16),
                jax.ShapeDtypeStruct((2, plane * rows_of[0], 128), BF16),
                jax.ShapeDtypeStruct((2, plane * rows_of[1], 128), BF16),
            ),
            in_specs=[in_hbm] * 4,
            out_specs=(in_vmem,) * 4,
            scratch_shapes=scratch,
            compiler_params=pltpu.CompilerParams(
                collective_id=0, has_side_effects=True, vmem_limit_bytes=61 * 2**20
            ),
            cost_estimate=pl.CostEstimate(flops=7 * 10**9, bytes_accessed=4 * 10**6, transcendentals=500000),
        )(
            coarse.reshape(4, 2, 64, CIN),
            jnp.swapaxes(tw, 3, 4).reshape(27 * C, CIN),
            cw.reshape(27 * C, C),
            cot.reshape(2048, 128),
        )
        any_space = pl.BlockSpec(memory_space=pl.ANY)
        field, gc, gcw, gtw = pl.pallas_call(
            functools.partial(unpack, n_slab * nx),
            out_shape=(
                jax.ShapeDtypeStruct((2048, 128), BF16),
                jax.ShapeDtypeStruct((4, 2, 64, CIN), BF16),
                jax.ShapeDtypeStruct((27, C, C), F32),
                jax.ShapeDtypeStruct((27 * C, CIN), F32),
            ),
            in_specs=[any_space] * 4,
            out_specs=(any_space,) * 4,
            scratch_shapes=[
                *(vmem(part.shape, BF16) for part in parts),
                vmem((27, C, C), F32),
                vmem((27 * C, CIN), F32),
                dma((8,)),
            ],
            compiler_params=pltpu.CompilerParams(vmem_limit_bytes=61 * 2**20),
        )(*parts)
        return (
            field.reshape(1, 1, C, 8, 4, 128),
            gc.reshape(1, 1, 4, 2, 64, CIN),
            gcw.reshape(3, 3, 3, C, C),
            jnp.swapaxes(gtw.reshape(3, 3, 3, C, CIN), 3, 4),
        )

    blocks = P("group", "slab", None, None, None, None)
    return jax.shard_map(
        step,
        mesh=mesh,
        in_specs=(blocks, P(), P(), blocks),
        out_specs=(blocks, blocks, P(), P()),
        check_vma=False,
    )
```

```python
import functools
import math

import jax
import jax.numpy as jnp
from jax import lax
from jax.experimental import pallas as pl
from jax.experimental.pallas import tpu as pltpu
from jax.sharding import PartitionSpec as P

MESH = pl.DeviceIdType.MESH
F32 = jnp.float32
BF16 = jnp.bfloat16
PY = 4
CIN = 128
C = 64
NT = (((1,), (1,)), ((), ()))

DIRS = [(0, 1), (0, -1), (1, 0), (-1, 0), (1, 1), (1, -1), (-1, 1), (-1, -1)]
COT_Z = {1: (7, 1), 0: (0, 8), -1: (0, 1)}
COT_Y = {1: (384, 128), 0: (0, 512), -1: (0, 128)}
COA_Z = {1: (3, 1), 0: (0, 4), -1: (0, 1)}
COA_Y = {1: (1, 1), 0: (0, 2), -1: (0, 1)}
BACK = {(0, 1): (4, 64, CIN), (1, 0): (2, 64, CIN), (1, 1): (1, 64, CIN)}


def dot(a, b):
    return jnp.dot(a, b, preferred_element_type=F32)


def dot_nt(a, b):
    return lax.dot_general(a, b, NT, preferred_element_type=F32)


def unrolled(start, stop):
    def run(body):
        for i in range(start, stop):
            body(i)

    return run


def ceil16(n):
    return -(-n // 16) * 16


class Place:
    def __init__(self, nz, ny, nx):
        self.nz, self.ny, self.nx = nz, ny, nx
        self.plane = ny * nx
        self.slab = lax.axis_index("slab")
        self.x = lax.axis_index("group")
        self.core = lax.rem(self.slab, 2)
        chip = lax.div(self.slab, 2)
        self.y = lax.rem(chip, ny)
        self.z = lax.div(chip, ny)
        self.p = self.y * nx + self.x
        lane = lax.rem(self.slab, PY)
        zb = lax.div(self.slab, PY)
        self.has_y = {1: lane < PY - 1, -1: lane > 0}
        self.has_z = {1: zb < nz * ny * 2 // PY - 1, -1: zb > 0}

    def has(self, dz, dy):
        if dz == 0:
            return self.has_y[dy]
        if dy == 0:
            return self.has_z[dz]
        return jnp.logical_and(self.has_z[dz], self.has_y[dy])

    def halo(self, dz, dy):
        return (self.slab + PY * dz + dy, self.x)

    def pair(self):
        return (self.slab + 1 - 2 * self.core, self.x)

    def in_plane(self, k):
        p = lax.rem(self.p + k, self.plane)
        y, x = lax.div(p, self.nx), lax.rem(p, self.nx)
        return p, ((self.z * self.ny + y) * 2 + self.core, x)

    def along_z(self, k):
        z = lax.rem(self.z + k, self.nz)
        return ((z * self.ny + self.y) * 2 + self.core, self.x)


def remote(src, dst, send, recv, device):
    return pltpu.make_async_remote_copy(
        src_ref=src, dst_ref=dst, send_sem=send, recv_sem=recv, device_id=device, device_id_type=MESH
    )


class Reduction:
    def __init__(self, at, rows, bufs, sems):
        self.at, self.r = at, rows
        self.v, self.r0, self.s0, self.r1, self.s1, self.r2, self.g = bufs
        self.pair_sems, self.plane_send, self.plane_recv, self.z_send, self.z_recv, self.back_send, self.back_recv = sems[:7]
        self.share_send, self.share_recv = sems[7:]
        self.sent = []

    def go(self, copy):
        copy.start()
        self.sent.append(copy)
        return copy

    def start_pair(self):
        at = self.at
        self.c0 = self.go(remote(self.v.at[1 - at.core], self.r0, self.pair_sems.at[0], self.pair_sems.at[1], at.pair()))

    def start_plane(self):
        at, r = self.at, self.r
        self.c0.wait_recv()
        self.s0[...] = (self.v[at.core].astype(F32) + self.r0[...].astype(F32)).astype(BF16)
        self.c1 = []
        for k in range(1, at.plane):
            p, device = at.in_plane(k)
            rows = pl.ds(pl.multiple_of(p * r, 16), r)
            self.c1.append(
                self.go(remote(self.s0.at[rows], self.r1.at[k - 1], self.plane_send.at[k - 1], self.plane_recv.at[k - 1], device))
            )

    def start_z(self):
        at, r = self.at, self.r
        total = self.s0[pl.ds(pl.multiple_of(at.p * r, 16), r), :].astype(F32)
        for k, c in enumerate(self.c1):
            c.wait_recv()
            total = total + self.r1[k].astype(F32)
        self.s1[...] = total.astype(BF16)
        self.r2[at.z] = self.s1[...]
        self.c2 = []
        for k in range(1, at.nz):
            self.c2.append(
                self.go(remote(self.s1, self.r2.at[at.z], self.z_send.at[k - 1], self.z_recv.at[k - 1], at.along_z(k)))
            )

    def start_back(self):
        at, r = self.at, self.r
        for c in self.c2:
            c.wait_recv()
        total = self.r2[0].astype(F32)
        for k in range(1, at.nz):
            total = total + self.r2[k].astype(F32)
        rows = pl.ds(pl.multiple_of(at.p * r, 16), r)
        self.g[at.core, rows, :] = total.astype(BF16)
        self.c3 = []
        for k in range(1, at.plane):
            _, device = at.in_plane(k)
            self.c3.append(
                self.go(
                    remote(
                        self.g.at[at.core, rows], self.g.at[at.core, rows], self.back_send.at[k - 1], self.back_recv.at[k - 1], device
                    )
                )
            )

    def start_share(self):
        at, r = self.at, self.r
        self.c4 = []
        for k in range(at.plane):
            if k:
                self.c3[k - 1].wait_recv()
            p = lax.rem(at.p + at.plane - k, at.plane)
            piece = self.g.at[at.core, pl.ds(pl.multiple_of(p * r, 16), r)]
            self.c4.append(self.go(remote(piece, piece, self.share_send.at[k], self.share_recv.at[k], at.pair())))

    def finish(self):
        for c in self.c4:
            c.wait_recv()
        for c in self.sent:
            c.wait_send()


def kernel(
    dims,
    rows_of,
    coarse_hbm,
    tw_hbm,
    cw_hbm,
    cot_hbm,
    field_out,
    gc_out,
    conv_out,
    tconv_out,
    coarse,
    tw,
    cw,
    cot,
    wide,
    rows_cot,
    *rest,
):
    rest = list(rest)
    cot_halo = {d: rest.pop(0) for d in DIRS}
    coa_halo = {d: rest.pop(0) for d in DIRS}
    back_from = {d: rest.pop(0) for d in BACK}
    back_to = {d: rest.pop(0) for d in BACK}
    up, w1, w2, w4, w3, act, ds, bb, gh, taps, et, cols, local_gc = (rest.pop(0) for _ in range(13))
    bufs = [[rest.pop(0) for _ in range(6)] for _ in range(2)]
    bufs = [b + [out] for b, out in zip(bufs, (conv_out, tconv_out))]
    sems = [[rest.pop(0) for _ in range(9)] for _ in range(2)]
    load_sem, cot_send, cot_recv, coa_send, coa_recv, back_send, back_recv = rest
    nz, ny, nx = dims
    at = Place(nz, ny, nx)

    barrier = pltpu.get_barrier_semaphore()
    others = [at.pair()]
    others += [at.in_plane(k)[1] for k in range(1, at.plane)]
    others += [at.along_z(k) for k in range(1, nz)]
    for device in others:
        pl.semaphore_signal(barrier, inc=1, device_id=device, device_id_type=MESH)
    for d in DIRS:

        @pl.when(at.has(*d))
        def _():
            pl.semaphore_signal(barrier, inc=1, device_id=at.halo(*d), device_id_type=MESH)

    loads = [
        pltpu.make_async_copy(src, dst, load_sem.at[i])
        for i, (src, dst) in enumerate(((cot_hbm, cot), (coarse_hbm, coarse), (tw_hbm, tw), (cw_hbm, cw)))
    ]
    for load in loads:
        load.start()

    loads[0].wait()
    wide[...] = cot[...].astype(F32)
    for z in (0, 7, 1, 2, 3, 4, 5, 6):
        for y in range(4):
            rows_cot[z, :, y * 128 : y * 128 + 128] = wide[pl.ds(z * 4 + y, C, stride=32), :].astype(BF16)
    count = len(others)
    for d in DIRS:
        count = count + jnp.where(at.has(*d), 1, 0)
    pl.semaphore_wait(barrier, count)

    def coa_copy(i, d):
        (z, dz), (y, dy) = COA_Z[d[0]], COA_Y[d[1]]
        return remote(
            coarse_hbm.at[pl.ds(z, dz), pl.ds(y, dy)], coa_halo[d], coa_send.at[i], coa_recv.at[i], at.halo(*d)
        )

    def cot_copy(i, d):
        (z, dz), (y, dy) = COT_Z[d[0]], COT_Y[d[1]]
        return remote(
            rows_cot.at[pl.ds(z, dz), :, pl.ds(y, dy)], cot_halo[d], cot_send.at[i], cot_recv.at[i], at.halo(*d)
        )

    def back_copy(i, d):
        return remote(back_to[d], back_from[d], back_send.at[i], back_recv.at[i], at.halo(*d))

    def start(copy_of, dirs=DIRS):
        for i, d in enumerate(dirs):

            @pl.when(at.has(*d))
            def _():
                copy_of(i, d).start()

    def arrived(copy_of, dirs=DIRS):
        for i, d in enumerate(dirs):

            @pl.when(at.has(-d[0], -d[1]))
            def _():
                copy_of(i, d).wait_recv()

    start(coa_copy)

    start(cot_copy)

    for d in DIRS:

        @pl.when(jnp.logical_not(at.has(-d[0], -d[1])))
        def _():
            cot_halo[d][...] = jnp.zeros_like(cot_halo[d])
            coa_halo[d][...] = jnp.zeros_like(coa_halo[d])
            if d in BACK:
                back_from[d][...] = jnp.zeros_like(back_from[d])

    loads[1].wait()

    loads[2].wait()
    loads[3].wait()
    for kz in range(3):
        for ky in range(3):
            for kx in range(3):
                block = tw[((kz * 3 + ky) * 3 + kx) * C : ((kz * 3 + ky) * 3 + kx + 1) * C, :]
                w1[kz, ky * C : (ky + 1) * C, kx * 128 : kx * 128 + 128] = block
                w3[ky * 3 + kx, kz * C : (kz + 1) * C, :] = block
    lane_at = lax.broadcasted_iota(jnp.int32, (C, 128), 1)
    not_first = jnp.where(lane_at == 0, 0.0, 1.0).astype(F32)
    not_last = jnp.where(lane_at == 127, 0.0, 1.0).astype(F32)

    def taps_of(row):
        return pltpu.roll(row, 1, 1) * not_first, row, pltpu.roll(row, 127, 1) * not_last

    def put_cot(ze, ye, row):
        before, row, after = taps_of(row.astype(F32))
        for i, value in enumerate((after, row, before)):
            bb[pl.ds(ze * 192 + i * C, C), ye * 128 : ye * 128 + 128] = value.astype(BF16)

    @unrolled(0, 8)
    def _(z):
        for y in range(4):
            put_cot(z + 1, y + 1, rows_cot[z, :, y * 128 : y * 128 + 128])

    cell = lax.broadcasted_iota(jnp.int32, (C, 384), 0)
    place = lax.broadcasted_iota(jnp.int32, (C, 384), 1)
    spread = jnp.zeros((C, 384), F32)
    for k in range(3):
        spread = spread + jnp.where(place == 2 * cell + (k - 1) + 128 * k, 1.0, 0.0) * jnp.where(
            jnp.logical_and(place >= 128 * k, place < 128 * k + 128), 1.0, 0.0
        )
    spread = spread.astype(BF16)

    def put_coarse(ze, ye, block):
        wide_block = dot(block.astype(F32).T.astype(BF16), spread).astype(BF16)
        for k in range(3):
            up[pl.ds(ze * 384 + k * 128, 128), ye * 128 : ye * 128 + 128] = wide_block[:, k * 128 : k * 128 + 128]

    @unrolled(0, 4)
    def _(z):
        for y in range(2):
            put_coarse(z + 1, y + 1, coarse[z, y])

    arrived(coa_copy)

    @unrolled(0, 4)
    def _(z):
        put_coarse(z + 1, 0, coa_halo[(0, 1)][z, 0])
        put_coarse(z + 1, 3, coa_halo[(0, -1)][z, 0])

    for dz, ze in ((1, 0), (-1, 5)):
        put_coarse(ze, 0, coa_halo[(dz, 1)][0, 0])
        for y in range(2):
            put_coarse(ze, y + 1, coa_halo[(dz, 0)][0, y])
        put_coarse(ze, 3, coa_halo[(dz, -1)][0, 0])

    has_zl = jnp.where(at.has_z[-1], 1.0, 0.0).astype(F32)
    has_zh = jnp.where(at.has_z[1], 1.0, 0.0).astype(F32)
    has_yl = jnp.where(at.has_y[-1], 1.0, 0.0).astype(F32)
    has_yh = jnp.where(at.has_y[1], 1.0, 0.0).astype(F32)

    def put_hidden(zf, partial, z_mask):
        for yf in range(6):
            n = yf // 2
            if yf % 2:
                h = partial[C : 2 * C, (n + 1) * 128 : (n + 2) * 128]
            else:
                h = partial[2 * C :, n * 128 : n * 128 + 128] + partial[:C, (n + 1) * 128 : (n + 2) * 128]
            mask = z_mask
            if yf in (0, 5):
                y_mask = has_yl if yf == 0 else has_yh
                mask = y_mask if mask is None else mask * y_mask
            s = 0.5 * jnp.tanh(0.5 * h) + 0.5
            row = h * s
            if mask is not None:
                row = row * mask
            for i, value in enumerate(taps_of(row)):
                act[pl.ds(zf * 192 + i * C, C), yf * 128 : yf * 128 + 128] = value.astype(BF16)
            if 0 < zf < 9 and 0 < yf < 5:
                ds[zf - 1, :, (yf - 1) * 128 : yf * 128] = s * (1.0 + h * (1.0 - s))

    w1_odd = jnp.concatenate([w1[2], w1[0]], axis=1)

    @unrolled(0, 5)
    def _(m):
        start = m * 384
        odd = dot(w1_odd, up[pl.ds(start, 768), :])
        put_hidden(2 * m, odd, has_zl if m == 0 else None)
        even = dot(w1[1], up[pl.ds(start + 384, 384), :])
        put_hidden(2 * m + 1, even, has_zh if m == 4 else None)

    gc_v, gt_v = bufs[0][0], bufs[1][0]
    conv_sum = Reduction(at, rows_of[0], bufs[0], sems[0])
    tconv_sum = Reduction(at, rows_of[1], bufs[1], sems[1])
    taps[...] = jnp.zeros_like(taps)

    @unrolled(0, 8)
    def _(z):
        blocks = [
            act[pl.ds((z + dz) * 192 + C, C), dy * 128 : dy * 128 + 512]
            for dz in range(3)
            for dy in range(3)
        ]
        right = bb[pl.ds((z + 1) * 192, 192), 128:640]
        taps[...] += dot_nt(jnp.concatenate(blocks, axis=0), right)

    def fill(v, half_rows, parts):
        at_row = 0
        for part in parts:
            done, n = 0, part.shape[0]
            while done < n:
                half, row = divmod(at_row, half_rows)
                m = min(n - done, half_rows - row)
                v[half, row : row + m, :] = part[done : done + m, :].astype(BF16)
                done, at_row = done + m, at_row + m
        while at_row < 2 * half_rows:
            half, row = divmod(at_row, half_rows)
            v[half, row:, :] = jnp.zeros((half_rows - row, 128), BF16)
            at_row += half_rows - row

    fill(
        gc_v,
        at.plane * rows_of[0],
        [taps[:, :128], jnp.concatenate([taps[:288, 128:], taps[288:, 128:]], axis=1)],
    )
    conv_sum.start_pair()

    for a in range(3):
        tall = jnp.concatenate([cw[(b * 3 + a) * 192 : (b * 3 + a + 1) * 192, :].astype(F32) for b in range(3)], axis=0)
        w4[a * C : (a + 1) * C, :] = tall.T.astype(BF16)
        w2[a * C : (a + 1) * C, :] = jnp.concatenate(
            [
                cw[((b * 3 + a) * 3 + x) * C : ((b * 3 + a) * 3 + x + 1) * C, :].astype(F32)
                for b in (2, 1, 0)
                for x in range(3)
            ],
            axis=1,
        ).astype(BF16)
    conv_sum.start_plane()

    arrived(cot_copy)

    @unrolled(0, 8)
    def _(z):
        put_cot(z + 1, 0, cot_halo[(0, 1)][z])
        put_cot(z + 1, 5, cot_halo[(0, -1)][z])

    for dz, ze in ((1, 0), (-1, 9)):
        put_cot(ze, 0, cot_halo[(dz, 1)][0])
        for y in range(4):
            put_cot(ze, y + 1, cot_halo[(dz, 0)][0, :, y * 128 : y * 128 + 128])
        put_cot(ze, 5, cot_halo[(dz, -1)][0])

    for half in range(2):
        for q in (0, 9):
            gh[half, q * C : q * C + C, :] = jnp.zeros((C, 256), BF16)

    @unrolled(0, 8)
    def _(z):
        partial = dot(w2[...], bb[pl.ds(z * 192, 576), :])
        for y in range(4):
            ga = partial[:C, (y + 2) * 128 : (y + 3) * 128]
            ga = ga + partial[C : 2 * C, (y + 1) * 128 : (y + 2) * 128]
            ga = ga + partial[2 * C :, y * 128 : y * 128 + 128]
            gh[y % 2, (z + 1) * C : (z + 2) * C, y // 2 * 128 : y // 2 * 128 + 128] = (
                ga * ds[z, :, y * 128 : y * 128 + 128]
            ).astype(BF16)

    def picks(shape, f_dim):
        f = lax.broadcasted_iota(jnp.int32, shape, f_dim)
        c = lax.broadcasted_iota(jnp.int32, shape, 1 - f_dim)
        out = jnp.zeros(shape, F32)
        for k in range(3):
            for y in range(2):
                cell0 = k * 128 + y * C
                inside = jnp.logical_and(c >= cell0, c < cell0 + C)
                hit = jnp.logical_and(f == 2 * (c - cell0) + (k - 1) + 128 * y, inside)
                own = jnp.logical_and(f >= 128 * y, f < 128 * y + 128)
                out = out + jnp.where(jnp.logical_and(hit, own), 1.0, 0.0)
        return out.astype(BF16)

    pick = picks((256, 384), 0)
    for half in range(2):
        some = dot(gh[half, C : 9 * C, :], pick).astype(BF16)
        for z in range(8):
            for kx in range(3):
                cols[z % 2, half, kx * C : (kx + 1) * C, z // 2 * 128 : z // 2 * 128 + 128] = some[
                    z * C : (z + 1) * C, kx * 128 : kx * 128 + 128
                ]

    def cells(z, y):
        if z < 4 and y < 2:
            return coarse[z, y]
        if z < 4:
            return coa_halo[(0, -1)][z, 0]
        return coa_halo[(-1, 0)][0, y] if y < 2 else coa_halo[(-1, -1)][0, 0]

    by_tap = {}
    for odd_z in range(2):
        for odd_y in range(2):
            shifts = [(z, y) for z in range(odd_z + 1) for y in range(odd_y + 1)]
            right = jnp.concatenate(
                [
                    jnp.concatenate([cells(z + sz, y + sy) for z in range(4) for y in range(2)], axis=0)
                    for sz, sy in shifts
                ],
                axis=1,
            )
            result = dot(cols[odd_z, odd_y], right)
            for n, (sz, sy) in enumerate(shifts):
                kz = 1 if not odd_z else 2 - 2 * sz
                ky = 1 if not odd_y else 2 - 2 * sy
                by_tap[kz, ky] = result[:, n * 128 : n * 128 + 128]
    fill(gt_v, at.plane * rows_of[1], [by_tap[kz, ky] for kz in range(3) for ky in range(3)])
    tconv_sum.start_pair()

    pick_t = picks((384, 256), 1)
    for half in range(2):
        et[half] = dot_nt(pick_t, gh[half]).astype(BF16)

    def gather(ky, zc):
        total = None
        for kx in range(3):
            rows = slice(kx * 128, kx * 128 + 128)
            if zc < 4:
                term = dot(et[int(ky != 1), rows, zc * 128 : zc * 128 + 192], w3[ky * 3 + kx])
            else:
                term = dot(et[int(ky != 1), rows, 512:576], w3[ky * 3 + kx, :C, :])
            total = term if total is None else total + term
        return total

    for zc in (4, 3, 2, 1, 0):
        low = gather(1, zc) + gather(2, zc)
        high = gather(0, zc)
        rows = (low[:C], low[C:] + high[:C])
        if zc < 4:
            for y in range(2):
                local_gc[zc, y] = rows[y]
            back_to[(0, 1)][zc] = high[C:].astype(BF16)
        else:
            for y in range(2):
                back_to[(1, 0)][y] = rows[y].astype(BF16)
            back_to[(1, 1)][0] = high[C:].astype(BF16)
    tconv_sum.start_plane()
    conv_sum.start_z()
    start(back_copy, BACK)

    @unrolled(0, 8)
    def _(z):
        partial = dot(w4[...], act[pl.ds(z * 192, 576), :])
        for y in range(4):
            row = partial[:C, y * 128 : y * 128 + 128]
            row = row + partial[C : 2 * C, (y + 1) * 128 : (y + 2) * 128]
            row = row + partial[2 * C :, (y + 2) * 128 : (y + 3) * 128]
            wide[pl.ds(z * 4 + y, C, stride=32), :] = row

    field_out[...] = wide[...].astype(BF16)
    tconv_sum.start_z()
    conv_sum.start_back()

    arrived(back_copy, BACK)
    for zc in range(4):
        for y in range(2):
            total = local_gc[zc, y]
            if y == 0:
                total = total + back_from[(0, 1)][zc].astype(F32)
            if zc == 0:
                total = total + back_from[(1, 0)][y].astype(F32)
            if zc == 0 and y == 0:
                total = total + back_from[(1, 1)][0].astype(F32)
            gc_out[zc, y] = total.astype(BF16)
    tconv_sum.start_back()
    conv_sum.start_share()

    def sent(copy_of, dirs=DIRS):
        for i, d in enumerate(dirs):

            @pl.when(at.has(*d))
            def _():
                copy_of(i, d).wait_send()

    sent(coa_copy)
    sent(cot_copy)
    sent(back_copy, BACK)
    conv_sum.finish()
    tconv_sum.start_share()
    tconv_sum.finish()


def unpack(n_dev, *refs):
    ins, outs, held, (gcw, gtw), (sems,) = refs[:4], refs[4:8], refs[8:12], refs[12:14], refs[14:]
    loads = [pltpu.make_async_copy(src, dst, sems.at[i]) for i, (src, dst) in enumerate(zip(ins, held))]
    stores = [
        pltpu.make_async_copy(src, dst, sems.at[4 + i])
        for i, (src, dst) in enumerate(zip((held[0], held[1], gcw, gtw), outs))
    ]
    for i in (2, 3, 0, 1):
        loads[i].start()
    conv, tconv = held[2:]
    loads[2].wait()
    conv_scale = 1.0 / math.sqrt(n_dev * 8 * 4 * 128)
    g = conv[...].reshape(-1, 128)
    first = g[:576].astype(F32) * conv_scale
    second = g[576:864].astype(F32) * conv_scale
    for zy in range(9):
        for dx in range(2):
            gcw[zy * 3 + dx] = first[zy * C : (zy + 1) * C, dx * C : (dx + 1) * C]
    for half in range(18):
        src = second[(half % 9) * 32 : (half % 9) * 32 + 32, (half // 9) * C : (half // 9 + 1) * C]
        gcw[(half // 2) * 3 + 2, (half % 2) * 32 : (half % 2) * 32 + 32, :] = src
    stores[2].start()
    loads[3].wait()
    tconv_scale = 1.0 / math.sqrt(n_dev * 4 * 2 * 64)
    gtw[...] = tconv[...].reshape(-1, 128)[:1728].astype(F32) * tconv_scale
    stores[3].start()
    for i in range(2):
        loads[i].wait()
        stores[i].start()
    for store in stores:
        store.wait()


def solution(mesh):
    nx = mesh.shape["group"]
    n_slab = mesh.shape["slab"]
    ny = 4
    nz = n_slab // (2 * ny)
    plane = ny * nx
    rows_of = [ceil16(-(-n // (2 * plane))) for n in (864, 1728)]

    def step(coarse, tw, cw, cot):
        dma = pltpu.SemaphoreType.DMA
        vmem = pltpu.VMEM
        scratch = [
            vmem((4, 2, 64, CIN), BF16),
            vmem((27 * C, CIN), BF16),
            vmem((27 * C, C), BF16),
            vmem((2048, 128), BF16),
            vmem((2048, 128), F32),
            vmem((8, C, 512), BF16),
        ]
        scratch += [vmem((COT_Z[dz][1], C, COT_Y[dy][1]), BF16) for dz, dy in DIRS]
        scratch += [vmem((COA_Z[dz][1], COA_Y[dy][1], 64, CIN), BF16) for dz, dy in DIRS]
        scratch += [vmem(shape, BF16) for shape in BACK.values()] * 2
        scratch += [
            vmem((6 * 384, 512), BF16),
            vmem((3, 192, 384), BF16),
            vmem((192, 576), BF16),
            vmem((192, 576), BF16),
            vmem((9, 192, CIN), BF16),
            vmem((10 * 192, 768), BF16),
            vmem((8, C, 512), F32),
            vmem((10 * 192, 768), BF16),
            vmem((2, 10 * C, 256), BF16),
            vmem((576, 192), F32),
            vmem((2, 384, 640), BF16),
            vmem((2, 2, 192, 512), BF16),
            vmem((4, 2, 64, CIN), F32),
        ]
        for r in rows_of:
            scratch += [
                vmem((2, plane * r, 128), BF16),
                vmem((plane * r, 128), BF16),
                vmem((plane * r, 128), BF16),
                vmem((plane - 1, r, 128), BF16),
                vmem((r, 128), BF16),
                vmem((nz, r, 128), BF16),
            ]
        for r in rows_of:
            scratch += [dma((2,)), dma((plane - 1,)), dma((plane - 1,)), dma((nz - 1,)), dma((nz - 1,))]
            scratch += [dma((plane - 1,)), dma((plane - 1,)), dma((plane,)), dma((plane,))]
        scratch += [dma((4,)), dma((8,)), dma((8,)), dma((8,)), dma((8,)), dma((3,)), dma((3,))]
        in_hbm = pl.BlockSpec(memory_space=pltpu.HBM)
        in_vmem = pl.BlockSpec(memory_space=pltpu.VMEM)
        parts = pl.pallas_call(
            functools.partial(kernel, (nz, ny, nx), rows_of),
            out_shape=(
                jax.ShapeDtypeStruct((2048, 128), BF16),
                jax.ShapeDtypeStruct((4, 2, 64, CIN), BF16),
                jax.ShapeDtypeStruct((2, plane * rows_of[0], 128), BF16),
                jax.ShapeDtypeStruct((2, plane * rows_of[1], 128), BF16),
            ),
            in_specs=[in_hbm] * 4,
            out_specs=(in_vmem,) * 4,
            scratch_shapes=scratch,
            compiler_params=pltpu.CompilerParams(
                collective_id=0, has_side_effects=True, vmem_limit_bytes=61 * 2**20
            ),
            cost_estimate=pl.CostEstimate(flops=7 * 10**9, bytes_accessed=4 * 10**6, transcendentals=500000),
        )(
            coarse.reshape(4, 2, 64, CIN),
            jnp.swapaxes(tw, 3, 4).reshape(27 * C, CIN),
            cw.reshape(27 * C, C),
            cot.reshape(2048, 128),
        )
        any_space = pl.BlockSpec(memory_space=pl.ANY)
        field, gc, gcw, gtw = pl.pallas_call(
            functools.partial(unpack, n_slab * nx),
            out_shape=(
                jax.ShapeDtypeStruct((2048, 128), BF16),
                jax.ShapeDtypeStruct((4, 2, 64, CIN), BF16),
                jax.ShapeDtypeStruct((27, C, C), F32),
                jax.ShapeDtypeStruct((27 * C, CIN), F32),
            ),
            in_specs=[any_space] * 4,
            out_specs=(any_space,) * 4,
            scratch_shapes=[
                *(vmem(part.shape, BF16) for part in parts),
                vmem((27, C, C), F32),
                vmem((27 * C, CIN), F32),
                dma((8,)),
            ],
            compiler_params=pltpu.CompilerParams(vmem_limit_bytes=61 * 2**20),
        )(*parts)
        return (
            field.reshape(1, 1, C, 8, 4, 128),
            gc.reshape(1, 1, 4, 2, 64, CIN),
            gcw.reshape(3, 3, 3, C, C),
            jnp.swapaxes(gtw.reshape(3, 3, 3, C, CIN), 3, 4),
        )

    blocks = P("group", "slab", None, None, None, None)
    return jax.shard_map(
        step,
        mesh=mesh,
        in_specs=(blocks, P(), P(), blocks),
        out_specs=(blocks, blocks, P(), P()),
        check_vma=False,
    )
```

```python
import functools
import math

import jax
import jax.numpy as jnp
from jax import lax
from jax.experimental import pallas as pl
from jax.experimental.pallas import tpu as pltpu
from jax.sharding import PartitionSpec as P

MESH = pl.DeviceIdType.MESH
F32 = jnp.float32
BF16 = jnp.bfloat16
PY = 4
CIN = 128
C = 64
NT = (((1,), (1,)), ((), ()))

DIRS = [(0, 1), (0, -1), (1, 0), (-1, 0), (1, 1), (1, -1), (-1, 1), (-1, -1)]
NEAR, FAR = DIRS[:2], DIRS[2:]
COT_Z = {1: (7, 1), 0: (0, 8), -1: (0, 1)}
COT_Y = {1: (384, 128), 0: (0, 512), -1: (0, 128)}
COA_Z = {1: (3, 1), 0: (0, 4), -1: (0, 1)}
COA_Y = {1: (1, 1), 0: (0, 2), -1: (0, 1)}
BACK = {(0, 1): (4, 64, CIN), (1, 0): (2, 64, CIN), (1, 1): (1, 64, CIN)}


def dot(a, b):
    return jnp.dot(a, b, preferred_element_type=F32)


def dot_nt(a, b):
    return lax.dot_general(a, b, NT, preferred_element_type=F32)


def unrolled(start, stop):
    def run(body):
        for i in range(start, stop):
            body(i)

    return run


def ceil16(n):
    return -(-n // 16) * 16


class Place:
    def __init__(self, nz, ny, nx):
        self.nz, self.ny, self.nx = nz, ny, nx
        self.plane = ny * nx
        self.slab = lax.axis_index("slab")
        self.x = lax.axis_index("group")
        self.core = lax.rem(self.slab, 2)
        chip = lax.div(self.slab, 2)
        self.y = lax.rem(chip, ny)
        self.z = lax.div(chip, ny)
        self.p = self.y * nx + self.x
        lane = lax.rem(self.slab, PY)
        zb = lax.div(self.slab, PY)
        self.has_y = {1: lane < PY - 1, -1: lane > 0}
        self.has_z = {1: zb < nz * ny * 2 // PY - 1, -1: zb > 0}

    def has(self, dz, dy):
        if dz == 0:
            return self.has_y[dy]
        if dy == 0:
            return self.has_z[dz]
        return jnp.logical_and(self.has_z[dz], self.has_y[dy])

    def halo(self, dz, dy):
        return (self.slab + PY * dz + dy, self.x)

    def pair(self):
        return (self.slab + 1 - 2 * self.core, self.x)

    def in_plane(self, k):
        p = lax.rem(self.p + k, self.plane)
        y, x = lax.div(p, self.nx), lax.rem(p, self.nx)
        return p, ((self.z * self.ny + y) * 2 + self.core, x)

    def along_z(self, k):
        z = lax.rem(self.z + k, self.nz)
        return ((z * self.ny + self.y) * 2 + self.core, self.x)


def remote(src, dst, send, recv, device):
    return pltpu.make_async_remote_copy(
        src_ref=src, dst_ref=dst, send_sem=send, recv_sem=recv, device_id=device, device_id_type=MESH
    )


class Reduction:
    def __init__(self, at, rows, bufs, sems):
        self.at, self.r = at, rows
        self.v, self.r0, self.s0, self.r1, self.s1, self.r2, self.g = bufs
        self.pair_sems, self.plane_send, self.plane_recv, self.z_send, self.z_recv, self.back_send, self.back_recv = sems[:7]
        self.share_send, self.share_recv = sems[7:]
        self.sent = []

    def go(self, copy):
        copy.start()
        self.sent.append(copy)
        return copy

    def start_pair(self):
        at = self.at
        self.c0 = self.go(remote(self.v.at[1 - at.core], self.r0, self.pair_sems.at[0], self.pair_sems.at[1], at.pair()))

    def start_plane(self):
        at, r = self.at, self.r
        self.c0.wait_recv()
        self.s0[...] = (self.v[at.core].astype(F32) + self.r0[...].astype(F32)).astype(BF16)
        self.c1 = []
        for k in range(1, at.plane):
            p, device = at.in_plane(k)
            rows = pl.ds(pl.multiple_of(p * r, 16), r)
            self.c1.append(
                self.go(remote(self.s0.at[rows], self.r1.at[k - 1], self.plane_send.at[k - 1], self.plane_recv.at[k - 1], device))
            )

    def start_z(self):
        at, r = self.at, self.r
        total = self.s0[pl.ds(pl.multiple_of(at.p * r, 16), r), :].astype(F32)
        for k, c in enumerate(self.c1):
            c.wait_recv()
            total = total + self.r1[k].astype(F32)
        self.s1[...] = total.astype(BF16)
        self.r2[at.z] = self.s1[...]
        self.c2 = []
        for k in range(1, at.nz):
            self.c2.append(
                self.go(remote(self.s1, self.r2.at[at.z], self.z_send.at[k - 1], self.z_recv.at[k - 1], at.along_z(k)))
            )

    def start_back(self):
        at, r = self.at, self.r
        for c in self.c2:
            c.wait_recv()
        total = self.r2[0].astype(F32)
        for k in range(1, at.nz):
            total = total + self.r2[k].astype(F32)
        rows = pl.ds(pl.multiple_of(at.p * r, 16), r)
        self.g[at.core, rows, :] = total.astype(BF16)
        self.c3 = []
        for k in range(1, at.plane):
            _, device = at.in_plane(k)
            self.c3.append(
                self.go(
                    remote(
                        self.g.at[at.core, rows], self.g.at[at.core, rows], self.back_send.at[k - 1], self.back_recv.at[k - 1], device
                    )
                )
            )

    def start_share(self):
        at, r = self.at, self.r
        self.c4 = []
        for k in range(at.plane):
            if k:
                self.c3[k - 1].wait_recv()
            p = lax.rem(at.p + at.plane - k, at.plane)
            piece = self.g.at[at.core, pl.ds(pl.multiple_of(p * r, 16), r)]
            self.c4.append(self.go(remote(piece, piece, self.share_send.at[k], self.share_recv.at[k], at.pair())))

    def arrive(self):
        for c in self.c4:
            c.wait_recv()

    def finish(self):
        for c in self.sent:
            c.wait_send()


def kernel(
    dims,
    rows_of,
    coarse_hbm,
    tw_hbm,
    cw_hbm,
    cot_hbm,
    field_out,
    gc_out,
    conv_out,
    tconv_out,
    coarse,
    tw,
    cw,
    cot,
    wide,
    rows_cot,
    *rest,
):
    rest = list(rest)
    cot_halo = {d: rest.pop(0) for d in DIRS}
    coa_halo = {d: rest.pop(0) for d in DIRS}
    back_from = {d: rest.pop(0) for d in BACK}
    back_to = {d: rest.pop(0) for d in BACK}
    up, w1, w2, w4, w3, act, ds, bb, gh, taps, et, cols, local_gc = (rest.pop(0) for _ in range(13))
    bufs = [[rest.pop(0) for _ in range(7)] for _ in range(2)]
    field, gc = rest.pop(0), rest.pop(0)
    sems = [[rest.pop(0) for _ in range(9)] for _ in range(2)]
    load_sem, cot_send, cot_recv, coa_send, coa_recv, back_send, back_recv, out_sem = rest
    nz, ny, nx = dims
    at = Place(nz, ny, nx)

    barrier = pltpu.get_barrier_semaphore()
    others = [at.pair()]
    others += [at.in_plane(k)[1] for k in range(1, at.plane)]
    others += [at.along_z(k) for k in range(1, nz)]
    for device in others:
        pl.semaphore_signal(barrier, inc=1, device_id=device, device_id_type=MESH)
    for d in DIRS:

        @pl.when(at.has(*d))
        def _():
            pl.semaphore_signal(barrier, inc=1, device_id=at.halo(*d), device_id_type=MESH)

    loads = [
        pltpu.make_async_copy(src, dst, load_sem.at[i])
        for i, (src, dst) in enumerate(((cot_hbm, cot), (coarse_hbm, coarse), (tw_hbm, tw), (cw_hbm, cw)))
    ]
    for load in loads:
        load.start()

    loads[0].wait()
    wide[...] = cot[...].astype(F32)
    for z in (0, 7, 1, 2, 3, 4, 5, 6):
        for y in range(4):
            rows_cot[z, :, y * 128 : y * 128 + 128] = wide[pl.ds(z * 4 + y, C, stride=32), :].astype(BF16)
    count = len(others)
    for d in DIRS:
        count = count + jnp.where(at.has(*d), 1, 0)
    pl.semaphore_wait(barrier, count)

    def coa_copy(i, d):
        (z, dz), (y, dy) = COA_Z[d[0]], COA_Y[d[1]]
        return remote(
            coarse_hbm.at[pl.ds(z, dz), pl.ds(y, dy)], coa_halo[d], coa_send.at[i], coa_recv.at[i], at.halo(*d)
        )

    def cot_copy(i, d):
        (z, dz), (y, dy) = COT_Z[d[0]], COT_Y[d[1]]
        return remote(
            rows_cot.at[pl.ds(z, dz), :, pl.ds(y, dy)], cot_halo[d], cot_send.at[i], cot_recv.at[i], at.halo(*d)
        )

    def back_copy(i, d):
        return remote(back_to[d], back_from[d], back_send.at[i], back_recv.at[i], at.halo(*d))

    def start(copy_of, dirs=DIRS):
        for i, d in enumerate(dirs):

            @pl.when(at.has(*d))
            def _():
                copy_of(i, d).start()

    def arrived(copy_of, dirs=DIRS):
        for i, d in enumerate(dirs):

            @pl.when(at.has(-d[0], -d[1]))
            def _():
                copy_of(i + (2 if dirs is FAR else 0), d).wait_recv()

    start(coa_copy)

    start(cot_copy)

    for d in DIRS:

        @pl.when(jnp.logical_not(at.has(-d[0], -d[1])))
        def _():
            cot_halo[d][...] = jnp.zeros_like(cot_halo[d])
            coa_halo[d][...] = jnp.zeros_like(coa_halo[d])
            if d in BACK:
                back_from[d][...] = jnp.zeros_like(back_from[d])

    loads[1].wait()

    loads[2].wait()
    loads[3].wait()
    for kz in range(3):
        for ky in range(3):
            for kx in range(3):
                block = tw[((kz * 3 + ky) * 3 + kx) * C : ((kz * 3 + ky) * 3 + kx + 1) * C, :]
                w1[kz, ky * C : (ky + 1) * C, kx * 128 : kx * 128 + 128] = block
                w3[ky * 3 + kx, kz * C : (kz + 1) * C, :] = block
    lane_at = lax.broadcasted_iota(jnp.int32, (C, 128), 1)
    not_first = jnp.where(lane_at == 0, 0.0, 1.0).astype(F32)
    not_last = jnp.where(lane_at == 127, 0.0, 1.0).astype(F32)

    def taps_of(row):
        return pltpu.roll(row, 1, 1) * not_first, row, pltpu.roll(row, 127, 1) * not_last

    def put_cot(ze, ye, row):
        before, row, after = taps_of(row.astype(F32))
        for i, value in enumerate((after, row, before)):
            bb[pl.ds(ze * 192 + i * C, C), ye * 128 : ye * 128 + 128] = value.astype(BF16)

    @unrolled(0, 8)
    def _(z):
        for y in range(4):
            put_cot(z + 1, y + 1, rows_cot[z, :, y * 128 : y * 128 + 128])

    cell = lax.broadcasted_iota(jnp.int32, (C, 384), 0)
    place = lax.broadcasted_iota(jnp.int32, (C, 384), 1)
    spread = jnp.zeros((C, 384), F32)
    for k in range(3):
        spread = spread + jnp.where(place == 2 * cell + (k - 1) + 128 * k, 1.0, 0.0) * jnp.where(
            jnp.logical_and(place >= 128 * k, place < 128 * k + 128), 1.0, 0.0
        )
    spread = spread.astype(BF16)

    def put_coarse(ze, ye, block):
        wide_block = dot(block.astype(F32).T.astype(BF16), spread).astype(BF16)
        for k in range(3):
            up[pl.ds(ze * 384 + k * 128, 128), ye * 128 : ye * 128 + 128] = wide_block[:, k * 128 : k * 128 + 128]

    @unrolled(0, 4)
    def _(z):
        for y in range(2):
            put_coarse(z + 1, y + 1, coarse[z, y])

    arrived(coa_copy, NEAR)

    @unrolled(0, 4)
    def _(z):
        put_coarse(z + 1, 0, coa_halo[(0, 1)][z, 0])
        put_coarse(z + 1, 3, coa_halo[(0, -1)][z, 0])

    has_zl = jnp.where(at.has_z[-1], 1.0, 0.0).astype(F32)
    has_zh = jnp.where(at.has_z[1], 1.0, 0.0).astype(F32)
    has_yl = jnp.where(at.has_y[-1], 1.0, 0.0).astype(F32)
    has_yh = jnp.where(at.has_y[1], 1.0, 0.0).astype(F32)

    def put_hidden(zf, partial, z_mask):
        for yf in range(6):
            n = yf // 2
            if yf % 2:
                h = partial[C : 2 * C, (n + 1) * 128 : (n + 2) * 128]
            else:
                h = partial[2 * C :, n * 128 : n * 128 + 128] + partial[:C, (n + 1) * 128 : (n + 2) * 128]
            mask = z_mask
            if yf in (0, 5):
                y_mask = has_yl if yf == 0 else has_yh
                mask = y_mask if mask is None else mask * y_mask
            s = 0.5 * jnp.tanh(0.5 * h) + 0.5
            row = h * s
            if mask is not None:
                row = row * mask
            for i, value in enumerate(taps_of(row)):
                act[pl.ds(zf * 192 + i * C, C), yf * 128 : yf * 128 + 128] = value.astype(BF16)
            if 0 < zf < 9 and 0 < yf < 5:
                ds[zf - 1, :, (yf - 1) * 128 : yf * 128] = s * (1.0 + h * (1.0 - s))

    w1_odd = jnp.concatenate([w1[2], w1[0]], axis=1)

    def odd_plane(m, z_mask=None):
        put_hidden(2 * m, dot(w1_odd, up[m * 384 : m * 384 + 768, :]), z_mask)

    def even_plane(m, z_mask=None):
        put_hidden(2 * m + 1, dot(w1[1], up[(m + 1) * 384 : (m + 2) * 384, :]), z_mask)

    for m in range(4):
        if m:
            odd_plane(m)
        even_plane(m)

    arrived(coa_copy, FAR)
    for dz, ze in ((1, 0), (-1, 5)):
        put_coarse(ze, 0, coa_halo[(dz, 1)][0, 0])
        for y in range(2):
            put_coarse(ze, y + 1, coa_halo[(dz, 0)][0, y])
        put_coarse(ze, 3, coa_halo[(dz, -1)][0, 0])

    odd_plane(0, has_zl)
    odd_plane(4)
    even_plane(4, has_zh)

    gc_v, gt_v = bufs[0][0], bufs[1][0]
    conv_sum = Reduction(at, rows_of[0], bufs[0], sems[0])
    tconv_sum = Reduction(at, rows_of[1], bufs[1], sems[1])
    taps[...] = jnp.zeros_like(taps)

    @unrolled(0, 8)
    def _(z):
        blocks = [
            act[pl.ds((z + dz) * 192 + C, C), dy * 128 : dy * 128 + 512]
            for dz in range(3)
            for dy in range(3)
        ]
        right = bb[pl.ds((z + 1) * 192, 192), 128:640]
        taps[...] += dot_nt(jnp.concatenate(blocks, axis=0), right)

    def fill(v, half_rows, parts):
        at_row = 0
        for part in parts:
            done, n = 0, part.shape[0]
            while done < n:
                half, row = divmod(at_row, half_rows)
                m = min(n - done, half_rows - row)
                v[half, row : row + m, :] = part[done : done + m, :].astype(BF16)
                done, at_row = done + m, at_row + m
        while at_row < 2 * half_rows:
            half, row = divmod(at_row, half_rows)
            v[half, row:, :] = jnp.zeros((half_rows - row, 128), BF16)
            at_row += half_rows - row

    fill(
        gc_v,
        at.plane * rows_of[0],
        [taps[:, :128], jnp.concatenate([taps[:288, 128:], taps[288:, 128:]], axis=1)],
    )
    conv_sum.start_pair()

    for a in range(3):
        tall = jnp.concatenate([cw[(b * 3 + a) * 192 : (b * 3 + a + 1) * 192, :].astype(F32) for b in range(3)], axis=0)
        w4[a * C : (a + 1) * C, :] = tall.T.astype(BF16)
        w2[a * C : (a + 1) * C, :] = jnp.concatenate(
            [
                cw[((b * 3 + a) * 3 + x) * C : ((b * 3 + a) * 3 + x + 1) * C, :].astype(F32)
                for b in (2, 1, 0)
                for x in range(3)
            ],
            axis=1,
        ).astype(BF16)
    conv_sum.start_plane()

    arrived(cot_copy, NEAR)

    @unrolled(0, 8)
    def _(z):
        put_cot(z + 1, 0, cot_halo[(0, 1)][z])
        put_cot(z + 1, 5, cot_halo[(0, -1)][z])

    for half in range(2):
        for q in (0, 9):
            gh[half, q * C : q * C + C, :] = jnp.zeros((C, 256), BF16)

    def grad_plane(z):
        partial = dot(w2[...], bb[pl.ds(z * 192, 576), :])
        for y in range(4):
            ga = partial[:C, (y + 2) * 128 : (y + 3) * 128]
            ga = ga + partial[C : 2 * C, (y + 1) * 128 : (y + 2) * 128]
            ga = ga + partial[2 * C :, y * 128 : y * 128 + 128]
            gh[y % 2, (z + 1) * C : (z + 2) * C, y // 2 * 128 : y // 2 * 128 + 128] = (
                ga * ds[z, :, y * 128 : y * 128 + 128]
            ).astype(BF16)

    unrolled(1, 7)(grad_plane)
    arrived(cot_copy, FAR)
    for dz, ze in ((1, 0), (-1, 9)):
        put_cot(ze, 0, cot_halo[(dz, 1)][0])
        for y in range(4):
            put_cot(ze, y + 1, cot_halo[(dz, 0)][0, :, y * 128 : y * 128 + 128])
        put_cot(ze, 5, cot_halo[(dz, -1)][0])
    grad_plane(0)
    grad_plane(7)

    def picks(shape, f_dim):
        f = lax.broadcasted_iota(jnp.int32, shape, f_dim)
        c = lax.broadcasted_iota(jnp.int32, shape, 1 - f_dim)
        out = jnp.zeros(shape, F32)
        for k in range(3):
            for y in range(2):
                cell0 = k * 128 + y * C
                inside = jnp.logical_and(c >= cell0, c < cell0 + C)
                hit = jnp.logical_and(f == 2 * (c - cell0) + (k - 1) + 128 * y, inside)
                own = jnp.logical_and(f >= 128 * y, f < 128 * y + 128)
                out = out + jnp.where(jnp.logical_and(hit, own), 1.0, 0.0)
        return out.astype(BF16)

    pick = picks((256, 384), 0)
    for half in range(2):
        some = dot(gh[half, C : 9 * C, :], pick).astype(BF16)
        for z in range(8):
            for kx in range(3):
                cols[z % 2, half, kx * C : (kx + 1) * C, z // 2 * 128 : z // 2 * 128 + 128] = some[
                    z * C : (z + 1) * C, kx * 128 : kx * 128 + 128
                ]

    def cells(z, y):
        if z < 4 and y < 2:
            return coarse[z, y]
        if z < 4:
            return coa_halo[(0, -1)][z, 0]
        return coa_halo[(-1, 0)][0, y] if y < 2 else coa_halo[(-1, -1)][0, 0]

    by_tap = {}
    for odd_z in range(2):
        for odd_y in range(2):
            shifts = [(z, y) for z in range(odd_z + 1) for y in range(odd_y + 1)]
            right = jnp.concatenate(
                [
                    jnp.concatenate([cells(z + sz, y + sy) for z in range(4) for y in range(2)], axis=0)
                    for sz, sy in shifts
                ],
                axis=1,
            )
            result = dot(cols[odd_z, odd_y], right)
            for n, (sz, sy) in enumerate(shifts):
                kz = 1 if not odd_z else 2 - 2 * sz
                ky = 1 if not odd_y else 2 - 2 * sy
                by_tap[kz, ky] = result[:, n * 128 : n * 128 + 128]
    fill(gt_v, at.plane * rows_of[1], [by_tap[kz, ky] for kz in range(3) for ky in range(3)])
    tconv_sum.start_pair()

    pick_t = picks((384, 256), 1)
    for half in range(2):
        et[half] = dot_nt(pick_t, gh[half]).astype(BF16)

    def gather(ky, zc):
        total = None
        for kx in range(3):
            rows = slice(kx * 128, kx * 128 + 128)
            if zc < 4:
                term = dot(et[int(ky != 1), rows, zc * 128 : zc * 128 + 192], w3[ky * 3 + kx])
            else:
                term = dot(et[int(ky != 1), rows, 512:576], w3[ky * 3 + kx, :C, :])
            total = term if total is None else total + term
        return total

    for zc in (4, 3, 2, 1, 0):
        low = gather(1, zc) + gather(2, zc)
        high = gather(0, zc)
        rows = (low[:C], low[C:] + high[:C])
        if zc < 4:
            for y in range(2):
                local_gc[zc, y] = rows[y]
            back_to[(0, 1)][zc] = high[C:].astype(BF16)
        else:
            for y in range(2):
                back_to[(1, 0)][y] = rows[y].astype(BF16)
            back_to[(1, 1)][0] = high[C:].astype(BF16)
    tconv_sum.start_plane()
    conv_sum.start_z()
    start(back_copy, BACK)

    @unrolled(0, 8)
    def _(z):
        partial = dot(w4[...], act[pl.ds(z * 192, 576), :])
        for y in range(4):
            row = partial[:C, y * 128 : y * 128 + 128]
            row = row + partial[C : 2 * C, (y + 1) * 128 : (y + 2) * 128]
            row = row + partial[2 * C :, (y + 2) * 128 : (y + 3) * 128]
            wide[pl.ds(z * 4 + y, C, stride=32), :] = row

    field[...] = wide[...].astype(BF16)
    outs = [pltpu.make_async_copy(field, field_out, out_sem.at[0]), pltpu.make_async_copy(gc, gc_out, out_sem.at[1])]
    outs[0].start()
    tconv_sum.start_z()
    conv_sum.start_back()

    arrived(back_copy, BACK)
    for zc in range(4):
        for y in range(2):
            total = local_gc[zc, y]
            if y == 0:
                total = total + back_from[(0, 1)][zc].astype(F32)
            if zc == 0:
                total = total + back_from[(1, 0)][y].astype(F32)
            if zc == 0 and y == 0:
                total = total + back_from[(1, 1)][0].astype(F32)
            gc[zc, y] = total.astype(BF16)
    outs[1].start()
    tconv_sum.start_back()
    conv_sum.start_share()

    def sent(copy_of, dirs=DIRS):
        for i, d in enumerate(dirs):

            @pl.when(at.has(*d))
            def _():
                copy_of(i, d).wait_send()

    sent(coa_copy)
    sent(cot_copy)
    sent(back_copy, BACK)
    for i, (total, out) in enumerate(((conv_sum, conv_out), (tconv_sum, tconv_out))):
        if total is tconv_sum:
            total.start_share()
        halves = [
            pltpu.make_async_copy(total.g.at[h], out.at[h], out_sem.at[2 * i + 2 + n])
            for n, h in enumerate((at.core, 1 - at.core))
        ]
        halves[0].start()
        total.arrive()
        halves[1].start()
        outs += halves
    conv_sum.finish()
    tconv_sum.finish()
    for copy in outs:
        copy.wait()


def unpack(n_dev, *refs):
    ins, outs, held, (gcw, gtw), (sems,) = refs[:4], refs[4:8], refs[8:12], refs[12:14], refs[14:]
    loads = [pltpu.make_async_copy(src, dst, sems.at[i]) for i, (src, dst) in enumerate(zip(ins, held))]
    stores = [
        pltpu.make_async_copy(src, dst, sems.at[4 + i])
        for i, (src, dst) in enumerate(zip((held[0], held[1], gcw, gtw), outs))
    ]
    for i in (2, 3, 0, 1):
        loads[i].start()
    conv, tconv = held[2:]
    loads[2].wait()
    conv_scale = 1.0 / math.sqrt(n_dev * 8 * 4 * 128)
    g = conv[...].reshape(-1, 128)
    first = g[:576].astype(F32) * conv_scale
    second = g[576:864].astype(F32) * conv_scale
    for zy in range(9):
        for dx in range(2):
            gcw[zy * 3 + dx] = first[zy * C : (zy + 1) * C, dx * C : (dx + 1) * C]
    for half in range(18):
        src = second[(half % 9) * 32 : (half % 9) * 32 + 32, (half // 9) * C : (half // 9 + 1) * C]
        gcw[(half // 2) * 3 + 2, (half % 2) * 32 : (half % 2) * 32 + 32, :] = src
    stores[2].start()
    loads[3].wait()
    tconv_scale = 1.0 / math.sqrt(n_dev * 4 * 2 * 64)
    gtw[...] = tconv[...].reshape(-1, 128)[:1728].astype(F32) * tconv_scale
    stores[3].start()
    for i in range(2):
        loads[i].wait()
        stores[i].start()
    for store in stores:
        store.wait()


def solution(mesh):
    nx = mesh.shape["group"]
    n_slab = mesh.shape["slab"]
    ny = 4
    nz = n_slab // (2 * ny)
    plane = ny * nx
    rows_of = [ceil16(-(-n // (2 * plane))) for n in (864, 1728)]

    def step(coarse, tw, cw, cot):
        dma = pltpu.SemaphoreType.DMA
        vmem = pltpu.VMEM
        scratch = [
            vmem((4, 2, 64, CIN), BF16),
            vmem((27 * C, CIN), BF16),
            vmem((27 * C, C), BF16),
            vmem((2048, 128), BF16),
            vmem((2048, 128), F32),
            vmem((8, C, 512), BF16),
        ]
        scratch += [vmem((COT_Z[dz][1], C, COT_Y[dy][1]), BF16) for dz, dy in DIRS]
        scratch += [vmem((COA_Z[dz][1], COA_Y[dy][1], 64, CIN), BF16) for dz, dy in DIRS]
        scratch += [vmem(shape, BF16) for shape in BACK.values()] * 2
        scratch += [
            vmem((6 * 384, 512), BF16),
            vmem((3, 192, 384), BF16),
            vmem((192, 576), BF16),
            vmem((192, 576), BF16),
            vmem((9, 192, CIN), BF16),
            vmem((10 * 192, 768), BF16),
            vmem((8, C, 512), F32),
            vmem((10 * 192, 768), BF16),
            vmem((2, 10 * C, 256), BF16),
            vmem((576, 192), F32),
            vmem((2, 384, 640), BF16),
            vmem((2, 2, 192, 512), BF16),
            vmem((4, 2, 64, CIN), F32),
        ]
        for r in rows_of:
            scratch += [
                vmem((2, plane * r, 128), BF16),
                vmem((plane * r, 128), BF16),
                vmem((plane * r, 128), BF16),
                vmem((plane - 1, r, 128), BF16),
                vmem((r, 128), BF16),
                vmem((nz, r, 128), BF16),
                vmem((2, plane * r, 128), BF16),
            ]
        scratch += [vmem((2048, 128), BF16), vmem((4, 2, 64, CIN), BF16)]
        for r in rows_of:
            scratch += [dma((2,)), dma((plane - 1,)), dma((plane - 1,)), dma((nz - 1,)), dma((nz - 1,))]
            scratch += [dma((plane - 1,)), dma((plane - 1,)), dma((plane,)), dma((plane,))]
        scratch += [dma((4,)), dma((8,)), dma((8,)), dma((8,)), dma((8,)), dma((3,)), dma((3,)), dma((6,))]
        in_hbm = pl.BlockSpec(memory_space=pltpu.HBM)
        parts = pl.pallas_call(
            functools.partial(kernel, (nz, ny, nx), rows_of),
            out_shape=(
                jax.ShapeDtypeStruct((2048, 128), BF16),
                jax.ShapeDtypeStruct((4, 2, 64, CIN), BF16),
                jax.ShapeDtypeStruct((2, plane * rows_of[0], 128), BF16),
                jax.ShapeDtypeStruct((2, plane * rows_of[1], 128), BF16),
            ),
            in_specs=[in_hbm] * 4,
            out_specs=(in_hbm,) * 4,
            scratch_shapes=scratch,
            compiler_params=pltpu.CompilerParams(
                collective_id=0, has_side_effects=True, vmem_limit_bytes=61 * 2**20
            ),
            cost_estimate=pl.CostEstimate(flops=7 * 10**9, bytes_accessed=4 * 10**6, transcendentals=500000),
        )(
            coarse.reshape(4, 2, 64, CIN),
            jnp.swapaxes(tw, 3, 4).reshape(27 * C, CIN),
            cw.reshape(27 * C, C),
            cot.reshape(2048, 128),
        )
        any_space = pl.BlockSpec(memory_space=pl.ANY)
        field, gc, gcw, gtw = pl.pallas_call(
            functools.partial(unpack, n_slab * nx),
            out_shape=(
                jax.ShapeDtypeStruct((2048, 128), BF16),
                jax.ShapeDtypeStruct((4, 2, 64, CIN), BF16),
                jax.ShapeDtypeStruct((27, C, C), F32),
                jax.ShapeDtypeStruct((27 * C, CIN), F32),
            ),
            in_specs=[any_space] * 4,
            out_specs=(any_space,) * 4,
            scratch_shapes=[
                *(vmem(part.shape, BF16) for part in parts),
                vmem((27, C, C), F32),
                vmem((27 * C, CIN), F32),
                dma((8,)),
            ],
            compiler_params=pltpu.CompilerParams(vmem_limit_bytes=61 * 2**20),
        )(*parts)
        return (
            field.reshape(1, 1, C, 8, 4, 128),
            gc.reshape(1, 1, 4, 2, 64, CIN),
            gcw.reshape(3, 3, 3, C, C),
            jnp.swapaxes(gtw.reshape(3, 3, 3, C, CIN), 3, 4),
        )

    blocks = P("group", "slab", None, None, None, None)
    return jax.shard_map(
        step,
        mesh=mesh,
        in_specs=(blocks, P(), P(), blocks),
        out_specs=(blocks, blocks, P(), P()),
        check_vma=False,
    )
```

```python
import functools
import math

import jax
import jax.numpy as jnp
from jax import lax
from jax.experimental import pallas as pl
from jax.experimental.pallas import tpu as pltpu
from jax.sharding import PartitionSpec as P

MESH = pl.DeviceIdType.MESH
F32 = jnp.float32
BF16 = jnp.bfloat16
PY = 4
CIN = 128
C = 64
NT = (((1,), (1,)), ((), ()))

DIRS = [(0, 1), (0, -1), (1, 0), (-1, 0), (1, 1), (1, -1), (-1, 1), (-1, -1)]
NEAR, FAR = DIRS[:2], DIRS[2:]
COT_Z = {1: (7, 1), 0: (0, 8), -1: (0, 1)}
COT_Y = {1: (384, 128), 0: (0, 512), -1: (0, 128)}
COA_Z = {1: (3, 1), 0: (0, 4), -1: (0, 1)}
COA_Y = {1: (1, 1), 0: (0, 2), -1: (0, 1)}
BACK = {(0, 1): (4, 64, CIN), (1, 0): (2, 64, CIN), (1, 1): (1, 64, CIN)}


def dot(a, b):
    return jnp.dot(a, b, preferred_element_type=F32)


def dot_nt(a, b):
    return lax.dot_general(a, b, NT, preferred_element_type=F32)


def unrolled(start, stop):
    def run(body):
        for i in range(start, stop):
            body(i)

    return run


def ceil16(n):
    return -(-n // 16) * 16


class Place:
    def __init__(self, nz, ny, nx):
        self.nz, self.ny, self.nx = nz, ny, nx
        self.plane = ny * nx
        self.slab = lax.axis_index("slab")
        self.x = lax.axis_index("group")
        self.core = lax.rem(self.slab, 2)
        chip = lax.div(self.slab, 2)
        self.y = lax.rem(chip, ny)
        self.z = lax.div(chip, ny)
        self.p = self.y * nx + self.x
        lane = lax.rem(self.slab, PY)
        zb = lax.div(self.slab, PY)
        self.has_y = {1: lane < PY - 1, -1: lane > 0}
        self.has_z = {1: zb < nz * ny * 2 // PY - 1, -1: zb > 0}
        ring = lambda d, n: min(d % n, n - d % n)
        steps = [(dy, dx) for dy in range(ny) for dx in range(nx) if (dy, dx) != (0, 0)]
        self.plane_far = sorted(steps, key=lambda s: -ring(s[0], ny) - ring(s[1], nx))
        self.z_far = sorted(range(1, nz), key=lambda d: -ring(d, nz))

    def has(self, dz, dy):
        if dz == 0:
            return self.has_y[dy]
        if dy == 0:
            return self.has_z[dz]
        return jnp.logical_and(self.has_z[dz], self.has_y[dy])

    def halo(self, dz, dy):
        return (self.slab + PY * dz + dy, self.x)

    def pair(self):
        return (self.slab + 1 - 2 * self.core, self.x)

    def in_plane(self, step):
        y, x = lax.rem(self.y + step[0], self.ny), lax.rem(self.x + step[1], self.nx)
        return y * self.nx + x, ((self.z * self.ny + y) * 2 + self.core, x)

    def back_in_plane(self, step):
        return self.in_plane((self.ny - step[0], self.nx - step[1]))[0]

    def along_z(self, k):
        z = lax.rem(self.z + k, self.nz)
        return ((z * self.ny + self.y) * 2 + self.core, self.x)


def remote(src, dst, send, recv, device):
    return pltpu.make_async_remote_copy(
        src_ref=src, dst_ref=dst, send_sem=send, recv_sem=recv, device_id=device, device_id_type=MESH
    )


class Reduction:
    def __init__(self, at, rows, bufs, sems):
        self.at, self.r = at, rows
        self.v, self.r0, self.s0, self.r1, self.s1, self.r2, self.g = bufs
        self.pair_sems, self.plane_send, self.plane_recv, self.z_send, self.z_recv, self.back_send, self.back_recv = sems[:7]
        self.share_send, self.share_recv = sems[7:]
        self.sent = []

    def go(self, copy):
        copy.start()
        self.sent.append(copy)
        return copy

    def start_pair(self):
        at = self.at
        self.c0 = self.go(remote(self.v.at[1 - at.core], self.r0, self.pair_sems.at[0], self.pair_sems.at[1], at.pair()))

    def start_plane(self):
        at, r = self.at, self.r
        self.c0.wait_recv()
        self.c1 = []
        for k, step in enumerate(at.plane_far):
            p, device = at.in_plane(step)
            rows = pl.ds(pl.multiple_of(p * r, 16), r)
            self.s0[rows, :] = (self.v[at.core, rows, :].astype(F32) + self.r0[rows, :].astype(F32)).astype(BF16)
            self.c1.append(
                self.go(remote(self.s0.at[rows], self.r1.at[k], self.plane_send.at[k], self.plane_recv.at[k], device))
            )

    def start_z(self):
        at, r = self.at, self.r
        rows = pl.ds(pl.multiple_of(at.p * r, 16), r)
        total = self.v[at.core, rows, :].astype(F32) + self.r0[rows, :].astype(F32)
        for k in reversed(range(at.plane - 1)):
            self.c1[k].wait_recv()
            total = total + self.r1[k].astype(F32)
        self.s1[...] = total.astype(BF16)
        self.r2[at.z] = self.s1[...]
        self.c2 = []
        for k, step in enumerate(at.z_far):
            self.c2.append(
                self.go(remote(self.s1, self.r2.at[at.z], self.z_send.at[k], self.z_recv.at[k], at.along_z(step)))
            )

    def start_back(self):
        at, r = self.at, self.r
        for c in self.c2:
            c.wait_recv()
        total = self.r2[0].astype(F32)
        for k in range(1, at.nz):
            total = total + self.r2[k].astype(F32)
        rows = pl.ds(pl.multiple_of(at.p * r, 16), r)
        self.g[at.core, rows, :] = total.astype(BF16)
        self.c3 = []
        piece = self.g.at[at.core, rows]
        for k, step in enumerate(at.plane_far):
            _, device = at.in_plane(step)
            self.c3.append(self.go(remote(piece, piece, self.back_send.at[k], self.back_recv.at[k], device)))

    def start_share(self):
        at, r = self.at, self.r
        self.c4 = []
        for k in reversed(range(at.plane)):
            p = at.p
            if k < at.plane - 1:
                self.c3[k].wait_recv()
                p = at.back_in_plane(at.plane_far[k])
            piece = self.g.at[at.core, pl.ds(pl.multiple_of(p * r, 16), r)]
            self.c4.append(self.go(remote(piece, piece, self.share_send.at[k], self.share_recv.at[k], at.pair())))

    def arrive(self):
        for c in self.c4:
            c.wait_recv()

    def finish(self):
        for c in self.sent:
            c.wait_send()


def kernel(
    dims,
    rows_of,
    coarse_hbm,
    tw_hbm,
    cw_hbm,
    cot_hbm,
    field_out,
    gc_out,
    conv_out,
    tconv_out,
    coarse,
    tw,
    cw,
    cot,
    wide,
    rows_cot,
    *rest,
):
    rest = list(rest)
    cot_halo = {d: rest.pop(0) for d in DIRS}
    coa_halo = {d: rest.pop(0) for d in DIRS}
    back_from = {d: rest.pop(0) for d in BACK}
    back_to = {d: rest.pop(0) for d in BACK}
    up, w1, w2, w4, w3, act, ds, bb, gh, taps, et, cols, local_gc = (rest.pop(0) for _ in range(13))
    bufs = [[rest.pop(0) for _ in range(7)] for _ in range(2)]
    field, gc = rest.pop(0), rest.pop(0)
    sems = [[rest.pop(0) for _ in range(9)] for _ in range(2)]
    load_sem, cot_send, cot_recv, coa_send, coa_recv, back_send, back_recv, out_sem = rest
    nz, ny, nx = dims
    at = Place(nz, ny, nx)

    loads = [
        pltpu.make_async_copy(src, dst, load_sem.at[i])
        for i, (src, dst) in enumerate(((cot_hbm, cot), (coarse_hbm, coarse), (tw_hbm, tw), (cw_hbm, cw)))
    ]
    for load in loads:
        load.start()

    barrier = pltpu.get_barrier_semaphore()
    others = [at.pair()]
    others += [at.in_plane(step)[1] for step in at.plane_far]
    others += [at.along_z(step) for step in at.z_far]
    for d in DIRS:

        @pl.when(at.has(*d))
        def _():
            pl.semaphore_signal(barrier, inc=1, device_id=at.halo(*d), device_id_type=MESH)

    for device in others:
        pl.semaphore_signal(barrier, inc=1, device_id=device, device_id_type=MESH)

    loads[0].wait()
    wide[...] = cot[...].astype(F32)
    for z in (0, 7, 1, 2, 3, 4, 5, 6):
        for y in range(4):
            rows_cot[z, :, y * 128 : y * 128 + 128] = wide[pl.ds(z * 4 + y, C, stride=32), :].astype(BF16)
    count = len(others)
    for d in DIRS:
        count = count + jnp.where(at.has(*d), 1, 0)
    pl.semaphore_wait(barrier, count)

    def coa_copy(i, d):
        (z, dz), (y, dy) = COA_Z[d[0]], COA_Y[d[1]]
        return remote(
            coarse_hbm.at[pl.ds(z, dz), pl.ds(y, dy)], coa_halo[d], coa_send.at[i], coa_recv.at[i], at.halo(*d)
        )

    def cot_copy(i, d):
        (z, dz), (y, dy) = COT_Z[d[0]], COT_Y[d[1]]
        return remote(
            rows_cot.at[pl.ds(z, dz), :, pl.ds(y, dy)], cot_halo[d], cot_send.at[i], cot_recv.at[i], at.halo(*d)
        )

    def back_copy(i, d):
        return remote(back_to[d], back_from[d], back_send.at[i], back_recv.at[i], at.halo(*d))

    def start(copy_of, dirs=DIRS):
        for i, d in enumerate(dirs):

            @pl.when(at.has(*d))
            def _():
                copy_of(i, d).start()

    def arrived(copy_of, dirs=DIRS):
        for i, d in enumerate(dirs):

            @pl.when(at.has(-d[0], -d[1]))
            def _():
                copy_of(i + (2 if dirs is FAR else 0), d).wait_recv()

    start(coa_copy)

    start(cot_copy)

    for d in DIRS:

        @pl.when(jnp.logical_not(at.has(-d[0], -d[1])))
        def _():
            cot_halo[d][...] = jnp.zeros_like(cot_halo[d])
            coa_halo[d][...] = jnp.zeros_like(coa_halo[d])
            if d in BACK:
                back_from[d][...] = jnp.zeros_like(back_from[d])

    loads[1].wait()

    loads[2].wait()
    loads[3].wait()
    for kz in range(3):
        for ky in range(3):
            for kx in range(3):
                block = tw[((kz * 3 + ky) * 3 + kx) * C : ((kz * 3 + ky) * 3 + kx + 1) * C, :]
                w1[kz, ky * C : (ky + 1) * C, kx * 128 : kx * 128 + 128] = block
                w3[ky * 3 + kx, kz * C : (kz + 1) * C, :] = block
    lane_at = lax.broadcasted_iota(jnp.int32, (C, 128), 1)
    not_first = jnp.where(lane_at == 0, 0.0, 1.0).astype(F32)
    not_last = jnp.where(lane_at == 127, 0.0, 1.0).astype(F32)

    def taps_of(row):
        return pltpu.roll(row, 1, 1) * not_first, row, pltpu.roll(row, 127, 1) * not_last

    def put_cot(ze, ye, row):
        before, row, after = taps_of(row.astype(F32))
        for i, value in enumerate((after, row, before)):
            bb[pl.ds(ze * 192 + i * C, C), ye * 128 : ye * 128 + 128] = value.astype(BF16)

    @unrolled(0, 8)
    def _(z):
        for y in range(4):
            put_cot(z + 1, y + 1, rows_cot[z, :, y * 128 : y * 128 + 128])

    cell = lax.broadcasted_iota(jnp.int32, (C, 384), 0)
    place = lax.broadcasted_iota(jnp.int32, (C, 384), 1)
    spread = jnp.zeros((C, 384), F32)
    for k in range(3):
        spread = spread + jnp.where(place == 2 * cell + (k - 1) + 128 * k, 1.0, 0.0) * jnp.where(
            jnp.logical_and(place >= 128 * k, place < 128 * k + 128), 1.0, 0.0
        )
    spread = spread.astype(BF16)

    def put_coarse(ze, ye, block):
        wide_block = dot(block.astype(F32).T.astype(BF16), spread).astype(BF16)
        for k in range(3):
            up[pl.ds(ze * 384 + k * 128, 128), ye * 128 : ye * 128 + 128] = wide_block[:, k * 128 : k * 128 + 128]

    @unrolled(0, 4)
    def _(z):
        for y in range(2):
            put_coarse(z + 1, y + 1, coarse[z, y])

    arrived(coa_copy, NEAR)

    @unrolled(0, 4)
    def _(z):
        put_coarse(z + 1, 0, coa_halo[(0, 1)][z, 0])
        put_coarse(z + 1, 3, coa_halo[(0, -1)][z, 0])

    has_zl = jnp.where(at.has_z[-1], 1.0, 0.0).astype(F32)
    has_zh = jnp.where(at.has_z[1], 1.0, 0.0).astype(F32)
    has_yl = jnp.where(at.has_y[-1], 1.0, 0.0).astype(F32)
    has_yh = jnp.where(at.has_y[1], 1.0, 0.0).astype(F32)

    def put_hidden(zf, partial, z_mask):
        for yf in range(6):
            n = yf // 2
            if yf % 2:
                h = partial[C : 2 * C, (n + 1) * 128 : (n + 2) * 128]
            else:
                h = partial[2 * C :, n * 128 : n * 128 + 128] + partial[:C, (n + 1) * 128 : (n + 2) * 128]
            mask = z_mask
            if yf in (0, 5):
                y_mask = has_yl if yf == 0 else has_yh
                mask = y_mask if mask is None else mask * y_mask
            s = 0.5 * jnp.tanh(0.5 * h) + 0.5
            row = h * s
            if mask is not None:
                row = row * mask
            for i, value in enumerate(taps_of(row)):
                act[pl.ds(zf * 192 + i * C, C), yf * 128 : yf * 128 + 128] = value.astype(BF16)
            if 0 < zf < 9 and 0 < yf < 5:
                ds[zf - 1, :, (yf - 1) * 128 : yf * 128] = s * (1.0 + h * (1.0 - s))

    w1_odd = jnp.concatenate([w1[2], w1[0]], axis=1)

    def odd_plane(m, z_mask=None):
        put_hidden(2 * m, dot(w1_odd, up[m * 384 : m * 384 + 768, :]), z_mask)

    def even_plane(m, z_mask=None):
        put_hidden(2 * m + 1, dot(w1[1], up[(m + 1) * 384 : (m + 2) * 384, :]), z_mask)

    for m in range(4):
        if m:
            odd_plane(m)
        even_plane(m)

    arrived(coa_copy, FAR)
    for dz, ze in ((1, 0), (-1, 5)):
        put_coarse(ze, 0, coa_halo[(dz, 1)][0, 0])
        for y in range(2):
            put_coarse(ze, y + 1, coa_halo[(dz, 0)][0, y])
        put_coarse(ze, 3, coa_halo[(dz, -1)][0, 0])

    odd_plane(0, has_zl)
    odd_plane(4)
    even_plane(4, has_zh)

    gc_v, gt_v = bufs[0][0], bufs[1][0]
    conv_sum = Reduction(at, rows_of[0], bufs[0], sems[0])
    tconv_sum = Reduction(at, rows_of[1], bufs[1], sems[1])
    taps[...] = jnp.zeros_like(taps)

    @unrolled(0, 8)
    def _(z):
        blocks = [
            act[pl.ds((z + dz) * 192 + C, C), dy * 128 : dy * 128 + 512]
            for dz in range(3)
            for dy in range(3)
        ]
        right = bb[pl.ds((z + 1) * 192, 192), 128:640]
        taps[...] += dot_nt(jnp.concatenate(blocks, axis=0), right)

    def fill(v, half_rows, parts):
        at_row = 0
        for part in parts:
            done, n = 0, part.shape[0]
            while done < n:
                half, row = divmod(at_row, half_rows)
                m = min(n - done, half_rows - row)
                v[half, row : row + m, :] = part[done : done + m, :].astype(BF16)
                done, at_row = done + m, at_row + m
        while at_row < 2 * half_rows:
            half, row = divmod(at_row, half_rows)
            v[half, row:, :] = jnp.zeros((half_rows - row, 128), BF16)
            at_row += half_rows - row

    fill(
        gc_v,
        at.plane * rows_of[0],
        [taps[:, :128], jnp.concatenate([taps[:288, 128:], taps[288:, 128:]], axis=1)],
    )
    conv_sum.start_pair()

    for a in range(3):
        tall = jnp.concatenate([cw[(b * 3 + a) * 192 : (b * 3 + a + 1) * 192, :].astype(F32) for b in range(3)], axis=0)
        w4[a * C : (a + 1) * C, :] = tall.T.astype(BF16)
        w2[a * C : (a + 1) * C, :] = jnp.concatenate(
            [
                cw[((b * 3 + a) * 3 + x) * C : ((b * 3 + a) * 3 + x + 1) * C, :].astype(F32)
                for b in (2, 1, 0)
                for x in range(3)
            ],
            axis=1,
        ).astype(BF16)
    conv_sum.start_plane()

    arrived(cot_copy, NEAR)

    @unrolled(0, 8)
    def _(z):
        put_cot(z + 1, 0, cot_halo[(0, 1)][z])
        put_cot(z + 1, 5, cot_halo[(0, -1)][z])

    for half in range(2):
        for q in (0, 9):
            gh[half, q * C : q * C + C, :] = jnp.zeros((C, 256), BF16)

    def grad_plane(z):
        partial = dot(w2[...], bb[pl.ds(z * 192, 576), :])
        for y in range(4):
            ga = partial[:C, (y + 2) * 128 : (y + 3) * 128]
            ga = ga + partial[C : 2 * C, (y + 1) * 128 : (y + 2) * 128]
            ga = ga + partial[2 * C :, y * 128 : y * 128 + 128]
            gh[y % 2, (z + 1) * C : (z + 2) * C, y // 2 * 128 : y // 2 * 128 + 128] = (
                ga * ds[z, :, y * 128 : y * 128 + 128]
            ).astype(BF16)

    unrolled(1, 7)(grad_plane)
    arrived(cot_copy, FAR)
    for dz, ze in ((1, 0), (-1, 9)):
        put_cot(ze, 0, cot_halo[(dz, 1)][0])
        for y in range(4):
            put_cot(ze, y + 1, cot_halo[(dz, 0)][0, :, y * 128 : y * 128 + 128])
        put_cot(ze, 5, cot_halo[(dz, -1)][0])
    grad_plane(0)
    grad_plane(7)

    def picks(shape, f_dim):
        f = lax.broadcasted_iota(jnp.int32, shape, f_dim)
        c = lax.broadcasted_iota(jnp.int32, shape, 1 - f_dim)
        out = jnp.zeros(shape, F32)
        for k in range(3):
            for y in range(2):
                cell0 = k * 128 + y * C
                inside = jnp.logical_and(c >= cell0, c < cell0 + C)
                hit = jnp.logical_and(f == 2 * (c - cell0) + (k - 1) + 128 * y, inside)
                own = jnp.logical_and(f >= 128 * y, f < 128 * y + 128)
                out = out + jnp.where(jnp.logical_and(hit, own), 1.0, 0.0)
        return out.astype(BF16)

    pick = picks((256, 384), 0)
    for half in range(2):
        some = dot(gh[half, C : 9 * C, :], pick).astype(BF16)
        for z in range(8):
            for kx in range(3):
                cols[z % 2, half, kx * C : (kx + 1) * C, z // 2 * 128 : z // 2 * 128 + 128] = some[
                    z * C : (z + 1) * C, kx * 128 : kx * 128 + 128
                ]

    def cells(z, y):
        if z < 4 and y < 2:
            return coarse[z, y]
        if z < 4:
            return coa_halo[(0, -1)][z, 0]
        return coa_halo[(-1, 0)][0, y] if y < 2 else coa_halo[(-1, -1)][0, 0]

    by_tap = {}
    for odd_z in range(2):
        for odd_y in range(2):
            shifts = [(z, y) for z in range(odd_z + 1) for y in range(odd_y + 1)]
            right = jnp.concatenate(
                [
                    jnp.concatenate([cells(z + sz, y + sy) for z in range(4) for y in range(2)], axis=0)
                    for sz, sy in shifts
                ],
                axis=1,
            )
            result = dot(cols[odd_z, odd_y], right)
            for n, (sz, sy) in enumerate(shifts):
                kz = 1 if not odd_z else 2 - 2 * sz
                ky = 1 if not odd_y else 2 - 2 * sy
                by_tap[kz, ky] = result[:, n * 128 : n * 128 + 128]
    fill(gt_v, at.plane * rows_of[1], [by_tap[kz, ky] for kz in range(3) for ky in range(3)])
    tconv_sum.start_pair()

    pick_t = picks((384, 256), 1)
    for half in range(2):
        et[half] = dot_nt(pick_t, gh[half]).astype(BF16)

    def gather(ky, zc):
        total = None
        for kx in range(3):
            rows = slice(kx * 128, kx * 128 + 128)
            if zc < 4:
                term = dot(et[int(ky != 1), rows, zc * 128 : zc * 128 + 192], w3[ky * 3 + kx])
            else:
                term = dot(et[int(ky != 1), rows, 512:576], w3[ky * 3 + kx, :C, :])
            total = term if total is None else total + term
        return total

    for zc in (4, 3, 2, 1, 0):
        low = gather(1, zc) + gather(2, zc)
        high = gather(0, zc)
        rows = (low[:C], low[C:] + high[:C])
        if zc < 4:
            for y in range(2):
                local_gc[zc, y] = rows[y]
            back_to[(0, 1)][zc] = high[C:].astype(BF16)
        else:
            for y in range(2):
                back_to[(1, 0)][y] = rows[y].astype(BF16)
            back_to[(1, 1)][0] = high[C:].astype(BF16)
    tconv_sum.start_plane()
    conv_sum.start_z()
    start(back_copy, BACK)

    @unrolled(0, 8)
    def _(z):
        partial = dot(w4[...], act[pl.ds(z * 192, 576), :])
        for y in range(4):
            row = partial[:C, y * 128 : y * 128 + 128]
            row = row + partial[C : 2 * C, (y + 1) * 128 : (y + 2) * 128]
            row = row + partial[2 * C :, (y + 2) * 128 : (y + 3) * 128]
            wide[pl.ds(z * 4 + y, C, stride=32), :] = row

    field[...] = wide[...].astype(BF16)
    outs = [pltpu.make_async_copy(field, field_out, out_sem.at[0]), pltpu.make_async_copy(gc, gc_out, out_sem.at[1])]
    outs[0].start()
    tconv_sum.start_z()
    conv_sum.start_back()

    arrived(back_copy, BACK)
    for zc in range(4):
        for y in range(2):
            total = local_gc[zc, y]
            if y == 0:
                total = total + back_from[(0, 1)][zc].astype(F32)
            if zc == 0:
                total = total + back_from[(1, 0)][y].astype(F32)
            if zc == 0 and y == 0:
                total = total + back_from[(1, 1)][0].astype(F32)
            gc[zc, y] = total.astype(BF16)
    outs[1].start()
    tconv_sum.start_back()
    conv_sum.start_share()

    def sent(copy_of, dirs=DIRS):
        for i, d in enumerate(dirs):

            @pl.when(at.has(*d))
            def _():
                copy_of(i, d).wait_send()

    sent(coa_copy)
    sent(cot_copy)
    sent(back_copy, BACK)
    for i, (total, out) in enumerate(((conv_sum, conv_out), (tconv_sum, tconv_out))):
        if total is tconv_sum:
            total.start_share()
        halves = [
            pltpu.make_async_copy(total.g.at[h], out.at[h], out_sem.at[2 * i + 2 + n])
            for n, h in enumerate((at.core, 1 - at.core))
        ]
        halves[0].start()
        total.arrive()
        halves[1].start()
        outs += halves
    conv_sum.finish()
    tconv_sum.finish()
    for copy in outs:
        copy.wait()


def unpack(n_dev, *refs):
    ins, outs, held, (gcw, gtw), (sems,) = refs[:4], refs[4:8], refs[8:12], refs[12:14], refs[14:]
    loads = [pltpu.make_async_copy(src, dst, sems.at[i]) for i, (src, dst) in enumerate(zip(ins, held))]
    stores = [
        pltpu.make_async_copy(src, dst, sems.at[4 + i])
        for i, (src, dst) in enumerate(zip((held[0], held[1], gcw, gtw), outs))
    ]
    for i in (2, 3, 0, 1):
        loads[i].start()
    conv, tconv = held[2:]
    loads[2].wait()
    conv_scale = 1.0 / math.sqrt(n_dev * 8 * 4 * 128)
    g = conv[...].reshape(-1, 128)
    first = g[:576].astype(F32) * conv_scale
    second = g[576:864].astype(F32) * conv_scale
    for zy in range(9):
        for dx in range(2):
            gcw[zy * 3 + dx] = first[zy * C : (zy + 1) * C, dx * C : (dx + 1) * C]
    for half in range(18):
        src = second[(half % 9) * 32 : (half % 9) * 32 + 32, (half // 9) * C : (half // 9 + 1) * C]
        gcw[(half // 2) * 3 + 2, (half % 2) * 32 : (half % 2) * 32 + 32, :] = src
    stores[2].start()
    loads[3].wait()
    tconv_scale = 1.0 / math.sqrt(n_dev * 4 * 2 * 64)
    gtw[...] = tconv[...].reshape(-1, 128)[:1728].astype(F32) * tconv_scale
    stores[3].start()
    for i in range(2):
        loads[i].wait()
        stores[i].start()
    for store in stores:
        store.wait()


def solution(mesh):
    nx = mesh.shape["group"]
    n_slab = mesh.shape["slab"]
    ny = 4
    nz = n_slab // (2 * ny)
    plane = ny * nx
    rows_of = [ceil16(-(-n // (2 * plane))) for n in (864, 1728)]

    def step(coarse, tw, cw, cot):
        dma = pltpu.SemaphoreType.DMA
        vmem = pltpu.VMEM
        scratch = [
            vmem((4, 2, 64, CIN), BF16),
            vmem((27 * C, CIN), BF16),
            vmem((27 * C, C), BF16),
            vmem((2048, 128), BF16),
            vmem((2048, 128), F32),
            vmem((8, C, 512), BF16),
        ]
        scratch += [vmem((COT_Z[dz][1], C, COT_Y[dy][1]), BF16) for dz, dy in DIRS]
        scratch += [vmem((COA_Z[dz][1], COA_Y[dy][1], 64, CIN), BF16) for dz, dy in DIRS]
        scratch += [vmem(shape, BF16) for shape in BACK.values()] * 2
        scratch += [
            vmem((6 * 384, 512), BF16),
            vmem((3, 192, 384), BF16),
            vmem((192, 576), BF16),
            vmem((192, 576), BF16),
            vmem((9, 192, CIN), BF16),
            vmem((10 * 192, 768), BF16),
            vmem((8, C, 512), F32),
            vmem((10 * 192, 768), BF16),
            vmem((2, 10 * C, 256), BF16),
            vmem((576, 192), F32),
            vmem((2, 384, 640), BF16),
            vmem((2, 2, 192, 512), BF16),
            vmem((4, 2, 64, CIN), F32),
        ]
        for r in rows_of:
            scratch += [
                vmem((2, plane * r, 128), BF16),
                vmem((plane * r, 128), BF16),
                vmem((plane * r, 128), BF16),
                vmem((plane - 1, r, 128), BF16),
                vmem((r, 128), BF16),
                vmem((nz, r, 128), BF16),
                vmem((2, plane * r, 128), BF16),
            ]
        scratch += [vmem((2048, 128), BF16), vmem((4, 2, 64, CIN), BF16)]
        for r in rows_of:
            scratch += [dma((2,)), dma((plane - 1,)), dma((plane - 1,)), dma((nz - 1,)), dma((nz - 1,))]
            scratch += [dma((plane - 1,)), dma((plane - 1,)), dma((plane,)), dma((plane,))]
        scratch += [dma((4,)), dma((8,)), dma((8,)), dma((8,)), dma((8,)), dma((3,)), dma((3,)), dma((6,))]
        in_hbm = pl.BlockSpec(memory_space=pltpu.HBM)
        parts = pl.pallas_call(
            functools.partial(kernel, (nz, ny, nx), rows_of),
            out_shape=(
                jax.ShapeDtypeStruct((2048, 128), BF16),
                jax.ShapeDtypeStruct((4, 2, 64, CIN), BF16),
                jax.ShapeDtypeStruct((2, plane * rows_of[0], 128), BF16),
                jax.ShapeDtypeStruct((2, plane * rows_of[1], 128), BF16),
            ),
            in_specs=[in_hbm] * 4,
            out_specs=(in_hbm,) * 4,
            scratch_shapes=scratch,
            compiler_params=pltpu.CompilerParams(
                collective_id=0, has_side_effects=True, vmem_limit_bytes=61 * 2**20
            ),
            cost_estimate=pl.CostEstimate(flops=7 * 10**9, bytes_accessed=4 * 10**6, transcendentals=500000),
        )(
            coarse.reshape(4, 2, 64, CIN),
            jnp.swapaxes(tw, 3, 4).reshape(27 * C, CIN),
            cw.reshape(27 * C, C),
            cot.reshape(2048, 128),
        )
        any_space = pl.BlockSpec(memory_space=pl.ANY)
        field, gc, gcw, gtw = pl.pallas_call(
            functools.partial(unpack, n_slab * nx),
            out_shape=(
                jax.ShapeDtypeStruct((2048, 128), BF16),
                jax.ShapeDtypeStruct((4, 2, 64, CIN), BF16),
                jax.ShapeDtypeStruct((27, C, C), F32),
                jax.ShapeDtypeStruct((27 * C, CIN), F32),
            ),
            in_specs=[any_space] * 4,
            out_specs=(any_space,) * 4,
            scratch_shapes=[
                *(vmem(part.shape, BF16) for part in parts),
                vmem((27, C, C), F32),
                vmem((27 * C, CIN), F32),
                dma((8,)),
            ],
            compiler_params=pltpu.CompilerParams(vmem_limit_bytes=61 * 2**20),
        )(*parts)
        return (
            field.reshape(1, 1, C, 8, 4, 128),
            gc.reshape(1, 1, 4, 2, 64, CIN),
            gcw.reshape(3, 3, 3, C, C),
            jnp.swapaxes(gtw.reshape(3, 3, 3, C, CIN), 3, 4),
        )

    blocks = P("group", "slab", None, None, None, None)
    return jax.shard_map(
        step,
        mesh=mesh,
        in_specs=(blocks, P(), P(), blocks),
        out_specs=(blocks, blocks, P(), P()),
        check_vma=False,
    )
```

```python
import functools
import math

import jax
import jax.numpy as jnp
from jax import lax
from jax.experimental import pallas as pl
from jax.experimental.pallas import tpu as pltpu
from jax.sharding import PartitionSpec as P

MESH = pl.DeviceIdType.MESH
F32 = jnp.float32
BF16 = jnp.bfloat16
PY = 4
CIN = 128
C = 64
NT = (((1,), (1,)), ((), ()))

DIRS = [(0, 1), (0, -1), (1, 0), (-1, 0), (1, 1), (1, -1), (-1, 1), (-1, -1)]
NEAR, FAR = DIRS[:2], DIRS[2:]
COT_Z = {1: (7, 1), 0: (0, 8), -1: (0, 1)}
COT_Y = {1: (384, 128), 0: (0, 512), -1: (0, 128)}
COA_Z = {1: (3, 1), 0: (0, 4), -1: (0, 1)}
COA_Y = {1: (1, 1), 0: (0, 2), -1: (0, 1)}
BACK = {(0, 1): (4, 64, CIN), (1, 0): (2, 64, CIN), (1, 1): (1, 64, CIN)}


def dot(a, b):
    return jnp.dot(a, b, preferred_element_type=F32)


def dot_nt(a, b):
    return lax.dot_general(a, b, NT, preferred_element_type=F32)


def unrolled(start, stop):
    def run(body):
        for i in range(start, stop):
            body(i)

    return run


def ceil16(n):
    return -(-n // 16) * 16


class Place:
    def __init__(self, nz, ny, nx):
        self.nz, self.ny, self.nx = nz, ny, nx
        self.plane = ny * nx
        self.slab = lax.axis_index("slab")
        self.x = lax.axis_index("group")
        self.core = lax.rem(self.slab, 2)
        chip = lax.div(self.slab, 2)
        self.y = lax.rem(chip, ny)
        self.z = lax.div(chip, ny)
        self.p = self.y * nx + self.x
        lane = lax.rem(self.slab, PY)
        zb = lax.div(self.slab, PY)
        self.has_y = {1: lane < PY - 1, -1: lane > 0}
        self.has_z = {1: zb < nz * ny * 2 // PY - 1, -1: zb > 0}
        ring = lambda d, n: min(d % n, n - d % n)
        steps = [(dy, dx) for dy in range(ny) for dx in range(nx) if (dy, dx) != (0, 0)]
        self.plane_far = sorted(steps, key=lambda s: -ring(s[0], ny) - ring(s[1], nx))
        self.z_far = sorted(range(1, nz), key=lambda d: -ring(d, nz))

    def has(self, dz, dy):
        if dz == 0:
            return self.has_y[dy]
        if dy == 0:
            return self.has_z[dz]
        return jnp.logical_and(self.has_z[dz], self.has_y[dy])

    def halo(self, dz, dy):
        return (self.slab + PY * dz + dy, self.x)

    def pair(self):
        return (self.slab + 1 - 2 * self.core, self.x)

    def in_plane(self, step):
        y, x = lax.rem(self.y + step[0], self.ny), lax.rem(self.x + step[1], self.nx)
        return y * self.nx + x, ((self.z * self.ny + y) * 2 + self.core, x)

    def back_in_plane(self, step):
        return self.in_plane((self.ny - step[0], self.nx - step[1]))[0]

    def along_z(self, k):
        z = lax.rem(self.z + k, self.nz)
        return ((z * self.ny + self.y) * 2 + self.core, self.x)


def remote(src, dst, send, recv, device):
    return pltpu.make_async_remote_copy(
        src_ref=src, dst_ref=dst, send_sem=send, recv_sem=recv, device_id=device, device_id_type=MESH
    )


class Reduction:
    def __init__(self, at, rows, bufs, sems):
        self.at, self.r = at, rows
        self.v, self.r0, self.s0, self.r1, self.s1, self.r2, self.g = bufs
        self.pair_sems, self.plane_send, self.plane_recv, self.z_send, self.z_recv, self.back_send, self.back_recv = sems[:7]
        self.share_send, self.share_recv = sems[7:]
        self.sent = []

    def go(self, copy):
        copy.start()
        self.sent.append(copy)
        return copy

    def start_pair(self):
        at = self.at
        self.c0 = self.go(remote(self.v.at[1 - at.core], self.r0, self.pair_sems.at[0], self.pair_sems.at[1], at.pair()))

    def start_plane(self):
        at, r = self.at, self.r
        self.c0.wait_recv()
        self.c1 = []
        for k, step in enumerate(at.plane_far):
            p, device = at.in_plane(step)
            rows = pl.ds(pl.multiple_of(p * r, 16), r)
            self.s0[rows, :] = (self.v[at.core, rows, :].astype(F32) + self.r0[rows, :].astype(F32)).astype(BF16)
            self.c1.append(
                self.go(remote(self.s0.at[rows], self.r1.at[k], self.plane_send.at[k], self.plane_recv.at[k], device))
            )

    def start_z(self):
        at, r = self.at, self.r
        rows = pl.ds(pl.multiple_of(at.p * r, 16), r)
        total = self.v[at.core, rows, :].astype(F32) + self.r0[rows, :].astype(F32)
        for k in reversed(range(at.plane - 1)):
            self.c1[k].wait_recv()
            total = total + self.r1[k].astype(F32)
        self.s1[...] = total.astype(BF16)
        self.r2[at.z] = self.s1[...]
        self.c2 = []
        for k, step in enumerate(at.z_far):
            self.c2.append(
                self.go(remote(self.s1, self.r2.at[at.z], self.z_send.at[k], self.z_recv.at[k], at.along_z(step)))
            )

    def start_back(self):
        at, r = self.at, self.r
        for c in self.c2:
            c.wait_recv()
        total = self.r2[0].astype(F32)
        for k in range(1, at.nz):
            total = total + self.r2[k].astype(F32)
        rows = pl.ds(pl.multiple_of(at.p * r, 16), r)
        self.g[at.core, rows, :] = total.astype(BF16)
        self.c3 = []
        piece = self.g.at[at.core, rows]
        for k, step in enumerate(at.plane_far):
            _, device = at.in_plane(step)
            self.c3.append(self.go(remote(piece, piece, self.back_send.at[k], self.back_recv.at[k], device)))

    def start_share(self):
        at, r = self.at, self.r
        self.c4 = []
        for k in reversed(range(at.plane)):
            p = at.p
            if k < at.plane - 1:
                self.c3[k].wait_recv()
                p = at.back_in_plane(at.plane_far[k])
            piece = self.g.at[at.core, pl.ds(pl.multiple_of(p * r, 16), r)]
            self.c4.append(self.go(remote(piece, piece, self.share_send.at[k], self.share_recv.at[k], at.pair())))

    def arrive(self):
        for c in self.c4:
            c.wait_recv()

    def finish(self):
        for c in self.sent:
            c.wait_send()


def kernel(
    dims,
    rows_of,
    coarse_hbm,
    tw_hbm,
    cw_hbm,
    cot_hbm,
    field_out,
    gc_out,
    conv_out,
    tconv_out,
    coarse,
    tw,
    cw,
    cot,
    wide,
    rows_cot,
    *rest,
):
    rest = list(rest)
    cot_halo = {d: rest.pop(0) for d in DIRS}
    coa_halo = {d: rest.pop(0) for d in DIRS}
    back_from = {d: rest.pop(0) for d in BACK}
    back_to = {d: rest.pop(0) for d in BACK}
    up, w1, w2, w4, w3, act, ds, bb, gh, taps, et, cols, local_gc = (rest.pop(0) for _ in range(13))
    bufs = [[rest.pop(0) for _ in range(7)] for _ in range(2)]
    field, gc = rest.pop(0), rest.pop(0)
    sems = [[rest.pop(0) for _ in range(9)] for _ in range(2)]
    load_sem, cot_send, cot_recv, coa_send, coa_recv, back_send, back_recv, out_sem = rest
    nz, ny, nx = dims
    at = Place(nz, ny, nx)

    loads = [
        pltpu.make_async_copy(src, dst, load_sem.at[i])
        for i, (src, dst) in enumerate(((cot_hbm, cot), (coarse_hbm, coarse), (tw_hbm, tw), (cw_hbm, cw)))
    ]
    for load in loads:
        load.start()

    barrier = pltpu.get_barrier_semaphore()
    others = [at.pair()]
    others += [at.in_plane(step)[1] for step in at.plane_far]
    others += [at.along_z(step) for step in at.z_far]
    for d in DIRS:

        @pl.when(at.has(*d))
        def _():
            pl.semaphore_signal(barrier, inc=1, device_id=at.halo(*d), device_id_type=MESH)

    for device in others:
        pl.semaphore_signal(barrier, inc=1, device_id=device, device_id_type=MESH)

    loads[0].wait()
    wide[...] = cot[...].astype(F32)
    for z in (0, 7, 1, 2, 3, 4, 5, 6):
        for y in range(4):
            rows_cot[z, :, y * 128 : y * 128 + 128] = wide[pl.ds(z * 4 + y, C, stride=32), :].astype(BF16)
    count = len(others)
    for d in DIRS:
        count = count + jnp.where(at.has(*d), 1, 0)
    pl.semaphore_wait(barrier, count)

    def coa_copy(i, d):
        (z, dz), (y, dy) = COA_Z[d[0]], COA_Y[d[1]]
        return remote(
            coarse_hbm.at[pl.ds(z, dz), pl.ds(y, dy)], coa_halo[d], coa_send.at[i], coa_recv.at[i], at.halo(*d)
        )

    def cot_copy(i, d):
        (z, dz), (y, dy) = COT_Z[d[0]], COT_Y[d[1]]
        return remote(
            rows_cot.at[pl.ds(z, dz), :, pl.ds(y, dy)], cot_halo[d], cot_send.at[i], cot_recv.at[i], at.halo(*d)
        )

    def back_copy(i, d):
        return remote(back_to[d], back_from[d], back_send.at[i], back_recv.at[i], at.halo(*d))

    def start(copy_of, dirs=DIRS):
        for i, d in enumerate(dirs):

            @pl.when(at.has(*d))
            def _():
                copy_of(i, d).start()

    def arrived(copy_of, dirs=DIRS):
        for i, d in enumerate(dirs):

            @pl.when(at.has(-d[0], -d[1]))
            def _():
                copy_of(i + (2 if dirs is FAR else 0), d).wait_recv()

    start(coa_copy)

    start(cot_copy)

    for d in DIRS:

        @pl.when(jnp.logical_not(at.has(-d[0], -d[1])))
        def _():
            cot_halo[d][...] = jnp.zeros_like(cot_halo[d])
            coa_halo[d][...] = jnp.zeros_like(coa_halo[d])
            if d in BACK:
                back_from[d][...] = jnp.zeros_like(back_from[d])

    loads[1].wait()

    loads[2].wait()
    loads[3].wait()
    for kz in range(3):
        for ky in range(3):
            for kx in range(3):
                block = tw[((kz * 3 + ky) * 3 + kx) * C : ((kz * 3 + ky) * 3 + kx + 1) * C, :]
                w1[kz, ky * C : (ky + 1) * C, kx * 128 : kx * 128 + 128] = block
                w3[ky * 3 + kx, kz * C : (kz + 1) * C, :] = block
    lane_at = lax.broadcasted_iota(jnp.int32, (C, 128), 1)
    not_first = jnp.where(lane_at == 0, 0.0, 1.0).astype(F32)
    not_last = jnp.where(lane_at == 127, 0.0, 1.0).astype(F32)

    def taps_of(row):
        return pltpu.roll(row, 1, 1) * not_first, row, pltpu.roll(row, 127, 1) * not_last

    def put_cot(ze, ye, row):
        before, row, after = taps_of(row.astype(F32))
        for i, value in enumerate((after, row, before)):
            bb[pl.ds(ze * 192 + i * C, C), ye * 128 : ye * 128 + 128] = value.astype(BF16)

    @unrolled(0, 8)
    def _(z):
        for y in range(4):
            put_cot(z + 1, y + 1, rows_cot[z, :, y * 128 : y * 128 + 128])

    cell = lax.broadcasted_iota(jnp.int32, (C, 384), 0)
    place = lax.broadcasted_iota(jnp.int32, (C, 384), 1)
    spread = jnp.zeros((C, 384), F32)
    for k in range(3):
        spread = spread + jnp.where(place == 2 * cell + (k - 1) + 128 * k, 1.0, 0.0) * jnp.where(
            jnp.logical_and(place >= 128 * k, place < 128 * k + 128), 1.0, 0.0
        )
    spread = spread.astype(BF16)

    def put_coarse(ze, ye, block):
        wide_block = dot(block.astype(F32).T.astype(BF16), spread).astype(BF16)
        for k in range(3):
            up[pl.ds(ze * 384 + k * 128, 128), ye * 128 : ye * 128 + 128] = wide_block[:, k * 128 : k * 128 + 128]

    @unrolled(0, 4)
    def _(z):
        for y in range(2):
            put_coarse(z + 1, y + 1, coarse[z, y])

    arrived(coa_copy, NEAR)

    @unrolled(0, 4)
    def _(z):
        put_coarse(z + 1, 0, coa_halo[(0, 1)][z, 0])
        put_coarse(z + 1, 3, coa_halo[(0, -1)][z, 0])

    has_zl = jnp.where(at.has_z[-1], 1.0, 0.0).astype(F32)
    has_zh = jnp.where(at.has_z[1], 1.0, 0.0).astype(F32)
    has_yl = jnp.where(at.has_y[-1], 1.0, 0.0).astype(F32)
    has_yh = jnp.where(at.has_y[1], 1.0, 0.0).astype(F32)

    def put_hidden(zf, partial, z_mask):
        for yf in range(6):
            n = yf // 2
            if yf % 2:
                h = partial[C : 2 * C, (n + 1) * 128 : (n + 2) * 128]
            else:
                h = partial[2 * C :, n * 128 : n * 128 + 128] + partial[:C, (n + 1) * 128 : (n + 2) * 128]
            mask = z_mask
            if yf in (0, 5):
                y_mask = has_yl if yf == 0 else has_yh
                mask = y_mask if mask is None else mask * y_mask
            s = 0.5 * jnp.tanh(0.5 * h) + 0.5
            row = h * s
            if mask is not None:
                row = row * mask
            for i, value in enumerate(taps_of(row)):
                act[pl.ds(zf * 192 + i * C, C), yf * 128 : yf * 128 + 128] = value.astype(BF16)
            if 0 < zf < 9 and 0 < yf < 5:
                ds[zf - 1, :, (yf - 1) * 128 : yf * 128] = s * (1.0 + h * (1.0 - s))

    w1_odd = jnp.concatenate([w1[2], w1[0]], axis=1)

    def odd_plane(m, z_mask=None):
        put_hidden(2 * m, dot(w1_odd, up[m * 384 : m * 384 + 768, :]), z_mask)

    def even_plane(m, z_mask=None):
        put_hidden(2 * m + 1, dot(w1[1], up[(m + 1) * 384 : (m + 2) * 384, :]), z_mask)

    for m in range(4):
        if m:
            odd_plane(m)
        even_plane(m)

    arrived(coa_copy, FAR)
    for dz, ze in ((1, 0), (-1, 5)):
        put_coarse(ze, 0, coa_halo[(dz, 1)][0, 0])
        for y in range(2):
            put_coarse(ze, y + 1, coa_halo[(dz, 0)][0, y])
        put_coarse(ze, 3, coa_halo[(dz, -1)][0, 0])

    odd_plane(0, has_zl)
    odd_plane(4)
    even_plane(4, has_zh)

    gc_v, gt_v = bufs[0][0], bufs[1][0]
    conv_sum = Reduction(at, rows_of[0], bufs[0], sems[0])
    tconv_sum = Reduction(at, rows_of[1], bufs[1], sems[1])
    taps[...] = jnp.zeros_like(taps)

    @unrolled(0, 8)
    def _(z):
        blocks = [
            act[pl.ds((z + dz) * 192 + C, C), dy * 128 : dy * 128 + 512]
            for dz in range(3)
            for dy in range(3)
        ]
        right = bb[pl.ds((z + 1) * 192, 192), 128:640]
        taps[...] += dot_nt(jnp.concatenate(blocks, axis=0), right)

    def fill(v, half_rows, parts):
        at_row = 0
        for part in parts:
            done, n = 0, part.shape[0]
            while done < n:
                half, row = divmod(at_row, half_rows)
                m = min(n - done, half_rows - row)
                v[half, row : row + m, :] = part[done : done + m, :].astype(BF16)
                done, at_row = done + m, at_row + m
        while at_row < 2 * half_rows:
            half, row = divmod(at_row, half_rows)
            v[half, row:, :] = jnp.zeros((half_rows - row, 128), BF16)
            at_row += half_rows - row

    fill(
        gc_v,
        at.plane * rows_of[0],
        [taps[:, :128], jnp.concatenate([taps[:288, 128:], taps[288:, 128:]], axis=1)],
    )
    conv_sum.start_pair()

    for a in range(3):
        tall = jnp.concatenate([cw[(b * 3 + a) * 192 : (b * 3 + a + 1) * 192, :].astype(F32) for b in range(3)], axis=0)
        w4[a * C : (a + 1) * C, :] = tall.T.astype(BF16)
        w2[a * C : (a + 1) * C, :] = jnp.concatenate(
            [
                cw[((b * 3 + a) * 3 + x) * C : ((b * 3 + a) * 3 + x + 1) * C, :].astype(F32)
                for b in (2, 1, 0)
                for x in range(3)
            ],
            axis=1,
        ).astype(BF16)
    conv_sum.start_plane()

    arrived(cot_copy, NEAR)

    @unrolled(0, 8)
    def _(z):
        put_cot(z + 1, 0, cot_halo[(0, 1)][z])
        put_cot(z + 1, 5, cot_halo[(0, -1)][z])

    def picks(shape, f_dim):
        f = lax.broadcasted_iota(jnp.int32, shape, f_dim)
        c = lax.broadcasted_iota(jnp.int32, shape, 1 - f_dim)
        out = jnp.zeros(shape, F32)
        for k in range(3):
            for y in range(2):
                cell0 = k * 128 + y * C
                inside = jnp.logical_and(c >= cell0, c < cell0 + C)
                hit = jnp.logical_and(f == 2 * (c - cell0) + (k - 1) + 128 * y, inside)
                own = jnp.logical_and(f >= 128 * y, f < 128 * y + 128)
                out = out + jnp.where(jnp.logical_and(hit, own), 1.0, 0.0)
        return out.astype(BF16)

    pick = picks((256, 384), 0)

    def put_picked(planes):
        for half in range(2):
            some = dot(gh[half, (planes[0] + 1) * C : (planes[-1] + 2) * C, :], pick).astype(BF16)
            for n, z in enumerate(planes):
                for kx in range(3):
                    cols[z % 2, half, kx * C : (kx + 1) * C, z // 2 * 128 : z // 2 * 128 + 128] = some[
                        n * C : (n + 1) * C, kx * 128 : kx * 128 + 128
                    ]

    for half in range(2):
        for q in (0, 9):
            gh[half, q * C : q * C + C, :] = jnp.zeros((C, 256), BF16)

    def grad_plane(z):
        partial = dot(w2[...], bb[pl.ds(z * 192, 576), :])
        for y in range(4):
            ga = partial[:C, (y + 2) * 128 : (y + 3) * 128]
            ga = ga + partial[C : 2 * C, (y + 1) * 128 : (y + 2) * 128]
            ga = ga + partial[2 * C :, y * 128 : y * 128 + 128]
            gh[y % 2, (z + 1) * C : (z + 2) * C, y // 2 * 128 : y // 2 * 128 + 128] = (
                ga * ds[z, :, y * 128 : y * 128 + 128]
            ).astype(BF16)

    unrolled(1, 7)(grad_plane)
    put_picked(range(1, 7))
    arrived(cot_copy, FAR)
    for dz, ze in ((1, 0), (-1, 9)):
        put_cot(ze, 0, cot_halo[(dz, 1)][0])
        for y in range(4):
            put_cot(ze, y + 1, cot_halo[(dz, 0)][0, :, y * 128 : y * 128 + 128])
        put_cot(ze, 5, cot_halo[(dz, -1)][0])
    grad_plane(0)
    grad_plane(7)
    put_picked([0])
    put_picked([7])


    def cells(z, y):
        if z < 4 and y < 2:
            return coarse[z, y]
        if z < 4:
            return coa_halo[(0, -1)][z, 0]
        return coa_halo[(-1, 0)][0, y] if y < 2 else coa_halo[(-1, -1)][0, 0]

    by_tap = {}
    for odd_z in range(2):
        for odd_y in range(2):
            shifts = [(z, y) for z in range(odd_z + 1) for y in range(odd_y + 1)]
            right = jnp.concatenate(
                [
                    jnp.concatenate([cells(z + sz, y + sy) for z in range(4) for y in range(2)], axis=0)
                    for sz, sy in shifts
                ],
                axis=1,
            )
            result = dot(cols[odd_z, odd_y], right)
            for n, (sz, sy) in enumerate(shifts):
                kz = 1 if not odd_z else 2 - 2 * sz
                ky = 1 if not odd_y else 2 - 2 * sy
                by_tap[kz, ky] = result[:, n * 128 : n * 128 + 128]
    fill(gt_v, at.plane * rows_of[1], [by_tap[kz, ky] for kz in range(3) for ky in range(3)])
    tconv_sum.start_pair()

    pick_t = picks((384, 256), 1)
    for half in range(2):
        et[half] = dot_nt(pick_t, gh[half]).astype(BF16)

    def gather(ky, zc):
        total = None
        for kx in range(3):
            rows = slice(kx * 128, kx * 128 + 128)
            if zc < 4:
                term = dot(et[int(ky != 1), rows, zc * 128 : zc * 128 + 192], w3[ky * 3 + kx])
            else:
                term = dot(et[int(ky != 1), rows, 512:576], w3[ky * 3 + kx, :C, :])
            total = term if total is None else total + term
        return total

    for zc in (4, 3, 2, 1, 0):
        low = gather(1, zc) + gather(2, zc)
        high = gather(0, zc)
        rows = (low[:C], low[C:] + high[:C])
        if zc < 4:
            for y in range(2):
                local_gc[zc, y] = rows[y]
            back_to[(0, 1)][zc] = high[C:].astype(BF16)
        else:
            for y in range(2):
                back_to[(1, 0)][y] = rows[y].astype(BF16)
            back_to[(1, 1)][0] = high[C:].astype(BF16)
    tconv_sum.start_plane()
    conv_sum.start_z()
    start(back_copy, BACK)

    @unrolled(0, 8)
    def _(z):
        partial = dot(w4[...], act[pl.ds(z * 192, 576), :])
        for y in range(4):
            row = partial[:C, y * 128 : y * 128 + 128]
            row = row + partial[C : 2 * C, (y + 1) * 128 : (y + 2) * 128]
            row = row + partial[2 * C :, (y + 2) * 128 : (y + 3) * 128]
            wide[pl.ds(z * 4 + y, C, stride=32), :] = row

    field[...] = wide[...].astype(BF16)
    outs = [pltpu.make_async_copy(field, field_out, out_sem.at[0]), pltpu.make_async_copy(gc, gc_out, out_sem.at[1])]
    outs[0].start()
    tconv_sum.start_z()
    conv_sum.start_back()

    arrived(back_copy, BACK)
    for zc in range(4):
        for y in range(2):
            total = local_gc[zc, y]
            if y == 0:
                total = total + back_from[(0, 1)][zc].astype(F32)
            if zc == 0:
                total = total + back_from[(1, 0)][y].astype(F32)
            if zc == 0 and y == 0:
                total = total + back_from[(1, 1)][0].astype(F32)
            gc[zc, y] = total.astype(BF16)
    outs[1].start()
    tconv_sum.start_back()
    conv_sum.start_share()

    def sent(copy_of, dirs=DIRS):
        for i, d in enumerate(dirs):

            @pl.when(at.has(*d))
            def _():
                copy_of(i, d).wait_send()

    sent(coa_copy)
    sent(cot_copy)
    sent(back_copy, BACK)
    for i, (total, out) in enumerate(((conv_sum, conv_out), (tconv_sum, tconv_out))):
        if total is tconv_sum:
            total.start_share()
        halves = [
            pltpu.make_async_copy(total.g.at[h], out.at[h], out_sem.at[2 * i + 2 + n])
            for n, h in enumerate((at.core, 1 - at.core))
        ]
        halves[0].start()
        total.arrive()
        halves[1].start()
        outs += halves
    conv_sum.finish()
    tconv_sum.finish()
    for copy in outs:
        copy.wait()


def unpack(n_dev, *refs):
    ins, outs, held, (gcw, gtw), (sems,) = refs[:4], refs[4:8], refs[8:12], refs[12:14], refs[14:]
    loads = [pltpu.make_async_copy(src, dst, sems.at[i]) for i, (src, dst) in enumerate(zip(ins, held))]
    stores = [
        pltpu.make_async_copy(src, dst, sems.at[4 + i])
        for i, (src, dst) in enumerate(zip((held[0], held[1], gcw, gtw), outs))
    ]
    for load in loads:
        load.start()
    for i in range(2):
        loads[i].wait()
        stores[i].start()
    conv, tconv = held[2:]
    loads[2].wait()
    conv_scale = 1.0 / math.sqrt(n_dev * 8 * 4 * 128)
    g = conv[...].reshape(-1, 128)
    first = g[:576].astype(F32) * conv_scale
    second = g[576:864].astype(F32) * conv_scale
    for zy in range(9):
        for dx in range(2):
            gcw[zy * 3 + dx] = first[zy * C : (zy + 1) * C, dx * C : (dx + 1) * C]
    for half in range(18):
        src = second[(half % 9) * 32 : (half % 9) * 32 + 32, (half // 9) * C : (half // 9 + 1) * C]
        gcw[(half // 2) * 3 + 2, (half % 2) * 32 : (half % 2) * 32 + 32, :] = src
    stores[2].start()
    loads[3].wait()
    tconv_scale = 1.0 / math.sqrt(n_dev * 4 * 2 * 64)
    gtw[...] = tconv[...].reshape(-1, 128)[:1728].astype(F32) * tconv_scale
    stores[3].start()
    for store in stores:
        store.wait()


def solution(mesh):
    nx = mesh.shape["group"]
    n_slab = mesh.shape["slab"]
    ny = 4
    nz = n_slab // (2 * ny)
    plane = ny * nx
    rows_of = [ceil16(-(-n // (2 * plane))) for n in (864, 1728)]

    def step(coarse, tw, cw, cot):
        dma = pltpu.SemaphoreType.DMA
        vmem = pltpu.VMEM
        scratch = [
            vmem((4, 2, 64, CIN), BF16),
            vmem((27 * C, CIN), BF16),
            vmem((27 * C, C), BF16),
            vmem((2048, 128), BF16),
            vmem((2048, 128), F32),
            vmem((8, C, 512), BF16),
        ]
        scratch += [vmem((COT_Z[dz][1], C, COT_Y[dy][1]), BF16) for dz, dy in DIRS]
        scratch += [vmem((COA_Z[dz][1], COA_Y[dy][1], 64, CIN), BF16) for dz, dy in DIRS]
        scratch += [vmem(shape, BF16) for shape in BACK.values()] * 2
        scratch += [
            vmem((6 * 384, 512), BF16),
            vmem((3, 192, 384), BF16),
            vmem((192, 576), BF16),
            vmem((192, 576), BF16),
            vmem((9, 192, CIN), BF16),
            vmem((10 * 192, 768), BF16),
            vmem((8, C, 512), F32),
            vmem((10 * 192, 768), BF16),
            vmem((2, 10 * C, 256), BF16),
            vmem((576, 192), F32),
            vmem((2, 384, 640), BF16),
            vmem((2, 2, 192, 512), BF16),
            vmem((4, 2, 64, CIN), F32),
        ]
        for r in rows_of:
            scratch += [
                vmem((2, plane * r, 128), BF16),
                vmem((plane * r, 128), BF16),
                vmem((plane * r, 128), BF16),
                vmem((plane - 1, r, 128), BF16),
                vmem((r, 128), BF16),
                vmem((nz, r, 128), BF16),
                vmem((2, plane * r, 128), BF16),
            ]
        scratch += [vmem((2048, 128), BF16), vmem((4, 2, 64, CIN), BF16)]
        for r in rows_of:
            scratch += [dma((2,)), dma((plane - 1,)), dma((plane - 1,)), dma((nz - 1,)), dma((nz - 1,))]
            scratch += [dma((plane - 1,)), dma((plane - 1,)), dma((plane,)), dma((plane,))]
        scratch += [dma((4,)), dma((8,)), dma((8,)), dma((8,)), dma((8,)), dma((3,)), dma((3,)), dma((6,))]
        in_hbm = pl.BlockSpec(memory_space=pltpu.HBM)
        parts = pl.pallas_call(
            functools.partial(kernel, (nz, ny, nx), rows_of),
            out_shape=(
                jax.ShapeDtypeStruct((2048, 128), BF16),
                jax.ShapeDtypeStruct((4, 2, 64, CIN), BF16),
                jax.ShapeDtypeStruct((2, plane * rows_of[0], 128), BF16),
                jax.ShapeDtypeStruct((2, plane * rows_of[1], 128), BF16),
            ),
            in_specs=[in_hbm] * 4,
            out_specs=(in_hbm,) * 4,
            scratch_shapes=scratch,
            compiler_params=pltpu.CompilerParams(
                collective_id=0, has_side_effects=True, vmem_limit_bytes=61 * 2**20
            ),
            cost_estimate=pl.CostEstimate(flops=7 * 10**9, bytes_accessed=4 * 10**6, transcendentals=500000),
        )(
            coarse.reshape(4, 2, 64, CIN),
            jnp.swapaxes(tw, 3, 4).reshape(27 * C, CIN),
            cw.reshape(27 * C, C),
            cot.reshape(2048, 128),
        )
        any_space = pl.BlockSpec(memory_space=pl.ANY)
        field, gc, gcw, gtw = pl.pallas_call(
            functools.partial(unpack, n_slab * nx),
            out_shape=(
                jax.ShapeDtypeStruct((2048, 128), BF16),
                jax.ShapeDtypeStruct((4, 2, 64, CIN), BF16),
                jax.ShapeDtypeStruct((27, C, C), F32),
                jax.ShapeDtypeStruct((27 * C, CIN), F32),
            ),
            in_specs=[any_space] * 4,
            out_specs=(any_space,) * 4,
            scratch_shapes=[
                *(vmem(part.shape, BF16) for part in parts),
                vmem((27, C, C), F32),
                vmem((27 * C, CIN), F32),
                dma((8,)),
            ],
            compiler_params=pltpu.CompilerParams(vmem_limit_bytes=61 * 2**20),
        )(*parts)
        return (
            field.reshape(1, 1, C, 8, 4, 128),
            gc.reshape(1, 1, 4, 2, 64, CIN),
            gcw.reshape(3, 3, 3, C, C),
            jnp.swapaxes(gtw.reshape(3, 3, 3, C, CIN), 3, 4),
        )

    blocks = P("group", "slab", None, None, None, None)
    return jax.shard_map(
        step,
        mesh=mesh,
        in_specs=(blocks, P(), P(), blocks),
        out_specs=(blocks, blocks, P(), P()),
        check_vma=False,
    )
```

```python
import functools
import math

import jax
import jax.numpy as jnp
from jax import lax
from jax.experimental import pallas as pl
from jax.experimental.pallas import tpu as pltpu
from jax.sharding import PartitionSpec as P

MESH = pl.DeviceIdType.MESH
F32 = jnp.float32
BF16 = jnp.bfloat16
PY = 4
CIN = 128
C = 64
NT = (((1,), (1,)), ((), ()))

DIRS = [(0, 1), (0, -1), (1, 0), (-1, 0), (1, 1), (1, -1), (-1, 1), (-1, -1)]
NEAR, FAR = DIRS[:2], DIRS[2:]
COT_Z = {1: (7, 1), 0: (0, 8), -1: (0, 1)}
COT_Y = {1: (384, 128), 0: (0, 512), -1: (0, 128)}
COA_Z = {1: (3, 1), 0: (0, 4), -1: (0, 1)}
COA_Y = {1: (1, 1), 0: (0, 2), -1: (0, 1)}
BACK = {(0, 1): (4, 64, CIN), (1, 0): (2, 64, CIN), (1, 1): (1, 64, CIN)}


def dot(a, b):
    return jnp.dot(a, b, preferred_element_type=F32)


def dot_nt(a, b):
    return lax.dot_general(a, b, NT, preferred_element_type=F32)


def unrolled(start, stop):
    def run(body):
        for i in range(start, stop):
            body(i)

    return run


def ceil16(n):
    return -(-n // 16) * 16


class Place:
    def __init__(self, nz, ny, nx):
        self.nz, self.ny, self.nx = nz, ny, nx
        self.plane = ny * nx
        self.slab = lax.axis_index("slab")
        self.x = lax.axis_index("group")
        self.core = lax.rem(self.slab, 2)
        chip = lax.div(self.slab, 2)
        self.y = lax.rem(chip, ny)
        self.z = lax.div(chip, ny)
        self.p = self.y * nx + self.x
        lane = lax.rem(self.slab, PY)
        zb = lax.div(self.slab, PY)
        self.has_y = {1: lane < PY - 1, -1: lane > 0}
        self.has_z = {1: zb < nz * ny * 2 // PY - 1, -1: zb > 0}
        ring = lambda d, n: min(d % n, n - d % n)
        steps = [(dy, dx) for dy in range(ny) for dx in range(nx) if (dy, dx) != (0, 0)]
        self.plane_far = sorted(steps, key=lambda s: -ring(s[0], ny) - ring(s[1], nx))
        self.z_far = sorted(range(1, nz), key=lambda d: -ring(d, nz))

    def has(self, dz, dy):
        if dz == 0:
            return self.has_y[dy]
        if dy == 0:
            return self.has_z[dz]
        return jnp.logical_and(self.has_z[dz], self.has_y[dy])

    def halo(self, dz, dy):
        return (self.slab + PY * dz + dy, self.x)

    def pair(self):
        return (self.slab + 1 - 2 * self.core, self.x)

    def in_plane(self, step):
        y, x = lax.rem(self.y + step[0], self.ny), lax.rem(self.x + step[1], self.nx)
        return y * self.nx + x, ((self.z * self.ny + y) * 2 + self.core, x)

    def back_in_plane(self, step):
        return self.in_plane((self.ny - step[0], self.nx - step[1]))[0]

    def along_z(self, k):
        z = lax.rem(self.z + k, self.nz)
        return ((z * self.ny + self.y) * 2 + self.core, self.x)


def remote(src, dst, send, recv, device):
    return pltpu.make_async_remote_copy(
        src_ref=src, dst_ref=dst, send_sem=send, recv_sem=recv, device_id=device, device_id_type=MESH
    )


class Reduction:
    def __init__(self, at, rows, bufs, sems):
        self.at, self.r = at, rows
        self.v, self.r0, self.s0, self.r1, self.s1, self.r2, self.g = bufs
        self.pair_sems, self.plane_send, self.plane_recv, self.z_send, self.z_recv, self.back_send, self.back_recv = sems[:7]
        self.share_send, self.share_recv = sems[7:]
        self.sent = []

    def go(self, copy):
        copy.start()
        self.sent.append(copy)
        return copy

    def start_pair(self):
        at = self.at
        self.c0 = self.go(remote(self.v.at[1 - at.core], self.r0, self.pair_sems.at[0], self.pair_sems.at[1], at.pair()))

    def start_plane(self):
        at, r = self.at, self.r
        self.c0.wait_recv()
        self.c1 = []
        for k, step in enumerate(at.plane_far):
            p, device = at.in_plane(step)
            rows = pl.ds(pl.multiple_of(p * r, 16), r)
            self.s0[rows, :] = (self.v[at.core, rows, :].astype(F32) + self.r0[rows, :].astype(F32)).astype(BF16)
            self.c1.append(
                self.go(remote(self.s0.at[rows], self.r1.at[k], self.plane_send.at[k], self.plane_recv.at[k], device))
            )

    def start_z(self):
        at, r = self.at, self.r
        rows = pl.ds(pl.multiple_of(at.p * r, 16), r)
        total = self.v[at.core, rows, :].astype(F32) + self.r0[rows, :].astype(F32)
        for k in reversed(range(at.plane - 1)):
            self.c1[k].wait_recv()
            total = total + self.r1[k].astype(F32)
        self.s1[...] = total.astype(BF16)
        self.r2[at.z] = self.s1[...]
        self.c2 = []
        for k, step in enumerate(at.z_far):
            self.c2.append(
                self.go(remote(self.s1, self.r2.at[at.z], self.z_send.at[k], self.z_recv.at[k], at.along_z(step)))
            )

    def start_back(self):
        at, r = self.at, self.r
        for c in self.c2:
            c.wait_recv()
        total = self.r2[0].astype(F32)
        for k in range(1, at.nz):
            total = total + self.r2[k].astype(F32)
        rows = pl.ds(pl.multiple_of(at.p * r, 16), r)
        self.g[at.core, rows, :] = total.astype(BF16)
        self.c3 = []
        piece = self.g.at[at.core, rows]
        for k, step in enumerate(at.plane_far):
            _, device = at.in_plane(step)
            self.c3.append(self.go(remote(piece, piece, self.back_send.at[k], self.back_recv.at[k], device)))

    def start_share(self):
        at, r = self.at, self.r
        self.c4 = []
        for k in reversed(range(at.plane)):
            p = at.p
            if k < at.plane - 1:
                self.c3[k].wait_recv()
                p = at.back_in_plane(at.plane_far[k])
            piece = self.g.at[at.core, pl.ds(pl.multiple_of(p * r, 16), r)]
            self.c4.append(self.go(remote(piece, piece, self.share_send.at[k], self.share_recv.at[k], at.pair())))

    def arrive(self):
        for c in self.c4:
            c.wait_recv()

    def finish(self):
        for c in self.sent:
            c.wait_send()


def kernel(
    dims,
    rows_of,
    coarse_hbm,
    tw_hbm,
    cw_hbm,
    cot_hbm,
    field_out,
    gc_out,
    conv_out,
    tconv_out,
    coarse,
    tw,
    cw,
    cot,
    wide,
    rows_cot,
    *rest,
):
    rest = list(rest)
    cot_halo = {d: rest.pop(0) for d in DIRS}
    coa_halo = {d: rest.pop(0) for d in DIRS}
    back_from = {d: rest.pop(0) for d in BACK}
    back_to = {d: rest.pop(0) for d in BACK}
    up, w1, w2, w4, w3, act, ds, bb, gh, taps, et, cols, local_gc = (rest.pop(0) for _ in range(13))
    bufs = [[rest.pop(0) for _ in range(7)] for _ in range(2)]
    field, gc = rest.pop(0), rest.pop(0)
    sems = [[rest.pop(0) for _ in range(9)] for _ in range(2)]
    load_sem, cot_send, cot_recv, coa_send, coa_recv, back_send, back_recv, out_sem = rest
    nz, ny, nx = dims
    at = Place(nz, ny, nx)

    loads = [
        pltpu.make_async_copy(src, dst, load_sem.at[i])
        for i, (src, dst) in enumerate(((cot_hbm, cot), (coarse_hbm, coarse), (tw_hbm, tw), (cw_hbm, cw)))
    ]
    for load in loads:
        load.start()

    barrier = pltpu.get_barrier_semaphore()
    others = [at.pair()]
    others += [at.in_plane(step)[1] for step in at.plane_far]
    others += [at.along_z(step) for step in at.z_far]
    for d in DIRS:

        @pl.when(at.has(*d))
        def _():
            pl.semaphore_signal(barrier, inc=1, device_id=at.halo(*d), device_id_type=MESH)

    for device in others:
        pl.semaphore_signal(barrier, inc=1, device_id=device, device_id_type=MESH)

    loads[0].wait()
    wide[...] = cot[...].astype(F32)
    for z in (0, 7, 1, 2, 3, 4, 5, 6):
        for y in range(4):
            rows_cot[z, :, y * 128 : y * 128 + 128] = wide[pl.ds(z * 4 + y, C, stride=32), :].astype(BF16)
    count = len(others)
    for d in DIRS:
        count = count + jnp.where(at.has(*d), 1, 0)
    pl.semaphore_wait(barrier, count)

    def coa_copy(i, d):
        (z, dz), (y, dy) = COA_Z[d[0]], COA_Y[d[1]]
        return remote(
            coarse_hbm.at[pl.ds(z, dz), pl.ds(y, dy)], coa_halo[d], coa_send.at[i], coa_recv.at[i], at.halo(*d)
        )

    def cot_copy(i, d):
        (z, dz), (y, dy) = COT_Z[d[0]], COT_Y[d[1]]
        return remote(
            rows_cot.at[pl.ds(z, dz), :, pl.ds(y, dy)], cot_halo[d], cot_send.at[i], cot_recv.at[i], at.halo(*d)
        )

    def back_copy(i, d):
        return remote(back_to[d], back_from[d], back_send.at[i], back_recv.at[i], at.halo(*d))

    def start(copy_of, dirs=DIRS):
        for i, d in enumerate(dirs):

            @pl.when(at.has(*d))
            def _():
                copy_of(i, d).start()

    def arrived(copy_of, dirs=DIRS):
        for i, d in enumerate(dirs):

            @pl.when(at.has(-d[0], -d[1]))
            def _():
                copy_of(i + (2 if dirs is FAR else 0), d).wait_recv()

    start(coa_copy)

    start(cot_copy)

    for d in DIRS:

        @pl.when(jnp.logical_not(at.has(-d[0], -d[1])))
        def _():
            cot_halo[d][...] = jnp.zeros_like(cot_halo[d])
            coa_halo[d][...] = jnp.zeros_like(coa_halo[d])
            if d in BACK:
                back_from[d][...] = jnp.zeros_like(back_from[d])

    loads[1].wait()

    loads[2].wait()
    loads[3].wait()
    for kz in range(3):
        for ky in range(3):
            for kx in range(3):
                block = tw[((kz * 3 + ky) * 3 + kx) * C : ((kz * 3 + ky) * 3 + kx + 1) * C, :]
                w1[kz, ky * C : (ky + 1) * C, kx * 128 : kx * 128 + 128] = block
                w3[ky * 3 + kx, kz * C : (kz + 1) * C, :] = block
    lane_at = lax.broadcasted_iota(jnp.int32, (C, 128), 1)
    not_first = jnp.where(lane_at == 0, 0.0, 1.0).astype(F32)
    not_last = jnp.where(lane_at == 127, 0.0, 1.0).astype(F32)

    def taps_of(row):
        return pltpu.roll(row, 1, 1) * not_first, row, pltpu.roll(row, 127, 1) * not_last

    def put_cot(ze, ye, row):
        before, row, after = taps_of(row.astype(F32))
        for i, value in enumerate((after, row, before)):
            bb[pl.ds(ze * 192 + i * C, C), ye * 128 : ye * 128 + 128] = value.astype(BF16)

    @unrolled(0, 8)
    def _(z):
        for y in range(4):
            put_cot(z + 1, y + 1, rows_cot[z, :, y * 128 : y * 128 + 128])

    cell = lax.broadcasted_iota(jnp.int32, (C, 384), 0)
    place = lax.broadcasted_iota(jnp.int32, (C, 384), 1)
    spread = jnp.zeros((C, 384), F32)
    for k in range(3):
        spread = spread + jnp.where(place == 2 * cell + (k - 1) + 128 * k, 1.0, 0.0) * jnp.where(
            jnp.logical_and(place >= 128 * k, place < 128 * k + 128), 1.0, 0.0
        )
    spread = spread.astype(BF16)

    def put_coarse(ze, ye, block):
        wide_block = dot(block.astype(F32).T.astype(BF16), spread).astype(BF16)
        for k in range(3):
            up[pl.ds(ze * 384 + k * 128, 128), ye * 128 : ye * 128 + 128] = wide_block[:, k * 128 : k * 128 + 128]

    @unrolled(0, 4)
    def _(z):
        for y in range(2):
            put_coarse(z + 1, y + 1, coarse[z, y])

    arrived(coa_copy, NEAR)

    @unrolled(0, 4)
    def _(z):
        put_coarse(z + 1, 0, coa_halo[(0, 1)][z, 0])
        put_coarse(z + 1, 3, coa_halo[(0, -1)][z, 0])

    has_zl = jnp.where(at.has_z[-1], 1.0, 0.0).astype(F32)
    has_zh = jnp.where(at.has_z[1], 1.0, 0.0).astype(F32)
    has_yl = jnp.where(at.has_y[-1], 1.0, 0.0).astype(F32)
    has_yh = jnp.where(at.has_y[1], 1.0, 0.0).astype(F32)

    def put_hidden(zf, partial, z_mask):
        for yf in range(6):
            n = yf // 2
            if yf % 2:
                h = partial[C : 2 * C, (n + 1) * 128 : (n + 2) * 128]
            else:
                h = partial[2 * C :, n * 128 : n * 128 + 128] + partial[:C, (n + 1) * 128 : (n + 2) * 128]
            mask = z_mask
            if yf in (0, 5):
                y_mask = has_yl if yf == 0 else has_yh
                mask = y_mask if mask is None else mask * y_mask
            s = 0.5 * jnp.tanh(0.5 * h) + 0.5
            row = h * s
            if mask is not None:
                row = row * mask
            for i, value in enumerate(taps_of(row)):
                act[pl.ds(zf * 192 + i * C, C), yf * 128 : yf * 128 + 128] = value.astype(BF16)
            if 0 < zf < 9 and 0 < yf < 5:
                ds[zf - 1, :, (yf - 1) * 128 : yf * 128] = s * (1.0 + h * (1.0 - s))

    w1_odd = jnp.concatenate([w1[2], w1[0]], axis=1)

    def odd_plane(m, z_mask=None):
        put_hidden(2 * m, dot(w1_odd, up[m * 384 : m * 384 + 768, :]), z_mask)

    def even_plane(m, z_mask=None):
        put_hidden(2 * m + 1, dot(w1[1], up[(m + 1) * 384 : (m + 2) * 384, :]), z_mask)

    for m in range(4):
        if m:
            odd_plane(m)
        even_plane(m)

    arrived(coa_copy, FAR)
    for dz, ze in ((1, 0), (-1, 5)):
        put_coarse(ze, 0, coa_halo[(dz, 1)][0, 0])
        for y in range(2):
            put_coarse(ze, y + 1, coa_halo[(dz, 0)][0, y])
        put_coarse(ze, 3, coa_halo[(dz, -1)][0, 0])

    odd_plane(0, has_zl)
    odd_plane(4)
    even_plane(4, has_zh)

    gc_v, gt_v = bufs[0][0], bufs[1][0]
    conv_sum = Reduction(at, rows_of[0], bufs[0], sems[0])
    tconv_sum = Reduction(at, rows_of[1], bufs[1], sems[1])
    taps[...] = jnp.zeros_like(taps)

    @unrolled(0, 8)
    def _(z):
        blocks = [
            act[pl.ds((z + dz) * 192 + C, C), dy * 128 : dy * 128 + 512]
            for dz in range(3)
            for dy in range(3)
        ]
        right = bb[pl.ds((z + 1) * 192, 192), 128:640]
        taps[...] += dot_nt(jnp.concatenate(blocks, axis=0), right)

    def fill(v, half_rows, parts):
        at_row = 0
        for part in parts:
            done, n = 0, part.shape[0]
            while done < n:
                half, row = divmod(at_row, half_rows)
                m = min(n - done, half_rows - row)
                v[half, row : row + m, :] = part[done : done + m, :].astype(BF16)
                done, at_row = done + m, at_row + m
        while at_row < 2 * half_rows:
            half, row = divmod(at_row, half_rows)
            v[half, row:, :] = jnp.zeros((half_rows - row, 128), BF16)
            at_row += half_rows - row

    fill(
        gc_v,
        at.plane * rows_of[0],
        [taps[:, :128], jnp.concatenate([taps[:288, 128:], taps[288:, 128:]], axis=1)],
    )
    conv_sum.start_pair()

    for a in range(3):
        tall = jnp.concatenate([cw[(b * 3 + a) * 192 : (b * 3 + a + 1) * 192, :].astype(F32) for b in range(3)], axis=0)
        w4[a * C : (a + 1) * C, :] = tall.T.astype(BF16)
        w2[a * C : (a + 1) * C, :] = jnp.concatenate(
            [
                cw[((b * 3 + a) * 3 + x) * C : ((b * 3 + a) * 3 + x + 1) * C, :].astype(F32)
                for b in (2, 1, 0)
                for x in range(3)
            ],
            axis=1,
        ).astype(BF16)

    arrived(cot_copy, NEAR)

    @unrolled(0, 8)
    def _(z):
        put_cot(z + 1, 0, cot_halo[(0, 1)][z])
        put_cot(z + 1, 5, cot_halo[(0, -1)][z])

    conv_sum.start_plane()

    def picks(shape, f_dim):
        f = lax.broadcasted_iota(jnp.int32, shape, f_dim)
        c = lax.broadcasted_iota(jnp.int32, shape, 1 - f_dim)
        out = jnp.zeros(shape, F32)
        for k in range(3):
            for y in range(2):
                cell0 = k * 128 + y * C
                inside = jnp.logical_and(c >= cell0, c < cell0 + C)
                hit = jnp.logical_and(f == 2 * (c - cell0) + (k - 1) + 128 * y, inside)
                own = jnp.logical_and(f >= 128 * y, f < 128 * y + 128)
                out = out + jnp.where(jnp.logical_and(hit, own), 1.0, 0.0)
        return out.astype(BF16)

    pick = picks((256, 384), 0)
    pick_t = picks((384, 256), 1)

    def put_picked(planes):
        for half in range(2):
            some = dot(gh[half, (planes[0] + 1) * C : (planes[-1] + 2) * C, :], pick).astype(BF16)
            for n, z in enumerate(planes):
                for kx in range(3):
                    cols[z % 2, half, kx * C : (kx + 1) * C, z // 2 * 128 : z // 2 * 128 + 128] = some[
                        n * C : (n + 1) * C, kx * 128 : kx * 128 + 128
                    ]

    for half in range(2):
        for q in (0, 9):
            gh[half, q * C : q * C + C, :] = jnp.zeros((C, 256), BF16)

    def grad_plane(z):
        partial = dot(w2[...], bb[pl.ds(z * 192, 576), :])
        for y in range(4):
            ga = partial[:C, (y + 2) * 128 : (y + 3) * 128]
            ga = ga + partial[C : 2 * C, (y + 1) * 128 : (y + 2) * 128]
            ga = ga + partial[2 * C :, y * 128 : y * 128 + 128]
            gh[y % 2, (z + 1) * C : (z + 2) * C, y // 2 * 128 : y // 2 * 128 + 128] = (
                ga * ds[z, :, y * 128 : y * 128 + 128]
            ).astype(BF16)

    unrolled(1, 7)(grad_plane)
    put_picked(range(1, 7))
    arrived(cot_copy, FAR)
    for dz, ze in ((1, 0), (-1, 9)):
        put_cot(ze, 0, cot_halo[(dz, 1)][0])
        for y in range(4):
            put_cot(ze, y + 1, cot_halo[(dz, 0)][0, :, y * 128 : y * 128 + 128])
        put_cot(ze, 5, cot_halo[(dz, -1)][0])
    grad_plane(0)
    grad_plane(7)
    put_picked([0])
    put_picked([7])


    def cells(z, y):
        if z < 4 and y < 2:
            return coarse[z, y]
        if z < 4:
            return coa_halo[(0, -1)][z, 0]
        return coa_halo[(-1, 0)][0, y] if y < 2 else coa_halo[(-1, -1)][0, 0]

    by_tap = {}
    for odd_z in range(2):
        for odd_y in range(2):
            shifts = [(z, y) for z in range(odd_z + 1) for y in range(odd_y + 1)]
            right = jnp.concatenate(
                [
                    jnp.concatenate([cells(z + sz, y + sy) for z in range(4) for y in range(2)], axis=0)
                    for sz, sy in shifts
                ],
                axis=1,
            )
            result = dot(cols[odd_z, odd_y], right)
            for n, (sz, sy) in enumerate(shifts):
                kz = 1 if not odd_z else 2 - 2 * sz
                ky = 1 if not odd_y else 2 - 2 * sy
                by_tap[kz, ky] = result[:, n * 128 : n * 128 + 128]
    fill(gt_v, at.plane * rows_of[1], [by_tap[kz, ky] for kz in range(3) for ky in range(3)])
    tconv_sum.start_pair()

    for half in range(2):
        et[half] = dot_nt(pick_t, gh[half]).astype(BF16)

    def gather(ky, zc):
        total = None
        for kx in range(3):
            rows = slice(kx * 128, kx * 128 + 128)
            if zc < 4:
                term = dot(et[int(ky != 1), rows, zc * 128 : zc * 128 + 192], w3[ky * 3 + kx])
            else:
                term = dot(et[int(ky != 1), rows, 512:576], w3[ky * 3 + kx, :C, :])
            total = term if total is None else total + term
        return total

    for zc in (4, 3, 2, 1, 0):
        low = gather(1, zc) + gather(2, zc)
        high = gather(0, zc)
        rows = (low[:C], low[C:] + high[:C])
        if zc < 4:
            for y in range(2):
                local_gc[zc, y] = rows[y]
            back_to[(0, 1)][zc] = high[C:].astype(BF16)
        else:
            for y in range(2):
                back_to[(1, 0)][y] = rows[y].astype(BF16)
            back_to[(1, 1)][0] = high[C:].astype(BF16)
    tconv_sum.start_plane()
    conv_sum.start_z()
    start(back_copy, BACK)

    @unrolled(0, 8)
    def _(z):
        partial = dot(w4[...], act[pl.ds(z * 192, 576), :])
        for y in range(4):
            row = partial[:C, y * 128 : y * 128 + 128]
            row = row + partial[C : 2 * C, (y + 1) * 128 : (y + 2) * 128]
            row = row + partial[2 * C :, (y + 2) * 128 : (y + 3) * 128]
            wide[pl.ds(z * 4 + y, C, stride=32), :] = row

    field[...] = wide[...].astype(BF16)
    outs = [pltpu.make_async_copy(field, field_out, out_sem.at[0]), pltpu.make_async_copy(gc, gc_out, out_sem.at[1])]
    outs[0].start()
    tconv_sum.start_z()
    conv_sum.start_back()

    arrived(back_copy, BACK)
    for zc in range(4):
        for y in range(2):
            total = local_gc[zc, y]
            if y == 0:
                total = total + back_from[(0, 1)][zc].astype(F32)
            if zc == 0:
                total = total + back_from[(1, 0)][y].astype(F32)
            if zc == 0 and y == 0:
                total = total + back_from[(1, 1)][0].astype(F32)
            gc[zc, y] = total.astype(BF16)
    outs[1].start()
    tconv_sum.start_back()
    conv_sum.start_share()

    def sent(copy_of, dirs=DIRS):
        for i, d in enumerate(dirs):

            @pl.when(at.has(*d))
            def _():
                copy_of(i, d).wait_send()

    sent(coa_copy)
    sent(cot_copy)
    sent(back_copy, BACK)
    for i, (total, out) in enumerate(((conv_sum, conv_out), (tconv_sum, tconv_out))):
        if total is tconv_sum:
            total.start_share()
        halves = [
            pltpu.make_async_copy(total.g.at[h], out.at[h], out_sem.at[2 * i + 2 + n])
            for n, h in enumerate((at.core, 1 - at.core))
        ]
        halves[0].start()
        total.arrive()
        halves[1].start()
        outs += halves
    conv_sum.finish()
    tconv_sum.finish()
    for copy in outs:
        copy.wait()


def unpack(n_dev, *refs):
    ins, outs, held, (gcw, gtw), (sems,) = refs[:4], refs[4:8], refs[8:12], refs[12:14], refs[14:]
    loads = [pltpu.make_async_copy(src, dst, sems.at[i]) for i, (src, dst) in enumerate(zip(ins, held))]
    stores = [
        pltpu.make_async_copy(src, dst, sems.at[4 + i])
        for i, (src, dst) in enumerate(zip((held[0], held[1], gcw, gtw), outs))
    ]
    for load in loads:
        load.start()
    for i in range(2):
        loads[i].wait()
        stores[i].start()
    conv, tconv = held[2:]
    loads[2].wait()
    conv_scale = 1.0 / math.sqrt(n_dev * 8 * 4 * 128)
    g = conv[...].reshape(-1, 128)
    first = g[:576].astype(F32) * conv_scale
    second = g[576:864].astype(F32) * conv_scale
    for zy in range(9):
        for dx in range(2):
            gcw[zy * 3 + dx] = first[zy * C : (zy + 1) * C, dx * C : (dx + 1) * C]
    for half in range(18):
        src = second[(half % 9) * 32 : (half % 9) * 32 + 32, (half // 9) * C : (half // 9 + 1) * C]
        gcw[(half // 2) * 3 + 2, (half % 2) * 32 : (half % 2) * 32 + 32, :] = src
    stores[2].start()
    loads[3].wait()
    tconv_scale = 1.0 / math.sqrt(n_dev * 4 * 2 * 64)
    gtw[...] = tconv[...].reshape(-1, 128)[:1728].astype(F32) * tconv_scale
    stores[3].start()
    for store in stores:
        store.wait()


def solution(mesh):
    nx = mesh.shape["group"]
    n_slab = mesh.shape["slab"]
    ny = 4
    nz = n_slab // (2 * ny)
    plane = ny * nx
    rows_of = [ceil16(-(-n // (2 * plane))) for n in (864, 1728)]

    def step(coarse, tw, cw, cot):
        dma = pltpu.SemaphoreType.DMA
        vmem = pltpu.VMEM
        scratch = [
            vmem((4, 2, 64, CIN), BF16),
            vmem((27 * C, CIN), BF16),
            vmem((27 * C, C), BF16),
            vmem((2048, 128), BF16),
            vmem((2048, 128), F32),
            vmem((8, C, 512), BF16),
        ]
        scratch += [vmem((COT_Z[dz][1], C, COT_Y[dy][1]), BF16) for dz, dy in DIRS]
        scratch += [vmem((COA_Z[dz][1], COA_Y[dy][1], 64, CIN), BF16) for dz, dy in DIRS]
        scratch += [vmem(shape, BF16) for shape in BACK.values()] * 2
        scratch += [
            vmem((6 * 384, 512), BF16),
            vmem((3, 192, 384), BF16),
            vmem((192, 576), BF16),
            vmem((192, 576), BF16),
            vmem((9, 192, CIN), BF16),
            vmem((10 * 192, 768), BF16),
            vmem((8, C, 512), F32),
            vmem((10 * 192, 768), BF16),
            vmem((2, 10 * C, 256), BF16),
            vmem((576, 192), F32),
            vmem((2, 384, 640), BF16),
            vmem((2, 2, 192, 512), BF16),
            vmem((4, 2, 64, CIN), F32),
        ]
        for r in rows_of:
            scratch += [
                vmem((2, plane * r, 128), BF16),
                vmem((plane * r, 128), BF16),
                vmem((plane * r, 128), BF16),
                vmem((plane - 1, r, 128), BF16),
                vmem((r, 128), BF16),
                vmem((nz, r, 128), BF16),
                vmem((2, plane * r, 128), BF16),
            ]
        scratch += [vmem((2048, 128), BF16), vmem((4, 2, 64, CIN), BF16)]
        for r in rows_of:
            scratch += [dma((2,)), dma((plane - 1,)), dma((plane - 1,)), dma((nz - 1,)), dma((nz - 1,))]
            scratch += [dma((plane - 1,)), dma((plane - 1,)), dma((plane,)), dma((plane,))]
        scratch += [dma((4,)), dma((8,)), dma((8,)), dma((8,)), dma((8,)), dma((3,)), dma((3,)), dma((6,))]
        in_hbm = pl.BlockSpec(memory_space=pltpu.HBM)
        parts = pl.pallas_call(
            functools.partial(kernel, (nz, ny, nx), rows_of),
            out_shape=(
                jax.ShapeDtypeStruct((2048, 128), BF16),
                jax.ShapeDtypeStruct((4, 2, 64, CIN), BF16),
                jax.ShapeDtypeStruct((2, plane * rows_of[0], 128), BF16),
                jax.ShapeDtypeStruct((2, plane * rows_of[1], 128), BF16),
            ),
            in_specs=[in_hbm] * 4,
            out_specs=(in_hbm,) * 4,
            scratch_shapes=scratch,
            compiler_params=pltpu.CompilerParams(
                collective_id=0, has_side_effects=True, vmem_limit_bytes=61 * 2**20
            ),
            cost_estimate=pl.CostEstimate(flops=7 * 10**9, bytes_accessed=4 * 10**6, transcendentals=500000),
        )(
            coarse.reshape(4, 2, 64, CIN),
            jnp.swapaxes(tw, 3, 4).reshape(27 * C, CIN),
            cw.reshape(27 * C, C),
            cot.reshape(2048, 128),
        )
        any_space = pl.BlockSpec(memory_space=pl.ANY)
        field, gc, gcw, gtw = pl.pallas_call(
            functools.partial(unpack, n_slab * nx),
            out_shape=(
                jax.ShapeDtypeStruct((2048, 128), BF16),
                jax.ShapeDtypeStruct((4, 2, 64, CIN), BF16),
                jax.ShapeDtypeStruct((27, C, C), F32),
                jax.ShapeDtypeStruct((27 * C, CIN), F32),
            ),
            in_specs=[any_space] * 4,
            out_specs=(any_space,) * 4,
            scratch_shapes=[
                *(vmem(part.shape, BF16) for part in parts),
                vmem((27, C, C), F32),
                vmem((27 * C, CIN), F32),
                dma((8,)),
            ],
            compiler_params=pltpu.CompilerParams(vmem_limit_bytes=61 * 2**20),
        )(*parts)
        return (
            field.reshape(1, 1, C, 8, 4, 128),
            gc.reshape(1, 1, 4, 2, 64, CIN),
            gcw.reshape(3, 3, 3, C, C),
            jnp.swapaxes(gtw.reshape(3, 3, 3, C, CIN), 3, 4),
        )

    blocks = P("group", "slab", None, None, None, None)
    return jax.shard_map(
        step,
        mesh=mesh,
        in_specs=(blocks, P(), P(), blocks),
        out_specs=(blocks, blocks, P(), P()),
        check_vma=False,
    )
```
